32 devices in a mesh: dp: 2 (over x), row: 4 (over z), col: 4 (over y, core).
Axes of the slice: x: 2, y: 2, z: 4, core: 2. Of those that a mesh axis runs over, the one named last changes fastest.
Arguments:
- layer_in: bfloat16 [768, 4096], P('row', ('dp', 'col')), may hold values from -6 to 6
- seq_lengths: int32 [8], P('dp'), may hold values from 1 to 512, as said below
- w_qkv: bfloat16 [768, 3, 768], P('row', None, 'col'), may hold values from -0.21875 to 0.21875
- q_bias: bfloat16 [768], P('col'), may hold values from -3 to 3
- v_bias: bfloat16 [768], P('col'), may hold values from -3 to 3
- w_out: bfloat16 [768, 768], P('col', 'row'), may hold values from -2.5 to 2.5
- b_out: bfloat16 [768], P('row'), may hold values from -2 to 2
- ln1_gain: bfloat16 [768], P('row'), may hold values from 0.099609375 to 1.8984375
- ln1_bias: bfloat16 [768], P('row'), may hold values from -2 to 2
- w_in: bfloat16 [768, 3072], P('row', 'col'), may hold values from -0.21875 to 0.21875
- b_in: bfloat16 [3072], P('col'), may hold values from -3 to 3
- w_back: bfloat16 [768, 3072], P('row', 'col'), may hold values from -0.109375 to 0.109375
- b_back: bfloat16 [768], P('row'), may hold values from -2 to 2
- ln2_gain: bfloat16 [768], P('row'), may hold values from 0.099609375 to 1.8984375
- ln2_bias: bfloat16 [768], P('row'), may hold values from -2 to 2
- out_grad: float32 [768, 4096], P('row', ('dp', 'col')), may hold values from -6 to 6
Outputs:
- layer_out: bfloat16 [768, 4096], P('row', ('dp', 'col'))
- in_grad: float32 [768, 4096], P('row', ('dp', 'col'))
- w_qkv_grad: float32 [768, 3, 768], P('row', None, 'col')
- q_bias_grad: float32 [768], P('col')
- v_bias_grad: float32 [768], P('col')
- w_out_grad: float32 [768, 768], P('col', 'row')
- b_out_grad: float32 [768], P('row')
- ln1_gain_grad: float32 [768], P('row')
- ln1_bias_grad: float32 [768], P('row')
- w_in_grad: float32 [768, 3072], P('row', 'col')
- b_in_grad: float32 [3072], P('col')
- w_back_grad: float32 [768, 3072], P('row', 'col')
- b_back_grad: float32 [768], P('row')
- ln2_gain_grad: float32 [768], P('row')
- ln2_bias_grad: float32 [768], P('row')
The draws below stay inside these ranges and needn't reach their ends.
Inputs may be any that keep to these rules, and one draw needn't show every extreme that they name: `seq_lengths`: each replica's 4 * 1 slots (replicas one after another) hold at least one sequence of length 512.
All inputs are finite; a program needn't handle non-finite values.
Results may differ from the reference program's by a relative error of at most 0.015.
Values may be sent and summed in bfloat16 or wider, within the bound.
No kernel may reach another device: no remote copies, remote signals or barrier semaphores. Data moves between devices by JAX's collectives and lax.ppermute only.
A program may use at most 128 MiB of HBM per device.

```python
import jax
import jax.numpy as jnp
from jax import lax

HEAD_DIM = 64
FF = 3072
L = 512
SLOTS = 1
D = 768
SEQS = 8
TOKENS = 4096
N_DP = 2
N_ROW = 4


def draw_seq_lengths(key, part):
    key = jax.random.fold_in(key, 11)
    seed_cut, seed_load, seed_full = jax.random.split(key, 3)
    per_replica = N_ROW * SLOTS
    cut_draw = jax.random.randint(seed_cut, (N_DP, per_replica), 0, L)
    load_draw = jax.random.randint(seed_load, (N_DP, 1), 1, 9)
    lengths_all = L - cut_draw * load_draw // 8
    full_slot = jax.random.randint(seed_full, (N_DP, 1), 0, per_replica)
    lengths_all = jnp.where(jnp.arange(per_replica)[None, :] == full_slot, L, lengths_all)
    return lengths_all.reshape(N_DP * per_replica).astype(jnp.int32)


def shard_levels(stream_key, shape, shards, smallest, top_value):
    factor_of, own = 1.0, jax.random.fold_in(stream_key, 6)
    for axis_at, parts in shards:
        steps = jnp.exp(jax.random.uniform(jax.random.fold_in(own, axis_at), (parts,), jnp.float32, smallest / len(shards), top_value / len(shards)))
        factor_of = factor_of * jnp.repeat(steps, shape[axis_at] // parts).reshape([-1 if axis == axis_at else 1 for axis in range(len(shape))])
    return factor_of


def normal_values(own_key, shape, deviation, limit, pieces=(), held_as=jnp.bfloat16):
    entries = deviation * jax.random.normal(own_key, shape, jnp.float32)
    if pieces:
        entries = entries * shard_levels(own_key, shape, pieces, -0.22, 0.18)
    return jnp.clip(entries, -limit, limit).astype(held_as)


def setup_inputs(seed: int = 0) -> dict:
    splits = jax.random.split(jax.random.key(seed), 17)
    layer_in = normal_values(splits[0], (D, TOKENS), 1.0, 6.0, ((0, 4), (1, 8)))
    seq_lengths = draw_seq_lengths(jax.random.fold_in(splits[16], 71), 0)
    w_qkv = normal_values(splits[2], (D, 3, D), D ** -0.5, 0.21875, ((0, 4), (2, 4)))
    q_bias = normal_values(splits[3], (D,), 0.5, 3.0, ((0, 4),))
    v_bias = normal_values(splits[4], (D,), 0.5, 3.0, ((0, 4),))
    w_out = normal_values(splits[5], (D, D), (max(D // 128, 2)) ** -0.5, 2.5, ((0, 4), (1, 4)))
    b_out = normal_values(splits[6], (D,), 0.3, 2.0, ((0, 4),))
    ln1_gain = jnp.clip(1.0 + 0.18 * jax.random.normal(splits[7], (D,), jnp.float32), 0.099609375, 1.8984375).astype(jnp.bfloat16)
    ln1_bias = normal_values(splits[8], (D,), 0.3, 2.0, ((0, 4),))
    w_in = normal_values(splits[9], (D, FF), D ** -0.5, 0.21875, ((0, 4), (1, 4)))
    b_in = normal_values(splits[10], (FF,), 0.5, 3.0, ((0, 4),))
    w_back = normal_values(splits[11], (D, FF), FF ** -0.5, 0.109375, ((0, 4), (1, 4)))
    b_back = normal_values(splits[12], (D,), 0.3, 2.0, ((0, 4),))
    ln2_gain = jnp.clip(1.0 + 0.18 * jax.random.normal(splits[13], (D,), jnp.float32), 0.099609375, 1.8984375).astype(jnp.bfloat16)
    ln2_bias = normal_values(splits[14], (D,), 0.3, 2.0, ((0, 4),))
    out_grad = normal_values(splits[15], (D, TOKENS), 1.0, 6.0, ((0, 4), (1, 8)), jnp.float32)
    return {"layer_in": layer_in, "seq_lengths": seq_lengths, "w_qkv": w_qkv, "q_bias": q_bias, "v_bias": v_bias, "w_out": w_out, "b_out": b_out, "ln1_gain": ln1_gain, "ln1_bias": ln1_bias, "w_in": w_in, "b_in": b_in, "w_back": w_back, "b_back": b_back, "ln2_gain": ln2_gain, "ln2_bias": ln2_bias, "out_grad": out_grad}


EPSILON = 1e-12
HIGHEST = lax.Precision.HIGHEST

@jax.custom_vjp
def low(v):
    return lax.optimization_barrier(v.astype(jnp.bfloat16)).astype(jnp.float32)

@jax.custom_vjp
def low_back(v):
    return v

def low_keep(v):
    return (low(v), None)

def low_pass(kept, grad):
    return (grad,)

def back_keep(v):
    return (v, None)

def back_low(kept, grad):
    return (low(grad),)
low.defvjp(low_keep, low_pass)
low_back.defvjp(back_keep, back_low)

def layer_norm(hidden, gain_row, shift_row):
    center = lax.optimization_barrier(jnp.mean(hidden, axis=-1, keepdims=True))
    spread = lax.optimization_barrier(jnp.mean(jnp.square(hidden - center), axis=-1, keepdims=True))
    return (hidden - center) * lax.rsqrt(spread + EPSILON) * gain_row + shift_row

def attend_block(block_args):
    queries, keys_in, values, key_live = block_args
    length = queries.shape[0]
    head_count = queries.shape[1] // HEAD_DIM
    q_heads = queries.reshape(length, head_count, HEAD_DIM)
    k_heads = keys_in.reshape(length, head_count, HEAD_DIM)
    v_heads = values.reshape(length, head_count, HEAD_DIM)
    scores = jnp.einsum('qhd,khd->hqk', q_heads, k_heads, precision=HIGHEST) * HEAD_DIM ** (-0.5)
    scores = low_back(scores)
    scores = jnp.where(key_live[None, None, :], scores, -1000000000.0)
    weights = jax.nn.softmax(scores, axis=-1)
    context = jnp.einsum('hqk,khd->qhd', low(weights), v_heads, precision=HIGHEST)
    return context.reshape(length, head_count * HEAD_DIM)

def layer_forward(layer_cols, w_qkv, q_bias, v_bias, w_out, b_out, ln1_gain, ln1_bias, w_in, b_in, w_back, b_back, ln2_gain, ln2_bias, valid_rows, key_live):
    layer_in = layer_cols.T
    tokens, model_width = layer_in.shape
    qkv_mixed = jnp.dot(layer_in, w_qkv.reshape(model_width, 3 * model_width), precision=HIGHEST).reshape(tokens, 3, model_width)
    queries = low(low_back(qkv_mixed[:, 0] + q_bias))
    keys_in = low(low_back(qkv_mixed[:, 1]))
    values = low(low_back(qkv_mixed[:, 2] + v_bias))
    seq_count = tokens // L
    context = lax.map(jax.checkpoint(attend_block), (queries.reshape(seq_count, L, model_width), keys_in.reshape(seq_count, L, model_width), values.reshape(seq_count, L, model_width), key_live))
    context = low(low_back(context.reshape(tokens, model_width)))
    attended = low_back(jnp.dot(context, w_out, precision=HIGHEST) + b_out)
    normed = layer_norm(layer_in + attended, ln1_gain, ln1_bias)
    hidden_pre = low_back(jnp.dot(low(normed), w_in, precision=HIGHEST) + b_in)
    hidden = low(jax.nn.gelu(hidden_pre, approximate=False))
    returned = low_back(jnp.dot(hidden, w_back.T, precision=HIGHEST) + b_back)
    final_out = layer_norm(normed + returned, ln2_gain, ln2_bias)
    return (final_out * valid_rows[:, None]).T

def reference(layer_in, seq_lengths, w_qkv, q_bias, v_bias, w_out, b_out, ln1_gain, ln1_bias, w_in, b_in, w_back, b_back, ln2_gain, ln2_bias, out_grad):
    position = jnp.arange(TOKENS, dtype=jnp.int32)
    slot_length = jnp.repeat(seq_lengths.astype(jnp.int32), L, total_repeat_length=TOKENS)
    valid_live = position % L < slot_length
    valid_rows = valid_live.astype(jnp.float32)
    key_live = valid_live.reshape(SEQS, L)
    floats = tuple((argument.astype(jnp.float32) for argument in (layer_in, w_qkv, q_bias, v_bias, w_out, b_out, ln1_gain, ln1_bias, w_in, b_in, w_back, b_back, ln2_gain, ln2_bias)))

    def forward(*params):
        return layer_forward(*params, valid_rows, key_live)
    final_out, pullback = jax.vjp(forward, *floats)
    gradients = pullback(out_grad.astype(jnp.float32))
    return (final_out.astype(jnp.bfloat16), gradients[0], gradients[1], gradients[2], gradients[3], gradients[4], gradients[5], gradients[6], gradients[7], gradients[8], gradients[9], gradients[10], gradients[11], gradients[12], gradients[13])
```

```python
import jax
import jax.numpy as jnp
from jax import lax
from jax.sharding import PartitionSpec as P

HEAD_DIM = 64
EPSILON = 1e-12
F32 = jnp.float32
BF16 = jnp.bfloat16


def dot(left, right, left_dim, right_dim):
    return lax.dot_general(
        left, right, (((left_dim,), (right_dim,)), ((), ())), preferred_element_type=F32
    )


def swap_bit(value, axis, bit):
    size = lax.axis_size(axis)
    return lax.ppermute(value, axis, [(at, at ^ bit) for at in range(size)])


def transpose_grid(value):
    rows, cols = lax.axis_size("row"), lax.axis_size("col")
    pairs = [(a * cols + b, b * cols + a) for a in range(rows) for b in range(cols)]
    return lax.ppermute(value, ("row", "col"), pairs)


def ordered(flag, own, other, axis):
    return jnp.concatenate(
        (jnp.where(flag, other, own), jnp.where(flag, own, other)), axis=axis
    )


def normalise(hidden, gain, shift):
    width = hidden.shape[0]
    center = jnp.sum(hidden, axis=0, keepdims=True) / width
    spread = jnp.sum(hidden * hidden, axis=0, keepdims=True) / width - center * center
    inverse = lax.rsqrt(spread + EPSILON)
    scaled = (hidden - center) * inverse
    return scaled, inverse, scaled * gain + shift


def normalise_back(upstream, scaled, inverse, gain):
    width = upstream.shape[0]
    weighted = upstream * gain
    mean = jnp.sum(weighted, axis=0, keepdims=True) / width
    slope = jnp.sum(weighted * scaled, axis=0, keepdims=True) / width
    return inverse * (weighted - mean - scaled * slope)


def shards(
    layer_in,
    seq_lengths,
    w_qkv,
    q_bias,
    v_bias,
    w_out,
    b_out,
    ln1_gain,
    ln1_bias,
    w_in,
    b_in,
    w_back,
    b_back,
    ln2_gain,
    ln2_bias,
    out_grad,
):
    n_rows = lax.axis_size("row")
    row, col = lax.axis_index("row"), lax.axis_index("col")
    low_bit, high_bit = (col % 2) == 1, (col // 2) == 1
    feats, slot = layer_in.shape
    half = slot // 2
    heads = w_out.shape[0] // HEAD_DIM
    head_cols = w_out.shape[0]

    def my_half(whole):
        return jnp.where(low_bit, whole[:, half:], whole[:, :half])

    def other_half(whole):
        return jnp.where(low_bit, whole[:, :half], whole[:, half:])

    def join_halves(own):
        return ordered(low_bit, own, swap_bit(own, "col", 1), 1)

    def sum_tokens(partial):
        mine = my_half(partial) + swap_bit(other_half(partial), "col", 1)
        mine = mine.astype(BF16)
        return mine.astype(F32) + swap_bit(mine, "col", 2).astype(F32)

    qkv_part = w_qkv.transpose(1, 2, 0).reshape(3 * head_cols, feats)
    vectors = jnp.stack((b_out, ln1_gain, ln1_bias, b_back, ln2_gain, ln2_bias))
    vectors = jnp.pad(vectors, ((0, 16 - vectors.shape[0]), (0, 0)))
    x_block = transpose_grid(layer_in)
    qkv_all = lax.all_gather(qkv_part, "row", axis=0)
    out_all = lax.all_gather(jnp.concatenate((w_out, vectors)), "row", axis=0)
    in_all = lax.all_gather(w_in, "row", axis=0, tiled=True)
    back_all = lax.all_gather(w_back, "row", axis=0, tiled=True)
    vec_all = out_all[:, head_cols : head_cols + 6].astype(F32)
    vec_all = vec_all.transpose(1, 0, 2).reshape(6, n_rows * feats, 1)
    b_out_all, gain_one, shift_one, b_back_all, gain_two, shift_two = [
        vec_all[i] for i in range(6)
    ]
    out_all = out_all[:, :head_cols]

    pair = ordered(low_bit, x_block, swap_bit(x_block, "col", 1), 0)
    x = ordered(high_bit, pair, swap_bit(pair, "col", 2), 0)
    length = lax.dynamic_slice_in_dim(seq_lengths, row, 1)
    key_live = jnp.arange(slot, dtype=jnp.int32)[:, None] < length
    first_token = jnp.where(low_bit, half, 0)
    live = (first_token + jnp.arange(half, dtype=jnp.int32)[None, :] < length).astype(F32)

    grad_block = transpose_grid(out_grad.astype(BF16))
    grad_pair = ordered(
        low_bit, my_half(grad_block), swap_bit(other_half(grad_block), "col", 1), 0
    )
    grad_out = ordered(high_bit, grad_pair, swap_bit(grad_pair, "col", 2), 0)

    qkv = sum(
        dot(qkv_all[b], x[b * feats : (b + 1) * feats], 1, 0) for b in range(n_rows)
    )
    queries = (qkv[:head_cols] + q_bias.astype(F32)[:, None]).astype(BF16)
    keys_in = qkv[head_cols : 2 * head_cols].astype(BF16)
    values = (qkv[2 * head_cols :] + v_bias.astype(F32)[:, None]).astype(BF16)
    head_shape = (heads, HEAD_DIM, slot)
    queries, keys_in, values = (
        part.reshape(head_shape) for part in (queries, keys_in, values)
    )
    scale = HEAD_DIM ** (-0.5)
    scores = (
        jnp.einsum("hdk,hdq->hkq", keys_in, queries, preferred_element_type=F32) * scale
    )
    scores = jnp.where(key_live[None], scores, -1000000000.0)
    peak = jnp.max(scores, axis=1, keepdims=True)
    exponent = jnp.exp(scores - peak)
    weights = (exponent / jnp.sum(exponent, axis=1, keepdims=True)).astype(BF16)
    context = jnp.einsum("hdk,hkq->hdq", values, weights, preferred_element_type=F32)
    context = context.reshape(head_cols, slot).astype(BF16)

    attended = jnp.concatenate([dot(out_all[b], context, 0, 0) for b in range(n_rows)])
    first = my_half(x).astype(F32) + sum_tokens(attended) + b_out_all
    scaled_one, inverse_one, normed = normalise(first, gain_one, shift_one)
    normed_all = join_halves(normed.astype(BF16))

    pre = dot(in_all, normed_all, 0, 0) + b_in.astype(F32)[:, None]
    share = 0.5 * (1.0 + lax.erf(pre * (0.5**0.5)))
    hidden = (pre * share).astype(BF16)
    slope = (share + pre * jnp.exp(-0.5 * pre * pre) * ((0.5 / jnp.pi) ** 0.5)).astype(BF16)
    second = normed + sum_tokens(dot(back_all, hidden, 1, 0)) + b_back_all
    scaled_two, inverse_two, final = normalise(second, gain_two, shift_two)
    final = (final * live).astype(BF16)

    grad_final = grad_out.astype(F32) * live
    ln2_gain_sum = jnp.sum(grad_final * scaled_two, axis=1)
    ln2_bias_sum = jnp.sum(grad_final, axis=1)
    grad_second = normalise_back(grad_final, scaled_two, inverse_two, gain_two)
    b_back_sum = jnp.sum(grad_second, axis=1)
    grad_returned = join_halves(grad_second.astype(BF16))

    w_back_part = dot(grad_returned, hidden, 1, 1)
    grad_hidden = dot(back_all, grad_returned, 0, 0)
    grad_pre = grad_hidden * slope.astype(F32)
    b_in_sum = jnp.sum(grad_pre, axis=1)
    grad_pre = grad_pre.astype(BF16)
    w_in_part = dot(normed_all, grad_pre, 1, 1)
    grad_normed = grad_second + sum_tokens(dot(in_all, grad_pre, 1, 0))
    ln1_gain_sum = jnp.sum(grad_normed * scaled_one, axis=1)
    ln1_bias_sum = jnp.sum(grad_normed, axis=1)
    grad_first = normalise_back(grad_normed, scaled_one, inverse_one, gain_one)
    b_out_sum = jnp.sum(grad_first, axis=1)
    grad_attended = join_halves(grad_first.astype(BF16))

    w_out_part = dot(context, grad_attended, 1, 1)
    grad_context = sum(
        dot(out_all[b], grad_attended[b * feats : (b + 1) * feats], 1, 0)
        for b in range(n_rows)
    )
    grad_context = grad_context.astype(BF16).reshape(head_shape)
    grad_weights = jnp.einsum(
        "hdk,hdq->hkq", values, grad_context, preferred_element_type=F32
    )
    weights_wide = weights.astype(F32)
    inner = jnp.sum(weights_wide * grad_weights, axis=1, keepdims=True)
    grad_scores = (weights_wide * (grad_weights - inner)).astype(BF16)
    grad_queries = (
        jnp.einsum("hdk,hkq->hdq", keys_in, grad_scores, preferred_element_type=F32) * scale
    )
    grad_keys = (
        jnp.einsum("hdq,hkq->hdk", queries, grad_scores, preferred_element_type=F32) * scale
    )
    grad_values = jnp.einsum(
        "hdq,hkq->hdk", grad_context, weights, preferred_element_type=F32
    )
    grad_qkv = jnp.concatenate(
        [
            part.reshape(head_cols, slot).astype(BF16)
            for part in (grad_queries, grad_keys, grad_values)
        ]
    )
    q_bias_sum = jnp.sum(grad_qkv[:head_cols], axis=1, dtype=F32)
    v_bias_sum = jnp.sum(grad_qkv[2 * head_cols :], axis=1, dtype=F32)

    half_grad = 0.5 * grad_first
    kept = jnp.concatenate(
        (jnp.where(low_bit, 0.0, half_grad), jnp.where(low_bit, half_grad, 0.0)), axis=1
    )
    blocks = [
        dot(qkv_all[b], grad_qkv, 0, 0) + kept[b * feats : (b + 1) * feats]
        for b in range(n_rows)
    ]
    evens = jnp.concatenate((blocks[0], blocks[2]))
    odds = jnp.concatenate((blocks[1], blocks[3]))
    mine = jnp.where(low_bit, odds, evens) + swap_bit(
        jnp.where(low_bit, evens, odds), "col", 1
    )
    own = jnp.where(high_bit, mine[feats:], mine[:feats])
    away = jnp.where(high_bit, mine[:feats], mine[feats:]).astype(BF16)
    in_grad = own + swap_bit(away, "col", 2).astype(F32)
    in_grad = transpose_grid(in_grad.astype(BF16)).astype(F32)

    final = final.reshape(n_rows, feats, half)
    own = lax.dynamic_index_in_dim(final, col, 0, False)
    away = lax.dynamic_index_in_dim(final, col ^ 1, 0, False)
    layer_out = transpose_grid(ordered(low_bit, own, swap_bit(away, "col", 1), 1))

    def reduce_rows(part):
        kept_rows = lax.psum_scatter(part.astype(BF16), "row", scatter_dimension=0, tiled=True)
        return lax.psum(kept_rows, "dp").astype(F32)

    w_back_grad = reduce_rows(w_back_part)
    w_in_grad = reduce_rows(w_in_part)
    w_out_blocks = w_out_part.reshape(head_cols, n_rows, feats).transpose(1, 0, 2)
    w_out_grad = reduce_rows(w_out_blocks.reshape(n_rows * head_cols, feats))
    vector_sums = jnp.stack(
        (ln1_gain_sum, ln1_bias_sum, ln2_gain_sum, ln2_bias_sum, b_out_sum, b_back_sum)
    )
    vector_sums = vector_sums + swap_bit(vector_sums, "col", 1)
    vector_blocks = vector_sums.reshape(6, n_rows, feats).transpose(1, 0, 2)
    shared = jnp.concatenate((q_bias_sum[None], v_bias_sum[None], b_in_sum.reshape(-1, feats)))
    n_extra = 6 + shared.shape[0]
    extra = [
        jnp.concatenate((vector_blocks[b], shared, jnp.zeros((16 - n_extra, feats), F32)))
        for b in range(n_rows)
    ]
    qkv_blocks = []
    for b in range(n_rows):
        qkv_blocks += [dot(grad_qkv, x[b * feats : (b + 1) * feats], 1, 1), extra[b]]
    qkv_sum = reduce_rows(jnp.concatenate(qkv_blocks))
    w_qkv_grad = qkv_sum[: 3 * head_cols].reshape(3, head_cols, feats).transpose(2, 0, 1)
    tail = qkv_sum[3 * head_cols :]
    return (
        layer_out,
        in_grad,
        w_qkv_grad,
        tail[6],
        tail[7],
        w_out_grad,
        tail[4],
        tail[0],
        tail[1],
        w_in_grad,
        tail[8:n_extra].reshape(-1),
        w_back_grad,
        tail[5],
        tail[2],
        tail[3],
    )


def solution(mesh):
    tokens = P("row", ("dp", "col"))
    block = P("row", "col")
    in_specs = (
        tokens,
        P("dp"),
        P("row", None, "col"),
        P("col"),
        P("col"),
        P("col", "row"),
        P("row"),
        P("row"),
        P("row"),
        block,
        P("col"),
        block,
        P("row"),
        P("row"),
        P("row"),
        tokens,
    )
    out_specs = (
        tokens,
        tokens,
        P("row", None, "col"),
        P("col"),
        P("col"),
        P("col", "row"),
        P("row"),
        P("row"),
        P("row"),
        block,
        P("col"),
        block,
        P("row"),
        P("row"),
        P("row"),
    )
    return jax.shard_map(shards, mesh=mesh, in_specs=in_specs, out_specs=out_specs, check_vma=False)
```

```python
import jax
import jax.numpy as jnp
from jax import lax
from jax.sharding import PartitionSpec as P

HEAD_DIM = 64
EPSILON = 1e-12
F32 = jnp.float32
BF16 = jnp.bfloat16


def dot(left, right, left_dim, right_dim):
    return lax.dot_general(
        left, right, (((left_dim,), (right_dim,)), ((), ())), preferred_element_type=F32
    )


def swap_bit(value, axis, bit):
    size = lax.axis_size(axis)
    return lax.ppermute(value, axis, [(at, at ^ bit) for at in range(size)])


def grid_pairs():
    size = lax.axis_size("row")
    return [
        (a * size + b, b * size + (a - b) % size) for a in range(size) for b in range(size)
    ]


def to_slot(value):
    return lax.ppermute(value, ("row", "col"), grid_pairs())


def from_slot(value):
    return lax.ppermute(value, ("row", "col"), [(b, a) for a, b in grid_pairs()])


def from_row(value, away):
    size = lax.axis_size("row")
    return lax.ppermute(value, "row", [((a + away) % size, a) for a in range(size)])


def after(value, *others):
    return lax.optimization_barrier((value,) + others)[0]


def ordered(flag, own, other, axis):
    return jnp.concatenate(
        (jnp.where(flag, other, own), jnp.where(flag, own, other)), axis=axis
    )


def normalise(hidden, gain, shift):
    width = hidden.shape[0]
    center = jnp.sum(hidden, axis=0, keepdims=True) / width
    spread = jnp.sum(hidden * hidden, axis=0, keepdims=True) / width - center * center
    inverse = lax.rsqrt(spread + EPSILON)
    scaled = (hidden - center) * inverse
    return scaled, inverse, scaled * gain + shift


def normalise_back(upstream, scaled, inverse, gain):
    width = upstream.shape[0]
    weighted = upstream * gain
    mean = jnp.sum(weighted, axis=0, keepdims=True) / width
    slope = jnp.sum(weighted * scaled, axis=0, keepdims=True) / width
    return inverse * (weighted - mean - scaled * slope)


def shards(
    layer_in,
    seq_lengths,
    w_qkv,
    q_bias,
    v_bias,
    w_out,
    b_out,
    ln1_gain,
    ln1_bias,
    w_in,
    b_in,
    w_back,
    b_back,
    ln2_gain,
    ln2_bias,
    out_grad,
):
    n_rows = lax.axis_size("row")
    row, col = lax.axis_index("row"), lax.axis_index("col")
    low_bit, high_bit = (col % 2) == 1, (col // 2) == 1
    feats, slot = layer_in.shape
    half = slot // 2
    heads = w_out.shape[0] // HEAD_DIM
    head_cols = w_out.shape[0]

    def my_half(whole):
        return jnp.where(low_bit, whole[:, half:], whole[:, :half])

    def other_half(whole):
        return jnp.where(low_bit, whole[:, :half], whole[:, half:])

    def join_halves(own):
        return ordered(low_bit, own, swap_bit(own, "col", 1), 1)

    def sum_tokens(partial):
        mine = my_half(partial) + swap_bit(other_half(partial), "col", 1)
        mine = mine.astype(BF16)
        return mine.astype(F32) + swap_bit(mine, "col", 2).astype(F32)

    odd = (lax.axis_index("dp") % 2) == 1
    x_block = to_slot(layer_in)
    qkv_part = w_qkv.transpose(1, 2, 0).reshape(3 * head_cols, feats)
    vectors = jnp.stack((b_out, ln1_gain, ln1_bias, b_back, ln2_gain, ln2_bias))
    vectors = jnp.pad(vectors, ((0, 32 - vectors.shape[0]), (0, 0)))
    packed = jnp.concatenate((qkv_part, w_out, vectors))
    n_half = packed.shape[0] // 2
    packed_half = jnp.where(odd, packed[n_half:], packed[:n_half])
    fetched = [from_row(after(packed_half, x_block), k) for k in range(1, n_rows)]
    swapped = [swap_bit(part, "dp", 1) for part in fetched]
    packs = [packed] + [ordered(odd, f, o, 0) for f, o in zip(fetched, swapped)]
    qkv_all = [part[: 3 * head_cols] for part in packs]
    out_all = [part[3 * head_cols : 4 * head_cols] for part in packs]
    vec_all = jnp.stack([part[4 * head_cols : 4 * head_cols + 6] for part in packs], axis=1)
    vec_all = vec_all.reshape(6, n_rows * feats, 1).astype(F32)
    b_out_all, gain_one, shift_one, b_back_all, gain_two, shift_two = [
        vec_all[i] for i in range(6)
    ]
    wide_half = after(jnp.where(odd, w_back, w_in), *fetched)
    fetched = [from_row(wide_half, k) for k in range(1, n_rows)]
    swapped = [swap_bit(part, "dp", 1) for part in fetched]
    in_all = jnp.concatenate(
        [w_in] + [jnp.where(odd, o, f) for f, o in zip(fetched, swapped)]
    )
    back_all = jnp.concatenate(
        [w_back] + [jnp.where(odd, f, o) for f, o in zip(fetched, swapped)]
    )

    pair = ordered(low_bit, x_block, swap_bit(x_block, "col", 1), 0)
    x = ordered(high_bit, pair, swap_bit(pair, "col", 2), 0)
    length = lax.dynamic_slice_in_dim(seq_lengths, row, 1)
    key_live = jnp.arange(slot, dtype=jnp.int32)[:, None] < length
    first_token = jnp.where(low_bit, half, 0)
    live = (first_token + jnp.arange(half, dtype=jnp.int32)[None, :] < length).astype(F32)

    qkv = sum(
        dot(qkv_all[b], x[b * feats : (b + 1) * feats], 1, 0) for b in range(n_rows)
    )
    grad_block = to_slot(after(out_grad.astype(BF16), qkv))
    grad_pair = ordered(
        low_bit, my_half(grad_block), swap_bit(other_half(grad_block), "col", 1), 0
    )
    grad_out = ordered(high_bit, grad_pair, swap_bit(grad_pair, "col", 2), 0)

    queries = (qkv[:head_cols] + q_bias.astype(F32)[:, None]).astype(BF16)
    keys_in = qkv[head_cols : 2 * head_cols].astype(BF16)
    values = (qkv[2 * head_cols :] + v_bias.astype(F32)[:, None]).astype(BF16)
    head_shape = (heads, HEAD_DIM, slot)
    queries, keys_in, values = (
        part.reshape(head_shape) for part in (queries, keys_in, values)
    )
    scale = HEAD_DIM ** (-0.5)
    scores = (
        jnp.einsum("hdk,hdq->hkq", keys_in, queries, preferred_element_type=F32) * scale
    )
    scores = jnp.where(key_live[None], scores, -1000000000.0)
    peak = jnp.max(scores, axis=1, keepdims=True)
    exponent = jnp.exp(scores - peak)
    weights = (exponent / jnp.sum(exponent, axis=1, keepdims=True)).astype(BF16)
    context = jnp.einsum("hdk,hkq->hdq", values, weights, preferred_element_type=F32)
    context = context.reshape(head_cols, slot).astype(BF16)

    attended = jnp.concatenate([dot(out_all[b], context, 0, 0) for b in range(n_rows)])
    first = my_half(x).astype(F32) + sum_tokens(attended) + b_out_all
    scaled_one, inverse_one, normed = normalise(first, gain_one, shift_one)
    normed_all = join_halves(normed.astype(BF16))

    pre = dot(in_all, normed_all, 0, 0) + b_in.astype(F32)[:, None]
    share = 0.5 * (1.0 + lax.erf(pre * (0.5**0.5)))
    hidden = (pre * share).astype(BF16)
    slope = (share + pre * jnp.exp(-0.5 * pre * pre) * ((0.5 / jnp.pi) ** 0.5)).astype(BF16)
    second = normed + sum_tokens(dot(back_all, hidden, 1, 0)) + b_back_all
    scaled_two, inverse_two, final = normalise(second, gain_two, shift_two)
    final = (final * live).astype(BF16)

    grad_final = grad_out.astype(F32) * live
    ln2_gain_sum = jnp.sum(grad_final * scaled_two, axis=1)
    ln2_bias_sum = jnp.sum(grad_final, axis=1)
    grad_second = normalise_back(grad_final, scaled_two, inverse_two, gain_two)
    b_back_sum = jnp.sum(grad_second, axis=1)
    grad_returned = join_halves(grad_second.astype(BF16))

    w_back_part = dot(grad_returned, hidden, 1, 1)
    grad_hidden = dot(back_all, grad_returned, 0, 0)
    grad_pre = grad_hidden * slope.astype(F32)
    b_in_sum = jnp.sum(grad_pre, axis=1)
    grad_pre = grad_pre.astype(BF16)
    w_in_part = dot(normed_all, grad_pre, 1, 1)
    grad_normed = grad_second + sum_tokens(dot(in_all, grad_pre, 1, 0))
    ln1_gain_sum = jnp.sum(grad_normed * scaled_one, axis=1)
    ln1_bias_sum = jnp.sum(grad_normed, axis=1)
    grad_first = normalise_back(grad_normed, scaled_one, inverse_one, gain_one)
    b_out_sum = jnp.sum(grad_first, axis=1)
    grad_attended = join_halves(grad_first.astype(BF16))

    w_out_part = dot(context, grad_attended, 1, 1)
    grad_context = sum(
        dot(out_all[b], grad_attended[b * feats : (b + 1) * feats], 1, 0)
        for b in range(n_rows)
    )
    grad_context = grad_context.astype(BF16).reshape(head_shape)
    grad_weights = jnp.einsum(
        "hdk,hdq->hkq", values, grad_context, preferred_element_type=F32
    )
    weights_wide = weights.astype(F32)
    inner = jnp.sum(weights_wide * grad_weights, axis=1, keepdims=True)
    grad_scores = (weights_wide * (grad_weights - inner)).astype(BF16)
    grad_queries = (
        jnp.einsum("hdk,hkq->hdq", keys_in, grad_scores, preferred_element_type=F32) * scale
    )
    grad_keys = (
        jnp.einsum("hdq,hkq->hdk", queries, grad_scores, preferred_element_type=F32) * scale
    )
    grad_values = jnp.einsum(
        "hdq,hkq->hdk", grad_context, weights, preferred_element_type=F32
    )
    grad_qkv = jnp.concatenate(
        [
            part.reshape(head_cols, slot).astype(BF16)
            for part in (grad_queries, grad_keys, grad_values)
        ]
    )
    q_bias_sum = jnp.sum(grad_qkv[:head_cols], axis=1, dtype=F32)
    v_bias_sum = jnp.sum(grad_qkv[2 * head_cols :], axis=1, dtype=F32)

    half_grad = 0.5 * grad_first
    kept = jnp.concatenate(
        (jnp.where(low_bit, 0.0, half_grad), jnp.where(low_bit, half_grad, 0.0)), axis=1
    )
    blocks = [
        dot(qkv_all[b], grad_qkv, 0, 0) + kept[b * feats : (b + 1) * feats]
        for b in range(n_rows)
    ]
    evens = jnp.concatenate((blocks[0], blocks[2]))
    odds = jnp.concatenate((blocks[1], blocks[3]))
    mine = jnp.where(low_bit, odds, evens) + swap_bit(
        jnp.where(low_bit, evens, odds), "col", 1
    )
    own = jnp.where(high_bit, mine[feats:], mine[:feats])
    away = jnp.where(high_bit, mine[:feats], mine[feats:]).astype(BF16)
    in_grad = own + swap_bit(away, "col", 2).astype(F32)
    in_grad = from_slot(in_grad.astype(BF16)).astype(F32)

    final = after(final, grad_normed).reshape(n_rows, feats, half)
    own = lax.dynamic_index_in_dim(final, col, 0, False)
    away = lax.dynamic_index_in_dim(final, col ^ 1, 0, False)
    layer_out = from_slot(ordered(low_bit, own, swap_bit(away, "col", 1), 1))

    def reduce_rows(blocks):
        rows = blocks[0].shape[0] // 2
        blocks = jnp.stack(blocks).astype(BF16)
        keep = jnp.where(odd, blocks[:, rows:], blocks[:, :rows])
        give = jnp.where(odd, blocks[:, :rows], blocks[:, rows:])
        keep = keep.astype(F32) + swap_bit(give, "dp", 1).astype(F32)
        keep = keep.astype(BF16)
        terms = [keep[0]] + [from_row(keep[k], n_rows - k) for k in range(1, n_rows)]
        terms = [term.astype(F32) for term in terms]
        while len(terms) > 1:
            pairs = len(terms) // 2
            terms = [terms[i] + terms[i + pairs] for i in range(pairs)]
        total = terms[0].astype(BF16)
        bit = 2
        while bit < lax.axis_size("dp"):
            total = total.astype(F32) + swap_bit(total, "dp", bit).astype(F32)
            total = total.astype(BF16)
            bit *= 2
        return ordered(odd, total, swap_bit(total, "dp", 1), 0).astype(F32)

    w_back_grad = reduce_rows([w_back_part[b * feats : (b + 1) * feats] for b in range(n_rows)])
    w_in_grad = reduce_rows([w_in_part[b * feats : (b + 1) * feats] for b in range(n_rows)])
    vector_sums = jnp.stack(
        (ln1_gain_sum, ln1_bias_sum, ln2_gain_sum, ln2_bias_sum, b_out_sum, b_back_sum)
    )
    vector_sums = vector_sums + swap_bit(vector_sums, "col", 1)
    shared = jnp.concatenate((q_bias_sum[None], v_bias_sum[None], b_in_sum.reshape(-1, feats)))
    n_extra = 6 + shared.shape[0]
    packs = []
    for b in range(n_rows):
        span = slice(b * feats, (b + 1) * feats)
        packs += [
            jnp.concatenate(
                (
                    dot(grad_qkv, x[span], 1, 1),
                    w_out_part[:, span],
                    vector_sums[:, span],
                    shared,
                    jnp.zeros((32 - n_extra, feats), F32),
                )
            )
        ]
    total = reduce_rows(packs)
    w_qkv_grad = total[: 3 * head_cols].reshape(3, head_cols, feats).transpose(2, 0, 1)
    w_out_grad = total[3 * head_cols : 4 * head_cols]
    tail = total[4 * head_cols :]
    return (
        layer_out,
        in_grad,
        w_qkv_grad,
        tail[6],
        tail[7],
        w_out_grad,
        tail[4],
        tail[0],
        tail[1],
        w_in_grad,
        tail[8:n_extra].reshape(-1),
        w_back_grad,
        tail[5],
        tail[2],
        tail[3],
    )


def solution(mesh):
    tokens = P("row", ("dp", "col"))
    block = P("row", "col")
    in_specs = (
        tokens,
        P("dp"),
        P("row", None, "col"),
        P("col"),
        P("col"),
        P("col", "row"),
        P("row"),
        P("row"),
        P("row"),
        block,
        P("col"),
        block,
        P("row"),
        P("row"),
        P("row"),
        tokens,
    )
    out_specs = (
        tokens,
        tokens,
        P("row", None, "col"),
        P("col"),
        P("col"),
        P("col", "row"),
        P("row"),
        P("row"),
        P("row"),
        block,
        P("col"),
        block,
        P("row"),
        P("row"),
        P("row"),
    )
    return jax.shard_map(shards, mesh=mesh, in_specs=in_specs, out_specs=out_specs, check_vma=False)
```

```python
import jax
import jax.numpy as jnp
from jax import lax
from jax.experimental import pallas as pl
from jax.experimental.pallas import tpu as pltpu
from jax.sharding import PartitionSpec as P

HEAD_DIM = 64
EPSILON = 1e-12
F32 = jnp.float32
BF16 = jnp.bfloat16
EXTRA = 32


def dot(left, right, left_dim, right_dim):
    return lax.dot_general(
        left, right, (((left_dim,), (right_dim,)), ((), ())), preferred_element_type=F32
    )


def call(kernel, name, outs, args, flops=0, scratch=(), specs=None):
    vmem = pl.BlockSpec(memory_space=pltpu.VMEM)
    in_specs = [
        pl.BlockSpec(memory_space=pltpu.SMEM) if arg.dtype == jnp.int32 else vmem for arg in args
    ]
    for at, spec in (specs or {}).items():
        in_specs[at] = spec
    moved = sum(arg.size * arg.dtype.itemsize for arg in args)
    moved += sum(out.size * out.dtype.itemsize for out in outs)
    return pl.pallas_call(
        kernel,
        name=name,
        out_shape=outs,
        grid=(1,) if specs else (),
        in_specs=in_specs,
        out_specs=[vmem] * len(outs),
        scratch_shapes=list(scratch),
        compiler_params=pltpu.CompilerParams(vmem_limit_bytes=32 * 1024 * 1024),
        cost_estimate=pl.CostEstimate(flops=flops, bytes_accessed=moved, transcendentals=0),
    )(*args)


def shape(dims, dtype):
    return jax.ShapeDtypeStruct(dims, dtype)


def swap_bit(value, axis, bit):
    size = lax.axis_size(axis)
    return lax.ppermute(value, axis, [(at, at ^ bit) for at in range(size)])


def grid_pairs():
    size = lax.axis_size("row")
    return [
        (a * size + b, b * size + (a - b) % size) for a in range(size) for b in range(size)
    ]


def to_slot(value):
    return lax.ppermute(value, ("row", "col"), grid_pairs())


def from_slot(value):
    return lax.ppermute(value, ("row", "col"), [(b, a) for a, b in grid_pairs()])


def from_row(value, away):
    size = lax.axis_size("row")
    return lax.ppermute(value, "row", [((a + away) % size, a) for a in range(size)])


def after(value, *others):
    return lax.optimization_barrier((value,) + others)[0]


def ordered(flag, own, other, axis):
    return jnp.concatenate(
        (jnp.where(flag, other, own), jnp.where(flag, own, other)), axis=axis
    )


def row_sums(products):
    total = 0.0
    for at, product in products.items():
        pick = lax.broadcasted_iota(jnp.int32, (8, product.shape[1]), 0) == at
        pick = pick.astype(BF16)
        high = product.astype(BF16)
        rest = (product - high.astype(F32)).astype(BF16)
        total = total + dot(pick, high, 1, 1) + dot(pick, rest, 1, 1)
    return total


def attend_kernel(
    flags, x0, x1, x2, x3, w_qkv, w_out, f1, f2, f3, s1, s2, s3, bias,
    xs, packs, qkv, prob, context, mine, other,
):
    low, odd, col, length = flags[0], flags[1], flags[2], flags[3]
    feats, slot = x0.shape
    half = slot // 2
    width = w_out.shape[0]
    n_half = f1.shape[0]
    for bit, ref in enumerate((x0, x1, x2, x3)):
        rows = pl.ds(pl.multiple_of((col ^ bit) * feats, feats), feats)

        @pl.when(low == 0)
        def _():
            xs[rows, :] = ref[...]

        @pl.when(low == 1)
        def _():
            xs[rows, :half] = ref[:, half:]
            xs[rows, half:] = ref[:, :half]

    packs[0, : 3 * width] = w_qkv[...]
    packs[0, 3 * width :] = w_out[...]
    for k, (f, s) in enumerate(((f1, s1), (f2, s2), (f3, s3))):

        @pl.when(odd == 0)
        def _():
            packs[k + 1, :n_half] = f[...]
            packs[k + 1, n_half:] = s[...]

        @pl.when(odd == 1)
        def _():
            packs[k + 1, :n_half] = s[...]
            packs[k + 1, n_half:] = f[...]

    for part in range(3):
        rows = slice(part * width, (part + 1) * width)
        total = 0.0
        for k in range(4):
            total = total + dot(packs[k, rows], xs[k * feats : (k + 1) * feats], 1, 0)
        qkv[rows] = (total + bias[rows]).astype(BF16)

    place = lax.broadcasted_iota(jnp.int32, (slot, half), 0)
    place = jnp.where(low == 1, (place + half) % slot, place)
    live = place < length
    scale = HEAD_DIM ** (-0.5)
    for h in range(width // HEAD_DIM):
        q_rows = pl.ds(h * HEAD_DIM, HEAD_DIM)
        k_rows = pl.ds(width + h * HEAD_DIM, HEAD_DIM)
        v_rows = pl.ds(2 * width + h * HEAD_DIM, HEAD_DIM)
        for part in range(2):
            cols = slice(part * half, (part + 1) * half)
            scores = dot(qkv[k_rows, :], qkv[q_rows, cols], 0, 0) * scale
            scores = jnp.where(live, scores, -1000000000.0)
            exponent = jnp.exp(scores - jnp.max(scores, axis=0, keepdims=True))
            inverse = 1.0 / jnp.sum(exponent, axis=0, keepdims=True)
            weights = (exponent * inverse).astype(BF16)
            prob[h, :, cols] = weights
            context[q_rows, cols] = dot(qkv[v_rows, :], weights, 1, 0).astype(BF16)

    for k in range(4):
        rows = slice(k * feats, (k + 1) * feats)
        part = dot(packs[k, 3 * width :], context[...], 0, 0)
        mine[rows] = part[:, :half]
        other[rows] = part[:, half:].astype(BF16)


def vector_kernel(v0, v1, v2, v3, out):
    feats = out.shape[0] // 4
    eye = (
        lax.broadcasted_iota(jnp.int32, (feats, feats), 0)
        == lax.broadcasted_iota(jnp.int32, (feats, feats), 1)
    ).astype(BF16)
    for k, ref in enumerate((v0, v1, v2, v3)):
        out[k * feats : (k + 1) * feats] = dot(eye, ref[:, :feats], 1, 1)


def norm_kernel(x, own, away, vecs, scaled, inverse, low_normed):
    first = x[...].astype(F32) + own[...].astype(F32) + away[...].astype(F32) + vecs[:, 0:1]
    center = jnp.mean(first, axis=0, keepdims=True)
    first = first - center
    inv = lax.rsqrt(jnp.mean(first * first, axis=0, keepdims=True) + EPSILON)
    first = first * inv
    scaled[...] = first
    inverse[...] = jnp.broadcast_to(inv, inverse.shape)
    low_normed[...] = (first * vecs[:, 1:2] + vecs[:, 2:3]).astype(BF16)


def forward_kernel(n_own, n_away, w_in, w_back, bias, hidden, slope, mine, other):
    half = n_own.shape[1]
    step = 256
    for part, ref in enumerate((n_own, n_away)):
        cols = slice(part * half, (part + 1) * half)
        for at in range(0, w_in.shape[1], step):
            rows = slice(at, at + step)
            pre = dot(w_in[:, rows], ref[...], 0, 0) + bias[rows]
            share = 0.5 * (1.0 + lax.erf(pre * (0.5**0.5)))
            hidden[rows, cols] = (pre * share).astype(BF16)
            bell = jnp.exp(-0.5 * pre * pre) * ((0.5 / jnp.pi) ** 0.5)
            slope[rows, cols] = (share + pre * bell).astype(BF16)
    mine[...] = dot(w_back[...], hidden[:, :half], 1, 0)
    other[...] = dot(w_back[...], hidden[:, half:], 1, 0).astype(BF16)


def turn_kernel(
    flags, scaled_one, own, away, vecs, g_own, g_high, g_low,
    keep, give, grad_second, grad_returned, sums, final, grad,
):
    low, col, length = flags[0], flags[2], flags[3]
    feats = g_own.shape[0]
    half = own.shape[1]

    def rows(bit):
        return pl.ds(pl.multiple_of((col ^ bit) * feats, feats), feats)

    for bit, ref in ((0, g_own), (2, g_high)):

        @pl.when(low == 0)
        def _():
            grad[rows(bit), :] = ref[:, :half]

        @pl.when(low == 1)
        def _():
            grad[rows(bit), :] = ref[:, half:]

    grad[rows(1), :] = g_low[:feats]
    grad[rows(3), :] = g_low[feats:]

    normed = scaled_one[...] * vecs[:, 1:2] + vecs[:, 2:3]
    second = normed + own[...].astype(F32) + away[...].astype(F32) + vecs[:, 3:4]
    second = second - jnp.mean(second, axis=0, keepdims=True)
    inv = lax.rsqrt(jnp.mean(second * second, axis=0, keepdims=True) + EPSILON)
    scaled = second * inv
    place = low * half + lax.broadcasted_iota(jnp.int32, (1, half), 1)
    live = (place < length).astype(F32)
    final[...] = ((scaled * vecs[:, 4:5] + vecs[:, 5:6]) * live).astype(BF16)
    keep[...] = final[rows(0), :]
    give[...] = final[rows(1), :]
    upstream = grad[...].astype(F32) * live
    weighted = upstream * vecs[:, 4:5]
    mean = jnp.mean(weighted, axis=0, keepdims=True)
    tilt = jnp.mean(weighted * scaled, axis=0, keepdims=True)
    back = inv * (weighted - mean - scaled * tilt)
    grad_second[...] = back
    grad_returned[...] = back.astype(BF16)
    sums[...] = row_sums({2: upstream * scaled, 3: upstream, 5: back})


def backward_kernel(r_own, r_away, slope, w_in, w_back, mine, other, grad_pre, b_in_sums):
    half = r_own.shape[1]
    step = 256
    for part, ref in enumerate((r_own, r_away)):
        cols = slice(part * half, (part + 1) * half)
        for at in range(0, w_in.shape[1], step):
            rows = slice(at, at + step)
            grad_hidden = dot(w_back[:, rows], ref[...], 0, 0)
            grad_pre[rows, cols] = (grad_hidden * slope[rows, cols].astype(F32)).astype(BF16)
    mine[...] = dot(w_in[...], grad_pre[:, :half], 1, 0)
    other[...] = dot(w_in[...], grad_pre[:, half:], 1, 0).astype(BF16)
    size = b_in_sums.shape[1]
    total = 0.0
    for k in range(w_in.shape[1] // size):
        pick = lax.broadcasted_iota(jnp.int32, (8, 2 * half), 0) == k
        total = total + dot(pick.astype(BF16), grad_pre[k * size : (k + 1) * size], 1, 1)
    b_in_sums[...] = total


def wide_grad_kernel(r_own, r_away, hidden, n_own, n_away, grad_pre, *outs):
    half = r_own.shape[1]
    feats = outs[0].shape[0]
    for k in range(4):
        rows = slice(k * feats, (k + 1) * feats)
        for out, own, away, right in (
            (outs[k], r_own, r_away, hidden),
            (outs[4 + k], n_own, n_away, grad_pre),
        ):
            total = dot(own[rows], right[:, :half], 1, 1)
            out[...] = (total + dot(away[rows], right[:, half:], 1, 1)).astype(BF16)


def norm_back_kernel(
    own, away, grad_second, scaled, inverse, vecs, sums, grad_first, low_first, sums_out
):
    upstream = grad_second[...] + own[...].astype(F32) + away[...].astype(F32)
    weighted = upstream * vecs[:, 1:2]
    mean = jnp.mean(weighted, axis=0, keepdims=True)
    tilt = jnp.mean(weighted * scaled[...], axis=0, keepdims=True)
    back = inverse[0:1] * (weighted - mean - scaled[...] * tilt)
    grad_first[...] = back
    low_first[...] = back.astype(BF16)
    sums_out[...] = sums[...] + row_sums({0: upstream * scaled[...], 1: upstream, 4: back})


def attend_back_kernel(
    flags, a_own, a_away, packs, qkv, prob, grad_first, grad_qkv, keep, give, grad_context
):
    low = flags[0]
    half = a_own.shape[1]
    feats = packs.shape[2]
    width = grad_context.shape[0]
    for part, ref in enumerate((a_own, a_away)):
        cols = slice(part * half, (part + 1) * half)
        total = 0.0
        for k in range(4):
            total = total + dot(
                packs[k, 3 * width :], ref[k * feats : (k + 1) * feats], 1, 0
            )
        grad_context[:, cols] = total.astype(BF16)
    scale = HEAD_DIM ** (-0.5)
    for h in range(width // HEAD_DIM):
        q_rows = pl.ds(h * HEAD_DIM, HEAD_DIM)
        k_rows = pl.ds(width + h * HEAD_DIM, HEAD_DIM)
        v_rows = pl.ds(2 * width + h * HEAD_DIM, HEAD_DIM)
        grad_keys, grad_values = 0.0, 0.0
        for part in range(2):
            cols = slice(part * half, (part + 1) * half)
            weights = prob[h, :, cols]
            wide = weights.astype(F32)
            grad_weights = dot(qkv[v_rows, :], grad_context[q_rows, cols], 0, 0)
            inner = jnp.sum(wide * grad_weights, axis=0, keepdims=True)
            grad_scores = (wide * (grad_weights - inner)).astype(BF16)
            grad_qkv[q_rows, cols] = (dot(qkv[k_rows, :], grad_scores, 1, 0) * scale).astype(BF16)
            grad_keys = grad_keys + dot(qkv[q_rows, cols], grad_scores, 1, 1)
            grad_values = grad_values + dot(grad_context[q_rows, cols], weights, 1, 1)
        grad_qkv[k_rows, :] = (grad_keys * scale).astype(BF16)
        grad_qkv[v_rows, :] = grad_values.astype(BF16)

    def block(k):
        part = dot(packs[k, : 3 * width], grad_qkv[...], 0, 0)
        rows = pl.ds(pl.multiple_of(k * feats, feats), feats)
        return part[:, :half] + 0.5 * grad_first[rows, :], part[:, half:]

    for j in range(2):
        rows = slice(j * feats, (j + 1) * feats)
        near, far = block(2 * j + 1 - low)
        give[rows, :half] = near.astype(BF16)
        give[rows, half:] = far.astype(BF16)
        near, far = block(2 * j + low)
        keep[rows, :half] = near
        keep[rows, half:] = far


def pack_grad_kernel(
    flags, xs, grad_qkv, a_own, a_away, context, sums, sums_away, b_in_sums, keep, give, pack
):
    odd = flags[1]
    feats = pack.shape[1]
    width = context.shape[0]
    half = a_own.shape[1]
    rows = keep.shape[1]
    ones = (lax.broadcasted_iota(jnp.int32, (8, 2 * half), 0) == 4).astype(BF16)
    more = (lax.broadcasted_iota(jnp.int32, (8, 2 * half), 0) == 5).astype(BF16)
    shared = b_in_sums[...] + dot(ones, grad_qkv[:width], 1, 1)
    shared = shared + dot(more, grad_qkv[2 * width :], 1, 1)
    vector_sums = sums[...] + sums_away[...]
    for k in range(4):
        span = slice(k * feats, (k + 1) * feats)
        pack[: 3 * width] = dot(grad_qkv[...], xs[span], 1, 1).astype(BF16)
        total = dot(context[:, :half], a_own[span], 1, 1)
        total = total + dot(context[:, half:], a_away[span], 1, 1)
        pack[3 * width : 4 * width] = total.astype(BF16)
        tail = jnp.concatenate(
            (vector_sums[:, span], shared, jnp.zeros((EXTRA - 16, feats), F32)), axis=0
        )
        pack[4 * width :] = tail.astype(BF16)

        @pl.when(odd == 0)
        def _():
            keep[k] = pack[:rows]
            give[k] = pack[rows:]

        @pl.when(odd == 1)
        def _():
            keep[k] = pack[rows:]
            give[k] = pack[:rows]


def join_kernel(flags, kept, got, own, away):
    high = flags[4]
    feats = own.shape[0]
    half = own.shape[1] // 2
    for out, at in ((own, high), (away, 1 - high)):
        rows = pl.ds(pl.multiple_of(at * feats, feats), feats)
        near = kept[rows, :half] + got[rows, half:].astype(F32)
        far = kept[rows, half:] + got[rows, :half].astype(F32)
        out[:, :half] = near.astype(out.dtype)
        out[:, half:] = far.astype(out.dtype)


def finish_kernel(flags, own, got, out):
    low = flags[0]
    half = own.shape[1] // 2
    total = (own[...] + got[...].astype(F32)).astype(BF16)

    @pl.when(low == 0)
    def _():
        out[...] = total

    @pl.when(low == 1)
    def _():
        out[:, :half] = total[:, half:]
        out[:, half:] = total[:, :half]


def shards(
    layer_in,
    seq_lengths,
    w_qkv,
    q_bias,
    v_bias,
    w_out,
    b_out,
    ln1_gain,
    ln1_bias,
    w_in,
    b_in,
    w_back,
    b_back,
    ln2_gain,
    ln2_bias,
    out_grad,
):
    n_rows = lax.axis_size("row")
    row, col = lax.axis_index("row"), lax.axis_index("col")
    low_bit = (col % 2) == 1
    odd_bit = lax.axis_index("dp") % 2
    odd = odd_bit == 1
    feats, slot = layer_in.shape
    half = slot // 2
    width = w_out.shape[0]
    model = n_rows * feats
    units = w_in.shape[1]
    heads = width // HEAD_DIM
    length = lax.dynamic_index_in_dim(seq_lengths, row, 0, False)
    flags = jnp.stack((col % 2, odd_bit, col, length, col // 2)).astype(jnp.int32)
    halves = shape((model, half), BF16)
    wide_halves = shape((model, half), F32)

    def sum_cores(mine, other):
        return (mine + swap_bit(other, "col", 1).astype(F32)).astype(BF16)

    x0 = to_slot(layer_in)
    qkv_part = w_qkv.transpose(1, 2, 0).reshape(3 * width, feats)
    n_half = 2 * width
    pack_half = jnp.where(
        odd, jnp.concatenate((qkv_part[n_half:], w_out)), qkv_part[:n_half]
    )
    fetched = [from_row(pack_half, k) for k in range(1, n_rows)]
    x2 = swap_bit(x0, "col", 2)
    x1 = swap_bit(x0, "col", 1)
    x3 = swap_bit(x2, "col", 1)
    swapped = [swap_bit(part, "dp", 1) for part in fetched]

    vectors = jnp.concatenate((b_out, ln1_gain, ln1_bias, b_back, ln2_gain, ln2_bias))
    vectors = jnp.pad(vectors.reshape(6, feats), ((0, 10), (0, units - feats)))
    wide = jnp.concatenate((jnp.where(odd, w_back, w_in), vectors))
    wide = after(wide, *fetched)
    wide_fetched = [from_row(wide, k) for k in range(1, n_rows)]
    wide_swapped = [swap_bit(part, "dp", 1) for part in wide_fetched]
    in_all = jnp.concatenate(
        [w_in]
        + [jnp.where(odd, o[:feats], f[:feats]) for f, o in zip(wide_fetched, wide_swapped)]
    )
    back_all = jnp.concatenate(
        [w_back]
        + [jnp.where(odd, f[:feats], o[:feats]) for f, o in zip(wide_fetched, wide_swapped)]
    )
    at_vectors = pl.BlockSpec((16, units), lambda _: (feats // 16, 0))
    (vecs,) = call(
        vector_kernel,
        "vectors",
        [shape((model, 16), F32)],
        [vectors] + wide_fetched,
        specs={k: at_vectors for k in range(1, n_rows)},
    )

    qkv_bias = jnp.concatenate((q_bias, jnp.zeros_like(q_bias), v_bias)).astype(F32)[:, None]
    xs, packs, qkv, prob, context, mine, other = call(
        attend_kernel,
        "attend",
        [
            shape((model, slot), BF16),
            shape((n_rows, 4 * width, feats), BF16),
            shape((3 * width, slot), BF16),
            shape((heads, slot, slot), BF16),
            shape((width, slot), BF16),
            wide_halves,
            halves,
        ],
        [flags, x0, x1, x2, x3, qkv_part, w_out] + fetched + swapped + [qkv_bias],
        flops=8 * model * width * slot + 4 * slot * slot * width,
    )

    g_own = to_slot(after(out_grad.astype(BF16), xs))
    g_high = swap_bit(g_own, "col", 2)
    g_both = jnp.concatenate((g_own, g_high))
    g_low = swap_bit(jnp.where(low_bit, g_both[:, :half], g_both[:, half:]), "col", 1)

    own = sum_cores(mine, other)
    away = swap_bit(own, "col", 2)
    scaled_one, inverse_one, n_own = call(
        norm_kernel,
        "norm",
        [wide_halves, shape((8, half), F32), halves],
        [xs, own, away, vecs],
        specs={0: pl.BlockSpec((model, half), lambda _: (0, 0))},
    )
    n_away = swap_bit(n_own, "col", 1)
    hidden, slope, mine, other = call(
        forward_kernel,
        "feed_forward",
        [shape((units, slot), BF16), shape((units, slot), BF16), wide_halves, halves],
        [n_own, n_away, in_all, back_all, b_in.astype(F32)[:, None]],
        flops=4 * model * units * slot,
    )
    own = sum_cores(mine, other)
    away = swap_bit(own, "col", 2)
    out_own, out_give, grad_second, r_own, sums = call(
        turn_kernel,
        "turn",
        [
            shape((feats, half), BF16),
            shape((feats, half), BF16),
            wide_halves,
            halves,
            shape((8, model), F32),
        ],
        [flags, scaled_one, own, away, vecs, g_own, g_high, g_low],
        scratch=[pltpu.VMEM((model, half), BF16), pltpu.VMEM((model, half), BF16)],
    )
    r_away = swap_bit(r_own, "col", 1)
    mine, other, grad_pre, b_in_sums = call(
        backward_kernel,
        "feed_backward",
        [wide_halves, halves, shape((units, slot), BF16), shape((8, feats), F32)],
        [r_own, r_away, slope, in_all, back_all],
        flops=4 * model * units * slot,
    )
    own = sum_cores(mine, other)
    wide_grads = call(
        wide_grad_kernel,
        "wide_grads",
        [shape((feats, units), BF16)] * (2 * n_rows),
        [after(r_own, own), r_away, hidden, n_own, n_away, grad_pre],
        flops=4 * model * units * slot,
    )
    away = swap_bit(own, "col", 2)
    grad_first, a_own, sums = call(
        norm_back_kernel,
        "norm_back",
        [wide_halves, halves, shape((8, model), F32)],
        [own, away, grad_second, scaled_one, inverse_one, vecs, sums],
    )
    a_away = swap_bit(a_own, "col", 1)
    sums_away = swap_bit(sums, "col", 1)
    grad_qkv, kept, give = call(
        attend_back_kernel,
        "attend_back",
        [
            shape((3 * width, slot), BF16),
            shape((2 * feats, slot), F32),
            shape((2 * feats, slot), BF16),
        ],
        [flags, a_own, a_away, packs, qkv, prob, grad_first],
        flops=8 * model * width * slot + 10 * slot * slot * width,
        scratch=[pltpu.VMEM((width, slot), BF16)],
    )

    in_own, in_away = call(
        join_kernel,
        "join",
        [shape((feats, slot), F32), shape((feats, slot), BF16)],
        [flags, kept, swap_bit(give, "col", 1)],
    )
    (in_grad,) = call(
        finish_kernel,
        "finish",
        [shape((feats, slot), BF16)],
        [flags, in_own, swap_bit(in_away, "col", 2)],
    )
    in_grad = from_slot(in_grad).astype(F32)

    out_give = after(out_give, a_own)
    layer_out = from_slot(ordered(low_bit, out_own, swap_bit(out_give, "col", 1), 1))

    def add_rows(blocks):
        terms = [blocks[0]] + [from_row(blocks[k], n_rows - k) for k in range(1, n_rows)]
        terms = [term.astype(F32) for term in terms]
        while len(terms) > 1:
            pairs = len(terms) // 2
            terms = [terms[i] + terms[i + pairs] for i in range(pairs)]
        return terms[0].astype(BF16)

    def add_replicas(total, first):
        bit = first
        while bit < lax.axis_size("dp"):
            total = total.astype(F32) + swap_bit(total, "dp", bit).astype(F32)
            total = total.astype(BF16)
            bit *= 2
        return total

    pack_keep, pack_give = call(
        pack_grad_kernel,
        "pack_grads",
        [shape((n_rows, 2 * width + EXTRA // 2, feats), BF16)] * 2,
        [flags, xs, grad_qkv, a_own, a_away, context, sums, sums_away, b_in_sums],
        flops=8 * model * width * slot,
        scratch=[pltpu.VMEM((4 * width + EXTRA, feats), BF16)],
    )
    w_back_grad = add_replicas(add_rows(wide_grads[:n_rows]), 1).astype(F32)
    w_in_grad = add_replicas(add_rows(wide_grads[n_rows:]), 1).astype(F32)
    pack_got = swap_bit(pack_give, "dp", 1)
    total = add_rows(
        [
            (pack_keep[k].astype(F32) + pack_got[k].astype(F32)).astype(BF16)
            for k in range(n_rows)
        ]
    )
    total = add_replicas(total, 2)
    total = ordered(odd, total, swap_bit(total, "dp", 1), 0).astype(F32)
    w_qkv_grad = total[: 3 * width].reshape(3, width, feats).transpose(2, 0, 1)
    w_out_grad = total[3 * width : 4 * width]
    tail = total[4 * width :]
    return (
        layer_out,
        in_grad,
        w_qkv_grad,
        tail[12],
        tail[13],
        w_out_grad,
        tail[4],
        tail[0],
        tail[1],
        w_in_grad,
        tail[8:12].reshape(-1),
        w_back_grad,
        tail[5],
        tail[2],
        tail[3],
    )


def solution(mesh):
    tokens = P("row", ("dp", "col"))
    block = P("row", "col")
    in_specs = (
        tokens,
        P("dp"),
        P("row", None, "col"),
        P("col"),
        P("col"),
        P("col", "row"),
        P("row"),
        P("row"),
        P("row"),
        block,
        P("col"),
        block,
        P("row"),
        P("row"),
        P("row"),
        tokens,
    )
    out_specs = (
        tokens,
        tokens,
        P("row", None, "col"),
        P("col"),
        P("col"),
        P("col", "row"),
        P("row"),
        P("row"),
        P("row"),
        block,
        P("col"),
        block,
        P("row"),
        P("row"),
        P("row"),
    )
    return jax.shard_map(shards, mesh=mesh, in_specs=in_specs, out_specs=out_specs, check_vma=False)
```

```python
import jax
import jax.numpy as jnp
from jax import lax
from jax.experimental import pallas as pl
from jax.experimental.pallas import tpu as pltpu
from jax.sharding import PartitionSpec as P

HEAD_DIM = 64
EPSILON = 1e-12
F32 = jnp.float32
BF16 = jnp.bfloat16
EXTRA = 32


def dot(left, right, left_dim, right_dim):
    return lax.dot_general(
        left, right, (((left_dim,), (right_dim,)), ((), ())), preferred_element_type=F32
    )


def call(kernel, name, outs, args, weight=1, scratch=(), specs=None, windowed=False, vmem_mib=16):
    vmem = pl.BlockSpec(memory_space=pltpu.VMEM)
    in_specs = [
        pl.BlockSpec(memory_space=pltpu.SMEM) if arg.dtype == jnp.int32 else vmem for arg in args
    ]
    for at, spec in (specs or {}).items():
        in_specs[at] = spec
    return pl.pallas_call(
        kernel,
        name=name,
        out_shape=outs,
        grid=(1,) if windowed else (),
        in_specs=in_specs,
        out_specs=[vmem] * len(outs),
        scratch_shapes=list(scratch),
        compiler_params=pltpu.CompilerParams(vmem_limit_bytes=vmem_mib * 1024 * 1024),
        cost_estimate=pl.CostEstimate(
            flops=weight * 2**30, bytes_accessed=weight * 2**22, transcendentals=0
        ),
    )(*args)


def shape(dims, dtype):
    return jax.ShapeDtypeStruct(dims, dtype)


def swap_bit(value, axis, bit):
    size = lax.axis_size(axis)
    return lax.ppermute(value, axis, [(at, at ^ bit) for at in range(size)])


def grid_pairs():
    size = lax.axis_size("row")
    return [
        (a * size + b, b * size + (a - b) % size) for a in range(size) for b in range(size)
    ]


def to_slot(value):
    return lax.ppermute(value, ("row", "col"), grid_pairs())


def from_slot(value):
    return lax.ppermute(value, ("row", "col"), [(b, a) for a, b in grid_pairs()])


def from_row(value, away):
    size = lax.axis_size("row")
    return lax.ppermute(value, "row", [((a + away) % size, a) for a in range(size)])


def after(value, *others):
    return lax.optimization_barrier((value,) + others)[0]


def ordered(flag, own, other, axis):
    return jnp.concatenate(
        (jnp.where(flag, other, own), jnp.where(flag, own, other)), axis=axis
    )


def identity(size):
    at = lax.broadcasted_iota(jnp.int32, (size, size), 0)
    return (at == lax.broadcasted_iota(jnp.int32, (size, size), 1)).astype(BF16)


def row_sums(products):
    total = 0.0
    for at, product in products.items():
        pick = lax.broadcasted_iota(jnp.int32, (8, product.shape[1]), 0) == at
        pick = pick.astype(BF16)
        high = product.astype(BF16)
        rest = (product - high.astype(F32)).astype(BF16)
        total = total + dot(pick, high, 1, 1) + dot(pick, rest, 1, 1)
    return total


def half_kernel(odd, w_qkv, w_out, out, sems):
    size = w_out.shape[0]

    def move(copies):
        for copy in copies:
            copy.start()
        for copy in copies:
            copy.wait()

    @pl.when(odd[0] == 0)
    def _():
        move([pltpu.make_async_copy(w_qkv.at[pl.ds(0, 2 * size)], out, sems.at[0])])

    @pl.when(odd[0] == 1)
    def _():
        first, second = out.at[pl.ds(0, size)], out.at[pl.ds(size, size)]
        move(
            [
                pltpu.make_async_copy(w_qkv.at[pl.ds(2 * size, size)], first, sems.at[0]),
                pltpu.make_async_copy(w_out, second, sems.at[1]),
            ]
        )


def attend_kernel(
    flags, x0, x1, x2, x3, w_qkv, w_out, f1, f2, f3, swapped, vectors,
    xs, packs, qkv, prob, context, mine, other, raw, sems,
):
    low, odd, col, length = flags[0], flags[1], flags[2], flags[3]
    feats, slot = x0.shape
    half = slot // 2
    width = w_out.shape[0]
    n_half = f1.shape[0]
    copies = [
        pltpu.make_async_copy(w_qkv, packs.at[0, pl.ds(0, 3 * width)], sems.at[0]),
        pltpu.make_async_copy(w_out, packs.at[0, pl.ds(3 * width, width)], sems.at[1]),
    ]
    for k, f in enumerate((f1, f2, f3)):
        for ref, part in ((f, odd), (swapped.at[pl.ds(k * n_half, n_half)], 1 - odd)):
            rows = pl.ds(pl.multiple_of(part * n_half, n_half), n_half)
            copies += [pltpu.make_async_copy(ref, packs.at[k + 1, rows], sems.at[len(copies)])]
    for bit, ref in enumerate((x0, x1, x2, x3)):
        rows = pl.ds(pl.multiple_of((col ^ bit) * feats, feats), feats)
        copies += [pltpu.make_async_copy(ref, raw.at[rows], sems.at[len(copies)])]
    for copy in copies:
        copy.start()
    for copy in copies:
        copy.wait()

    @pl.when(low == 0)
    def _():
        xs[...] = raw[...]

    @pl.when(low == 1)
    def _():
        xs[:, :half] = raw[:, half:]
        xs[:, half:] = raw[:, :half]

    columns = dot(identity(width), vectors[:, :width], 1, 1)
    for part, bias in enumerate((columns[:, 6:7], 0.0, columns[:, 7:8])):
        total = bias
        for k in range(4):
            block = packs[k, part * feats : (part + 1) * feats]
            total = total + dot(block, xs[k * feats : (k + 1) * feats], 0, 0)
        qkv[part * width : (part + 1) * width] = total.astype(BF16)

    place = lax.broadcasted_iota(jnp.int32, (slot, half), 0)
    place = jnp.where(low == 1, (place + half) % slot, place)
    live = place < length
    scale = HEAD_DIM ** (-0.5)
    for h in range(width // HEAD_DIM):
        q_rows = pl.ds(h * HEAD_DIM, HEAD_DIM)
        k_rows = pl.ds(width + h * HEAD_DIM, HEAD_DIM)
        v_rows = pl.ds(2 * width + h * HEAD_DIM, HEAD_DIM)
        for part in range(2):
            cols = slice(part * half, (part + 1) * half)
            scores = dot(qkv[k_rows, :], qkv[q_rows, cols], 0, 0) * scale
            scores = jnp.where(live, scores, -1000000000.0)
            exponent = jnp.exp(scores - jnp.max(scores, axis=0, keepdims=True))
            inverse = 1.0 / jnp.sum(exponent, axis=0, keepdims=True)
            weights = (exponent * inverse).astype(BF16)
            prob[h, :, cols] = weights
            context[q_rows, cols] = dot(qkv[v_rows, :], weights, 1, 0).astype(BF16)

    for k in range(4):
        rows = slice(k * feats, (k + 1) * feats)
        part = dot(packs[k, 3 * width :], context[...], 0, 0)
        mine[rows] = part[:, :half]
        other[rows] = part[:, half:].astype(BF16)


def assemble_kernel(
    flags, own_in, own_back, v0, f1, f2, f3, s12, s3, w_in, w_back, vecs, bias, rows, sems
):
    odd = flags[1]
    feats = own_in.shape[0]
    first = pl.ds(0, feats)
    copies = [
        pltpu.make_async_copy(own_in, w_in.at[first], sems.at[0]),
        pltpu.make_async_copy(own_back, w_back.at[first], sems.at[1]),
    ]
    size = f1.shape[0]
    for k, (f, s, s_at) in enumerate(((f1, s12, 0), (f2, s12, size), (f3, s3, 0))):
        span = pl.ds((k + 1) * feats, feats)
        s = s.at[pl.ds(s_at, feats)]
        for ref, into in ((f.at[first], (w_in, w_back)), (s, (w_back, w_in))):
            at = len(copies)
            even = pltpu.make_async_copy(ref, into[0].at[span], sems.at[at])
            other = pltpu.make_async_copy(ref, into[1].at[span], sems.at[at])
            copies += [(even, other)]
    for k, ref in enumerate((f1, f2, f3)):
        tail = ref.at[pl.ds(feats, 16)]
        copies += [pltpu.make_async_copy(tail, rows.at[k], sems.at[len(copies)])]
    for begin in (True, False):
        for copy in copies:
            if isinstance(copy, tuple):

                @pl.when(odd == 0)
                def _():
                    copy[0].start() if begin else copy[0].wait()

                @pl.when(odd == 1)
                def _():
                    copy[1].start() if begin else copy[1].wait()

            elif begin:
                copy.start()
            else:
                copy.wait()
    eye = identity(feats)
    vecs[:feats] = dot(eye, v0[:, :feats], 1, 1)
    for k in range(4):
        span = slice(k * feats, (k + 1) * feats)
        bias[span] = dot(eye, v0[:, span], 1, 1)
    for k in range(3):
        span = slice((k + 1) * feats, (k + 2) * feats)
        vecs[span] = dot(eye, rows[k, :, :feats], 1, 1)


def norm_kernel(x, own, away, vecs, scaled, inverse, low_normed):
    first = x[...].astype(F32) + own[...].astype(F32) + away[...].astype(F32) + vecs[:, 0:1]
    center = jnp.mean(first, axis=0, keepdims=True)
    first = first - center
    inv = lax.rsqrt(jnp.mean(first * first, axis=0, keepdims=True) + EPSILON)
    first = first * inv
    scaled[...] = first
    inverse[...] = jnp.broadcast_to(inv, inverse.shape)
    low_normed[...] = (first * vecs[:, 1:2] + vecs[:, 2:3]).astype(BF16)


def forward_kernel(n_own, n_away, w_in, w_back, bias, hidden, slope, mine, other):
    half = n_own.shape[1]
    step = 256
    for part, ref in enumerate((n_own, n_away)):
        cols = slice(part * half, (part + 1) * half)
        for at in range(0, w_in.shape[1], step):
            rows = slice(at, at + step)
            pre = dot(w_in[:, rows], ref[...], 0, 0) + bias[rows, 8:9]
            share = 0.5 * (1.0 + lax.erf(pre * (0.5**0.5)))
            hidden[rows, cols] = (pre * share).astype(BF16)
            bell = jnp.exp(-0.5 * pre * pre) * ((0.5 / jnp.pi) ** 0.5)
            slope[rows, cols] = (share + pre * bell).astype(BF16)
    mine[...] = dot(w_back[...], hidden[:, :half], 1, 0)
    other[...] = dot(w_back[...], hidden[:, half:], 1, 0).astype(BF16)


def turn_kernel(
    flags, scaled_one, own, away, vecs, g_own, g_high, g_low,
    keep, give, grad_second, grad_returned, sums, final, grad,
):
    low, col, length = flags[0], flags[2], flags[3]
    feats = g_own.shape[0]
    half = own.shape[1]

    def rows(bit):
        return pl.ds(pl.multiple_of((col ^ bit) * feats, feats), feats)

    for bit, ref in ((0, g_own), (2, g_high)):

        @pl.when(low == 0)
        def _():
            grad[rows(bit), :] = ref[:, :half]

        @pl.when(low == 1)
        def _():
            grad[rows(bit), :] = ref[:, half:]

    grad[rows(1), :] = g_low[:feats]
    grad[rows(3), :] = g_low[feats:]

    normed = scaled_one[...] * vecs[:, 1:2] + vecs[:, 2:3]
    second = normed + own[...].astype(F32) + away[...].astype(F32) + vecs[:, 3:4]
    second = second - jnp.mean(second, axis=0, keepdims=True)
    inv = lax.rsqrt(jnp.mean(second * second, axis=0, keepdims=True) + EPSILON)
    scaled = second * inv
    place = low * half + lax.broadcasted_iota(jnp.int32, (1, half), 1)
    live = (place < length).astype(F32)
    final[...] = ((scaled * vecs[:, 4:5] + vecs[:, 5:6]) * live).astype(BF16)
    keep[...] = final[rows(0), :]
    give[...] = final[rows(1), :]
    upstream = grad[...].astype(F32) * live
    weighted = upstream * vecs[:, 4:5]
    mean = jnp.mean(weighted, axis=0, keepdims=True)
    tilt = jnp.mean(weighted * scaled, axis=0, keepdims=True)
    back = inv * (weighted - mean - scaled * tilt)
    grad_second[...] = back
    grad_returned[...] = back.astype(BF16)
    sums[...] = row_sums({2: upstream * scaled, 3: upstream, 5: back})


def backward_kernel(r_own, r_away, slope, w_in, w_back, mine, other, grad_pre, b_in_sums):
    half = r_own.shape[1]
    step = 256
    for part, ref in enumerate((r_own, r_away)):
        cols = slice(part * half, (part + 1) * half)
        for at in range(0, w_in.shape[1], step):
            rows = slice(at, at + step)
            grad_hidden = dot(w_back[:, rows], ref[...], 0, 0)
            grad_pre[rows, cols] = (grad_hidden * slope[rows, cols].astype(F32)).astype(BF16)
    mine[...] = dot(w_in[...], grad_pre[:, :half], 1, 0)
    other[...] = dot(w_in[...], grad_pre[:, half:], 1, 0).astype(BF16)
    size = b_in_sums.shape[1]
    total = 0.0
    for k in range(w_in.shape[1] // size):
        pick = lax.broadcasted_iota(jnp.int32, (8, 2 * half), 0) == k
        total = total + dot(pick.astype(BF16), grad_pre[k * size : (k + 1) * size], 1, 1)
    b_in_sums[...] = total


def wide_grad_kernel(
    flags, r_own, r_away, hidden, n_own, n_away, grad_pre, b0, b1, b2, b3, keep, give
):
    odd = flags[1]
    half = r_own.shape[1]
    feats = b0.shape[0]
    part = feats // 2
    for k, out in enumerate((b0, b1, b2, b3)):
        rows = slice(k * feats, (k + 1) * feats)
        total = dot(r_own[rows], hidden[:, :half], 1, 1)
        out[...] = (total + dot(r_away[rows], hidden[:, half:], 1, 1)).astype(BF16)
    for k in range(4):
        for out, at in ((keep, odd), (give, 1 - odd)):
            rows = pl.ds(pl.multiple_of(k * feats + at * part, part), part)
            total = dot(n_own[rows, :], grad_pre[:, :half], 1, 1)
            out[k] = (total + dot(n_away[rows, :], grad_pre[:, half:], 1, 1)).astype(BF16)


def norm_back_kernel(
    own, away, grad_second, scaled, inverse, vecs, sums, grad_first, low_first, sums_out
):
    upstream = grad_second[...] + own[...].astype(F32) + away[...].astype(F32)
    weighted = upstream * vecs[:, 1:2]
    mean = jnp.mean(weighted, axis=0, keepdims=True)
    tilt = jnp.mean(weighted * scaled[...], axis=0, keepdims=True)
    back = inverse[0:1] * (weighted - mean - scaled[...] * tilt)
    grad_first[...] = back
    low_first[...] = back.astype(BF16)
    sums_out[...] = sums[...] + row_sums({0: upstream * scaled[...], 1: upstream, 4: back})


def attend_back_kernel(
    flags, a_own, a_away, packs, qkv, prob, grad_first, grad_qkv, keep, give, grad_context
):
    low = flags[0]
    half = a_own.shape[1]
    feats = packs.shape[2]
    width = grad_context.shape[0]
    for part, ref in enumerate((a_own, a_away)):
        cols = slice(part * half, (part + 1) * half)
        total = 0.0
        for k in range(4):
            total = total + dot(
                packs[k, 3 * width :], ref[k * feats : (k + 1) * feats], 1, 0
            )
        grad_context[:, cols] = total.astype(BF16)
    scale = HEAD_DIM ** (-0.5)
    for h in range(width // HEAD_DIM):
        q_rows = pl.ds(h * HEAD_DIM, HEAD_DIM)
        k_rows = pl.ds(width + h * HEAD_DIM, HEAD_DIM)
        v_rows = pl.ds(2 * width + h * HEAD_DIM, HEAD_DIM)
        grad_keys, grad_values = 0.0, 0.0
        for part in range(2):
            cols = slice(part * half, (part + 1) * half)
            weights = prob[h, :, cols]
            wide = weights.astype(F32)
            grad_weights = dot(qkv[v_rows, :], grad_context[q_rows, cols], 0, 0)
            inner = jnp.sum(wide * grad_weights, axis=0, keepdims=True)
            grad_scores = (wide * (grad_weights - inner)).astype(BF16)
            grad_qkv[q_rows, cols] = (dot(qkv[k_rows, :], grad_scores, 1, 0) * scale).astype(BF16)
            grad_keys = grad_keys + dot(qkv[q_rows, cols], grad_scores, 1, 1)
            grad_values = grad_values + dot(grad_context[q_rows, cols], weights, 1, 1)
        grad_qkv[k_rows, :] = (grad_keys * scale).astype(BF16)
        grad_qkv[v_rows, :] = grad_values.astype(BF16)

    def block(k):
        part = 0.0
        for at in range(3):
            left = packs[k, at * feats : (at + 1) * feats]
            part = part + dot(left, grad_qkv[at * width : (at + 1) * width], 1, 0)
        rows = pl.ds(pl.multiple_of(k * feats, feats), feats)
        return part[:, :half] + 0.5 * grad_first[rows, :], part[:, half:]

    for j in range(2):
        rows = slice(j * feats, (j + 1) * feats)
        near, far = block(2 * j + 1 - low)
        give[rows, :half] = near.astype(BF16)
        give[rows, half:] = far.astype(BF16)
        near, far = block(2 * j + low)
        keep[rows, :half] = near
        keep[rows, half:] = far


def pack_grad_kernel(
    flags, xs, grad_qkv, a_own, a_away, context, sums, sums_away, b_in_sums, keep, give, pack
):
    odd = flags[1]
    feats = pack.shape[1]
    width = context.shape[0]
    half = a_own.shape[1]
    rows = keep.shape[1]
    ones = (lax.broadcasted_iota(jnp.int32, (8, 2 * half), 0) == 4).astype(BF16)
    more = (lax.broadcasted_iota(jnp.int32, (8, 2 * half), 0) == 5).astype(BF16)
    shared = b_in_sums[...] + dot(ones, grad_qkv[:width], 1, 1)
    shared = shared + dot(more, grad_qkv[2 * width :], 1, 1)
    vector_sums = sums[...] + sums_away[...]
    for k in range(4):
        span = slice(k * feats, (k + 1) * feats)
        for at in range(3):
            part = dot(xs[span], grad_qkv[at * width : (at + 1) * width], 1, 1)
            pack[at * feats : (at + 1) * feats] = part.astype(BF16)
        total = dot(context[:, :half], a_own[span], 1, 1)
        total = total + dot(context[:, half:], a_away[span], 1, 1)
        pack[3 * width : 4 * width] = total.astype(BF16)
        tail = jnp.concatenate(
            (vector_sums[:, span], shared, jnp.zeros((EXTRA - 16, feats), F32)), axis=0
        )
        pack[4 * width :] = tail.astype(BF16)

        @pl.when(odd == 0)
        def _():
            keep[k] = pack[:rows]
            give[k] = pack[rows:]

        @pl.when(odd == 1)
        def _():
            keep[k] = pack[rows:]
            give[k] = pack[:rows]


def join_kernel(flags, kept, got, own, away):
    high = flags[4]
    feats = own.shape[0]
    half = own.shape[1] // 2
    for out, at in ((own, high), (away, 1 - high)):
        rows = pl.ds(pl.multiple_of(at * feats, feats), feats)
        near = kept[rows, :half] + got[rows, half:].astype(F32)
        far = kept[rows, half:] + got[rows, :half].astype(F32)
        out[:, :half] = near.astype(out.dtype)
        out[:, half:] = far.astype(out.dtype)


def finish_kernel(flags, own, got, out):
    low = flags[0]
    half = own.shape[1] // 2
    total = (own[...] + got[...].astype(F32)).astype(BF16)

    @pl.when(low == 0)
    def _():
        out[...] = total

    @pl.when(low == 1)
    def _():
        out[:, :half] = total[:, half:]
        out[:, half:] = total[:, :half]


def shards(
    layer_in,
    seq_lengths,
    w_qkv,
    q_bias,
    v_bias,
    w_out,
    b_out,
    ln1_gain,
    ln1_bias,
    w_in,
    b_in,
    w_back,
    b_back,
    ln2_gain,
    ln2_bias,
    out_grad,
):
    n_rows = lax.axis_size("row")
    row, col = lax.axis_index("row"), lax.axis_index("col")
    low_bit = (col % 2) == 1
    odd_bit = lax.axis_index("dp") % 2
    odd = odd_bit == 1
    feats, slot = layer_in.shape
    half = slot // 2
    width = w_out.shape[0]
    model = n_rows * feats
    units = w_in.shape[1]
    heads = width // HEAD_DIM
    length = lax.dynamic_index_in_dim(seq_lengths, row, 0, False)
    flags = jnp.stack((col % 2, odd_bit, col, length, col // 2, row)).astype(jnp.int32)
    halves = shape((model, half), BF16)
    wide_halves = shape((model, half), F32)

    def sum_cores(mine, other):
        return (mine + swap_bit(other, "col", 1).astype(F32)).astype(BF16)

    def add_rows(blocks, *gates):
        terms = [blocks[0]]
        terms += [after(from_row(blocks[k], n_rows - k), *gates) for k in range(1, n_rows)]
        terms = [term.astype(F32) for term in terms]
        while len(terms) > 1:
            pairs = len(terms) // 2
            terms = [terms[i] + terms[i + pairs] for i in range(pairs)]
        return terms[0].astype(BF16)

    def add_replicas(total, first):
        bit = first
        while bit < lax.axis_size("dp"):
            total = total.astype(F32) + swap_bit(total, "dp", bit).astype(F32)
            total = total.astype(BF16)
            bit *= 2
        return total

    def add_shares(keep, got):
        total = add_rows(
            [(keep[k].astype(F32) + got[k].astype(F32)).astype(BF16) for k in range(n_rows)]
        )
        total = add_replicas(total, 2)
        return ordered(odd, total, swap_bit(total, "dp", 1), 0)

    x0 = to_slot(layer_in)
    qkv_part = w_qkv.transpose(1, 0, 2).reshape(3 * feats, width)
    n_half = 2 * feats
    (pack_half,) = call(
        half_kernel,
        "half",
        [shape((n_half, width), BF16)],
        [odd_bit.reshape(1), qkv_part, w_out],
        specs={k: pl.BlockSpec(memory_space=pl.ANY) for k in (1, 2)},
        scratch=[pltpu.SemaphoreType.DMA((2,))],
    )
    fetched = [from_row(pack_half, k) for k in range(1, n_rows)]
    vectors = jnp.concatenate(
        (b_out, ln1_gain, ln1_bias, b_back, ln2_gain, ln2_bias, q_bias, v_bias)
    )
    vectors = jnp.pad(vectors.reshape(8, feats), ((0, 0), (0, units - feats)))
    vectors = jnp.concatenate((vectors, jnp.pad(b_in[None], ((0, 7), (0, 0)))))
    wide = jnp.concatenate((jnp.where(odd, w_back, w_in), vectors))
    x0 = after(x0, flags, wide, *fetched)
    x2 = swap_bit(x0, "col", 2)
    x1 = swap_bit(x0, "col", 1)
    swapped = swap_bit(jnp.concatenate(fetched), "dp", 1)
    wide = after(wide, *fetched)
    wide_fetched = [from_row(wide, 1)]
    wide_fetched += [from_row(after(wide, wide_fetched[0]), k) for k in range(2, n_rows)]
    wide_swapped = [
        swap_bit(jnp.concatenate(wide_fetched[:2]), "dp", 1),
        swap_bit(wide_fetched[2], "dp", 1),
    ]
    x3 = swap_bit(after(x2, swapped, wide_fetched[0]), "col", 1)

    in_all, back_all, vecs, in_bias = call(
        assemble_kernel,
        "assemble",
        [shape((model, units), BF16)] * 2 + [shape((model, 16), F32), shape((units, 16), F32)],
        [flags, w_in, w_back, vectors] + wide_fetched + wide_swapped,
        specs={k: pl.BlockSpec(memory_space=pl.ANY) for k in (1, 2, 4, 5, 6, 7, 8)},
        scratch=[pltpu.VMEM((3, 16, units), BF16), pltpu.SemaphoreType.DMA((11,))],
        vmem_mib=56,
        weight=2,
    )

    xs, packs, qkv, prob, context, mine, other = call(
        attend_kernel,
        "attend",
        [
            shape((model, slot), BF16),
            shape((n_rows, 4 * width, feats), BF16),
            shape((3 * width, slot), BF16),
            shape((heads, slot, slot), BF16),
            shape((width, slot), BF16),
            wide_halves,
            halves,
        ],
        [flags, x0, x1, x2, x3, qkv_part, w_out] + fetched + [swapped, vectors],
        specs={k: pl.BlockSpec(memory_space=pl.ANY) for k in range(1, 11)},
        scratch=[pltpu.VMEM((model, slot), BF16), pltpu.SemaphoreType.DMA((12,))],
        vmem_mib=56,
        weight=12,
    )

    own = sum_cores(mine, other)
    away = swap_bit(own, "col", 2)
    scaled_one, inverse_one, n_own = call(
        norm_kernel,
        "norm",
        [wide_halves, shape((8, half), F32), halves],
        [xs, own, away, vecs],
        specs={0: pl.BlockSpec((model, half), lambda _: (0, 0))},
        windowed=True,
        weight=2,
    )
    g_own = to_slot(after(out_grad.astype(BF16), wide_fetched[2]))
    g_high = swap_bit(after(g_own, scaled_one), "col", 2)

    n_away = swap_bit(n_own, "col", 1)
    hidden, slope, mine, other = call(
        forward_kernel,
        "feed_forward",
        [shape((units, slot), BF16), shape((units, slot), BF16), wide_halves, halves],
        [n_own, n_away, in_all, back_all, in_bias],
        weight=6,
    )
    g_both = jnp.concatenate((after(g_own, hidden), g_high))
    g_low = swap_bit(jnp.where(low_bit, g_both[:, :half], g_both[:, half:]), "col", 1)
    own = sum_cores(after(mine, g_low), other)
    away = swap_bit(own, "col", 2)
    out_own, out_give, grad_second, r_own, sums = call(
        turn_kernel,
        "turn",
        [
            shape((feats, half), BF16),
            shape((feats, half), BF16),
            wide_halves,
            halves,
            shape((8, model), F32),
        ],
        [flags, scaled_one, own, away, vecs, g_own, g_high, g_low],
        scratch=[pltpu.VMEM((model, half), BF16), pltpu.VMEM((model, half), BF16)],
        weight=4,
    )
    r_away = swap_bit(r_own, "col", 1)
    mine, other, grad_pre, b_in_sums = call(
        backward_kernel,
        "feed_backward",
        [wide_halves, halves, shape((units, slot), BF16), shape((8, feats), F32)],
        [r_own, r_away, slope, in_all, back_all],
        weight=3,
    )
    own = sum_cores(mine, other)
    *back_grads, into_keep, into_give = call(
        wide_grad_kernel,
        "wide_grads",
        [shape((feats, units), BF16)] * n_rows + [shape((n_rows, feats // 2, units), BF16)] * 2,
        [flags, after(r_own, own), r_away, hidden, n_own, n_away, grad_pre],
        weight=8,
    )
    away = swap_bit(own, "col", 2)
    grad_first, a_own, sums = call(
        norm_back_kernel,
        "norm_back",
        [wide_halves, halves, shape((8, model), F32)],
        [own, after(away, into_give), grad_second, scaled_one, inverse_one, vecs, sums],
        weight=2,
    )
    a_away = swap_bit(a_own, "col", 1)
    sums_away = swap_bit(sums, "col", 1)
    grad_qkv, kept, give = call(
        attend_back_kernel,
        "attend_back",
        [
            shape((3 * width, slot), BF16),
            shape((2 * feats, slot), F32),
            shape((2 * feats, slot), BF16),
        ],
        [flags, a_own, a_away, packs, qkv, prob, grad_first],
        scratch=[pltpu.VMEM((width, slot), BF16)],
        weight=8,
    )

    pack_keep, pack_give = call(
        pack_grad_kernel,
        "pack_grads",
        [shape((n_rows, 2 * width + EXTRA // 2, feats), BF16)] * 2,
        [flags, xs, grad_qkv, a_own, a_away, context, sums, sums_away, b_in_sums],
        scratch=[pltpu.VMEM((4 * width + EXTRA, feats), BF16)],
        weight=5,
    )

    in_own, in_away = call(
        join_kernel,
        "join",
        [shape((feats, slot), F32), shape((feats, slot), BF16)],
        [flags, after(kept, pack_give), swap_bit(give, "col", 1)],
    )
    (in_done,) = call(
        finish_kernel,
        "finish",
        [shape((feats, slot), BF16)],
        [flags, in_own, swap_bit(in_away, "col", 2)],
    )
    in_grad = from_slot(in_done).astype(F32)

    into_got = swap_bit(into_give, "dp", 1)

    out_give = after(out_give, in_away)
    layer_out = from_slot(ordered(low_bit, out_own, swap_bit(out_give, "col", 1), 1))

    w_back_grad = add_replicas(add_rows(back_grads, in_away), 1).astype(F32)
    w_in_grad = add_shares(into_keep, after(into_got, in_away)).astype(F32)
    pack_got = swap_bit(pack_give, "dp", 1)
    total = add_shares(pack_keep, after(pack_got, in_done)).astype(F32)
    w_qkv_grad = total[: 3 * feats].reshape(3, feats, width).transpose(1, 0, 2)
    w_out_grad = total[3 * width : 4 * width]
    tail = total[4 * width :]
    return (
        layer_out,
        in_grad,
        w_qkv_grad,
        tail[12],
        tail[13],
        w_out_grad,
        tail[4],
        tail[0],
        tail[1],
        w_in_grad,
        tail[8:12].reshape(-1),
        w_back_grad,
        tail[5],
        tail[2],
        tail[3],
    )


def solution(mesh):
    tokens = P("row", ("dp", "col"))
    block = P("row", "col")
    in_specs = (
        tokens,
        P("dp"),
        P("row", None, "col"),
        P("col"),
        P("col"),
        P("col", "row"),
        P("row"),
        P("row"),
        P("row"),
        block,
        P("col"),
        block,
        P("row"),
        P("row"),
        P("row"),
        tokens,
    )
    out_specs = (
        tokens,
        tokens,
        P("row", None, "col"),
        P("col"),
        P("col"),
        P("col", "row"),
        P("row"),
        P("row"),
        P("row"),
        block,
        P("col"),
        block,
        P("row"),
        P("row"),
        P("row"),
    )
    return jax.shard_map(shards, mesh=mesh, in_specs=in_specs, out_specs=out_specs, check_vma=False)
```

```python
import jax
import jax.numpy as jnp
from jax import lax
from jax.experimental import pallas as pl
from jax.experimental.pallas import tpu as pltpu
from jax.sharding import PartitionSpec as P

HEAD_DIM = 64
EPSILON = 1e-12
F32 = jnp.float32
BF16 = jnp.bfloat16
EXTRA = 32


def dot(left, right, left_dim, right_dim):
    return lax.dot_general(
        left, right, (((left_dim,), (right_dim,)), ((), ())), preferred_element_type=F32
    )


def call(kernel, name, outs, args, weight=0, scratch=(), specs=None, windowed=False, vmem_mib=16, out_specs=None):
    vmem = pl.BlockSpec(memory_space=pltpu.VMEM)
    in_specs = [
        pl.BlockSpec(memory_space=pltpu.SMEM) if arg.dtype == jnp.int32 else vmem for arg in args
    ]
    for at, spec in (specs or {}).items():
        in_specs[at] = spec
    return pl.pallas_call(
        kernel,
        name=name,
        out_shape=outs,
        grid=(1,) if windowed else (),
        in_specs=in_specs,
        out_specs=out_specs or [vmem] * len(outs),
        scratch_shapes=list(scratch),
        compiler_params=pltpu.CompilerParams(vmem_limit_bytes=vmem_mib * 1024 * 1024),
        cost_estimate=pl.CostEstimate(
            flops=weight * 2**30, bytes_accessed=weight * 2**22, transcendentals=0
        ),
    )(*args)


def shape(dims, dtype):
    return jax.ShapeDtypeStruct(dims, dtype)


def swap_bit(value, axis, bit):
    size = lax.axis_size(axis)
    return lax.ppermute(value, axis, [(at, at ^ bit) for at in range(size)])


def plane_of(slot):
    return (slot % 2) * 2 + slot // 2


def grid_pairs():
    size = lax.axis_size("row")
    return [
        (a * size + b, plane_of(b) * size + (a - plane_of(b)) % size)
        for a in range(size)
        for b in range(size)
    ]


def to_slot(value):
    return lax.ppermute(value, ("row", "col"), grid_pairs())


def from_slot(value):
    return lax.ppermute(value, ("row", "col"), [(b, a) for a, b in grid_pairs()])


def from_row(value, away):
    size = lax.axis_size("row")
    return lax.ppermute(value, "row", [((a + away) % size, a) for a in range(size)])


def after(value, *others):
    return lax.optimization_barrier((value,) + others)[0]


def ordered(flag, own, other, axis):
    return jnp.concatenate(
        (jnp.where(flag, other, own), jnp.where(flag, own, other)), axis=axis
    )


def identity(size):
    at = lax.broadcasted_iota(jnp.int32, (size, size), 0)
    return (at == lax.broadcasted_iota(jnp.int32, (size, size), 1)).astype(BF16)


def row_sums(products):
    total = 0.0
    for at, product in products.items():
        pick = lax.broadcasted_iota(jnp.int32, (8, product.shape[1]), 0) == at
        pick = pick.astype(BF16)
        high = product.astype(BF16)
        rest = (product - high.astype(F32)).astype(BF16)
        total = total + dot(pick, high, 1, 1) + dot(pick, rest, 1, 1)
    return total


def send_kernel(
    odd, w_qkv, w_out, w_in, w_back, b_in, v0, v1, v2, v3, v4, v5, v6, v7,
    half, wide, vectors, blocks, long_line, sems, *lines,
):
    size = w_out.shape[0]
    feats = w_in.shape[0]
    copies = [pltpu.make_async_copy(b_in, long_line, sems.at[0])]
    for at, ref in enumerate((v0, v1, v2, v3, v4, v5, v6, v7)):
        copies += [pltpu.make_async_copy(ref, lines[at], sems.at[at + 1])]
    into = wide.at[pl.ds(0, feats)]
    for part in range(2):

        @pl.when(odd[0] == part)
        def _():
            pltpu.make_async_copy((w_in, w_back)[part], into, sems.at[9]).start()
            first = w_qkv.at[pl.ds(2 * part * size, size)]
            pltpu.make_async_copy(first, blocks.at[0], sems.at[10]).start()
            second = (w_qkv.at[pl.ds(size, size)], w_out)[part]
            pltpu.make_async_copy(second, blocks.at[1], sems.at[11]).start()

    for copy in copies:
        copy.start()
    vectors[...] = jnp.zeros_like(vectors)
    for copy in copies:
        copy.wait()
    for at in range(8):
        vectors[at : at + 1, :feats] = lines[at][...].reshape(1, feats)
    vectors[8:9, :] = long_line[...].reshape(1, long_line.shape[0])
    wide[feats:] = vectors[...]
    pltpu.make_async_copy(w_in, into, sems.at[9]).wait()
    for at in range(2):
        pltpu.make_async_copy(w_out, blocks.at[at], sems.at[10 + at]).wait()
        half[:, at * size : (at + 1) * size] = blocks[at]


def attend_kernel(
    flags, x0, x1, x2, x3, fetched, swapped, vectors,
    xs, packs, qkv, prob, context, mine, other, raw, sems,
):
    low, odd, col, length = flags[0], flags[1], flags[2], flags[3]
    feats, slot = x0.shape
    half = slot // 2
    width = context.shape[0]
    row = flags[5]
    copies = []
    for k in range(4):
        for ref, part in ((fetched, odd), (swapped, 1 - odd)):
            ref = ref.at[lax.rem(row + k, 4)]
            copies += [pltpu.make_async_copy(ref, packs.at[k, part], sems.at[len(copies)])]
    for bit, ref in enumerate((x0, x1, x2, x3)):
        rows = pl.ds(pl.multiple_of((col ^ bit) * feats, feats), feats)
        copies += [pltpu.make_async_copy(ref, raw.at[rows], sems.at[len(copies)])]
    for copy in copies:
        copy.start()
    for copy in copies:
        copy.wait()

    @pl.when(low == 0)
    def _():
        xs[...] = raw[...]

    @pl.when(low == 1)
    def _():
        xs[:, :half] = raw[:, half:]
        xs[:, half:] = raw[:, :half]

    columns = dot(identity(width), vectors[:, :width], 1, 1)
    for part, bias in enumerate((columns[:, 6:7], 0.0, columns[:, 7:8])):
        total = bias
        for k in range(4):
            block = packs[k, part // 2, :, part % 2 * width : (part % 2 + 1) * width]
            total = total + dot(block, xs[k * feats : (k + 1) * feats], 0, 0)
        qkv[part * width : (part + 1) * width] = total.astype(BF16)

    place = lax.broadcasted_iota(jnp.int32, (slot, half), 0)
    place = jnp.where(low == 1, (place + half) % slot, place)
    live = place < length
    scale = HEAD_DIM ** (-0.5)
    for h in range(width // HEAD_DIM):
        q_rows = pl.ds(h * HEAD_DIM, HEAD_DIM)
        k_rows = pl.ds(width + h * HEAD_DIM, HEAD_DIM)
        v_rows = pl.ds(2 * width + h * HEAD_DIM, HEAD_DIM)
        for part in range(2):
            cols = slice(part * half, (part + 1) * half)
            scores = dot(qkv[k_rows, :], qkv[q_rows, cols], 0, 0) * scale
            scores = jnp.where(live, scores, -1000000000.0)
            exponent = jnp.exp(scores - jnp.max(scores, axis=0, keepdims=True))
            inverse = 1.0 / jnp.sum(exponent, axis=0, keepdims=True)
            weights = (exponent * inverse).astype(BF16)
            prob[h, :, cols] = weights
            context[q_rows, cols] = dot(qkv[v_rows, :], weights, 1, 0).astype(BF16)

    for k in range(4):
        rows = slice(k * feats, (k + 1) * feats)
        part = dot(packs[k, 1, :, width:], context[...], 0, 0)
        mine[rows] = part[:, :half]
        other[rows] = part[:, half:].astype(BF16)


def assemble_kernel(
    flags, own_in, own_back, v0, f1, f2, f3, s1, s2, s3, w_in, w_back, vecs, bias, rows, sems
):
    odd = flags[1]
    feats = own_in.shape[0]
    first = pl.ds(0, feats)
    copies = [
        pltpu.make_async_copy(own_in, w_in.at[first], sems.at[0]),
        pltpu.make_async_copy(own_back, w_back.at[first], sems.at[1]),
    ]
    for k, (f, s) in enumerate(((f1, s1), (f2, s2), (f3, s3))):
        span = pl.ds((k + 1) * feats, feats)
        for ref, into in ((f, (w_in, w_back)), (s, (w_back, w_in))):
            at = len(copies)
            ref = ref.at[first]
            even = pltpu.make_async_copy(ref, into[0].at[span], sems.at[at])
            other = pltpu.make_async_copy(ref, into[1].at[span], sems.at[at])
            copies += [(even, other)]
    for k, ref in enumerate((f1, f2, f3)):
        tail = ref.at[pl.ds(feats, 16)]
        copies += [pltpu.make_async_copy(tail, rows.at[k], sems.at[len(copies)])]
    for begin in (True, False):
        for copy in copies:
            if isinstance(copy, tuple):

                @pl.when(odd == 0)
                def _():
                    copy[0].start() if begin else copy[0].wait()

                @pl.when(odd == 1)
                def _():
                    copy[1].start() if begin else copy[1].wait()

            elif begin:
                copy.start()
            else:
                copy.wait()
    eye = identity(feats)
    vecs[:feats] = dot(eye, v0[:, :feats], 1, 1)
    for k in range(4):
        span = slice(k * feats, (k + 1) * feats)
        bias[span] = dot(eye, v0[:, span], 1, 1)
    for k in range(3):
        span = slice((k + 1) * feats, (k + 2) * feats)
        vecs[span] = dot(eye, rows[k, :, :feats], 1, 1)


def norm_kernel(x, own, away, vecs, scaled, inverse, low_normed):
    first = x[...].astype(F32) + own[...].astype(F32) + away[...].astype(F32) + vecs[:, 0:1]
    center = jnp.mean(first, axis=0, keepdims=True)
    first = first - center
    inv = lax.rsqrt(jnp.mean(first * first, axis=0, keepdims=True) + EPSILON)
    first = first * inv
    scaled[...] = first
    inverse[...] = jnp.broadcast_to(inv, inverse.shape)
    low_normed[...] = (first * vecs[:, 1:2] + vecs[:, 2:3]).astype(BF16)


def forward_kernel(n_own, n_away, w_in, w_back, bias, hidden, slope, mine, other):
    half = n_own.shape[1]
    step = 256
    for part, ref in enumerate((n_own, n_away)):
        cols = slice(part * half, (part + 1) * half)
        for at in range(0, w_in.shape[1], step):
            rows = slice(at, at + step)
            pre = dot(w_in[:, rows], ref[...], 0, 0) + bias[rows, 8:9]
            share = 0.5 * (1.0 + lax.erf(pre * (0.5**0.5)))
            hidden[rows, cols] = (pre * share).astype(BF16)
            bell = jnp.exp(-0.5 * pre * pre) * ((0.5 / jnp.pi) ** 0.5)
            slope[rows, cols] = (share + pre * bell).astype(BF16)
    mine[...] = dot(w_back[...], hidden[:, :half], 1, 0)
    other[...] = dot(w_back[...], hidden[:, half:], 1, 0).astype(BF16)


def turn_kernel(
    flags, scaled_one, own, away, vecs, g_own, g_high, g_low,
    keep, give, grad_second, grad_returned, sums, final, grad,
):
    low, col, length = flags[0], flags[2], flags[3]
    feats = g_own.shape[0]
    half = own.shape[1]

    def rows(bit):
        return pl.ds(pl.multiple_of((col ^ bit) * feats, feats), feats)

    for bit, ref in ((0, g_own), (2, g_high)):

        @pl.when(low == 0)
        def _():
            grad[rows(bit), :] = ref[:, :half]

        @pl.when(low == 1)
        def _():
            grad[rows(bit), :] = ref[:, half:]

    grad[rows(1), :] = g_low[:feats]
    grad[rows(3), :] = g_low[feats:]

    normed = scaled_one[...] * vecs[:, 1:2] + vecs[:, 2:3]
    second = normed + own[...].astype(F32) + away[...].astype(F32) + vecs[:, 3:4]
    second = second - jnp.mean(second, axis=0, keepdims=True)
    inv = lax.rsqrt(jnp.mean(second * second, axis=0, keepdims=True) + EPSILON)
    scaled = second * inv
    place = low * half + lax.broadcasted_iota(jnp.int32, (1, half), 1)
    live = (place < length).astype(F32)
    final[...] = ((scaled * vecs[:, 4:5] + vecs[:, 5:6]) * live).astype(BF16)
    keep[...] = final[rows(0), :]
    give[...] = final[rows(1), :]
    upstream = grad[...].astype(F32) * live
    weighted = upstream * vecs[:, 4:5]
    mean = jnp.mean(weighted, axis=0, keepdims=True)
    tilt = jnp.mean(weighted * scaled, axis=0, keepdims=True)
    back = inv * (weighted - mean - scaled * tilt)
    grad_second[...] = back
    grad_returned[...] = back.astype(BF16)
    sums[...] = row_sums({2: upstream * scaled, 3: upstream, 5: back})


def backward_kernel(r_own, r_away, slope, w_in, w_back, mine, other, grad_pre, b_in_sums):
    half = r_own.shape[1]
    step = 256
    for part, ref in enumerate((r_own, r_away)):
        cols = slice(part * half, (part + 1) * half)
        for at in range(0, w_in.shape[1], step):
            rows = slice(at, at + step)
            grad_hidden = dot(w_back[:, rows], ref[...], 0, 0)
            grad_pre[rows, cols] = (grad_hidden * slope[rows, cols].astype(F32)).astype(BF16)
    mine[...] = dot(w_in[...], grad_pre[:, :half], 1, 0)
    other[...] = dot(w_in[...], grad_pre[:, half:], 1, 0).astype(BF16)
    size = b_in_sums.shape[1]
    total = 0.0
    for k in range(w_in.shape[1] // size):
        pick = lax.broadcasted_iota(jnp.int32, (8, 2 * half), 0) == k
        total = total + dot(pick.astype(BF16), grad_pre[k * size : (k + 1) * size], 1, 1)
    b_in_sums[...] = total


def wide_grad_kernel(
    flags, r_own, r_away, hidden, n_own, n_away, grad_pre, b_keep, b_give, i_keep, i_give
):
    odd = flags[1]
    half = r_own.shape[1]
    part = b_keep.shape[1]
    for k in range(4):
        for pick, b_out, i_out in ((1 - odd, b_give, i_give), (odd, b_keep, i_keep)):
            rows = pl.ds(pl.multiple_of((2 * k + pick) * part, part), part)
            for out, own, away, right in (
                (b_out, r_own, r_away, hidden),
                (i_out, n_own, n_away, grad_pre),
            ):
                total = dot(own[rows, :], right[:, :half], 1, 1)
                total = total + dot(away[rows, :], right[:, half:], 1, 1)
                out[k] = total.astype(BF16)


def norm_back_kernel(
    own, away, grad_second, scaled, inverse, vecs, sums, grad_first, low_first, sums_out
):
    upstream = grad_second[...] + own[...].astype(F32) + away[...].astype(F32)
    weighted = upstream * vecs[:, 1:2]
    mean = jnp.mean(weighted, axis=0, keepdims=True)
    tilt = jnp.mean(weighted * scaled[...], axis=0, keepdims=True)
    back = inverse[0:1] * (weighted - mean - scaled[...] * tilt)
    grad_first[...] = back
    low_first[...] = back.astype(BF16)
    sums_out[...] = sums[...] + row_sums({0: upstream * scaled[...], 1: upstream, 4: back})


def attend_back_kernel(
    flags, a_own, a_away, packs, qkv, prob, grad_first, grad_qkv, keep, give, grad_context
):
    low = flags[0]
    half = a_own.shape[1]
    feats = packs.shape[2]
    width = grad_context.shape[0]
    for part, ref in enumerate((a_own, a_away)):
        cols = slice(part * half, (part + 1) * half)
        total = 0.0
        for k in range(4):
            total = total + dot(packs[k, 1, :, width:], ref[k * feats : (k + 1) * feats], 1, 0)
        grad_context[:, cols] = total.astype(BF16)
    scale = HEAD_DIM ** (-0.5)
    for h in range(width // HEAD_DIM):
        q_rows = pl.ds(h * HEAD_DIM, HEAD_DIM)
        k_rows = pl.ds(width + h * HEAD_DIM, HEAD_DIM)
        v_rows = pl.ds(2 * width + h * HEAD_DIM, HEAD_DIM)
        grad_keys, grad_values = 0.0, 0.0
        for part in range(2):
            cols = slice(part * half, (part + 1) * half)
            weights = prob[h, :, cols]
            wide = weights.astype(F32)
            grad_weights = dot(qkv[v_rows, :], grad_context[q_rows, cols], 0, 0)
            inner = jnp.sum(wide * grad_weights, axis=0, keepdims=True)
            grad_scores = (wide * (grad_weights - inner)).astype(BF16)
            grad_qkv[q_rows, cols] = (dot(qkv[k_rows, :], grad_scores, 1, 0) * scale).astype(BF16)
            grad_keys = grad_keys + dot(qkv[q_rows, cols], grad_scores, 1, 1)
            grad_values = grad_values + dot(grad_context[q_rows, cols], weights, 1, 1)
        grad_qkv[k_rows, :] = (grad_keys * scale).astype(BF16)
        grad_qkv[v_rows, :] = grad_values.astype(BF16)

    def block(k):
        part = 0.0
        for at in range(3):
            left = packs[k, at // 2, :, at % 2 * width : (at % 2 + 1) * width]
            part = part + dot(left, grad_qkv[at * width : (at + 1) * width], 1, 0)
        rows = pl.ds(pl.multiple_of(k * feats, feats), feats)
        return part[:, :half] + 0.5 * grad_first[rows, :], part[:, half:]

    for j in range(2):
        rows = slice(j * feats, (j + 1) * feats)
        near, far = block(2 * j + 1 - low)
        give[rows, :half] = near.astype(BF16)
        give[rows, half:] = far.astype(BF16)
        near, far = block(2 * j + low)
        keep[rows, :half] = near
        keep[rows, half:] = far


def pack_grad_kernel(
    flags, xs, grad_qkv, a_own, a_away, context, sums, sums_away, b_in_sums, keep, give
):
    odd = flags[1]
    width = context.shape[0]
    feats = keep.shape[1] - 16
    half = a_own.shape[1]
    ones = (lax.broadcasted_iota(jnp.int32, (8, 2 * half), 0) == 4).astype(BF16)
    more = (lax.broadcasted_iota(jnp.int32, (8, 2 * half), 0) == 5).astype(BF16)
    shared = b_in_sums[...] + dot(ones, grad_qkv[:width], 1, 1)
    shared = shared + dot(more, grad_qkv[2 * width :], 1, 1)
    vector_sums = sums[...] + sums_away[...]
    none = jnp.zeros((16, 2 * feats), BF16)
    for k in range(4):
        span = slice(k * feats, (k + 1) * feats)
        blocks = [
            dot(xs[span], grad_qkv[at * width : (at + 1) * width], 1, 1) for at in range(3)
        ]
        last = dot(context[:, :half], a_own[span], 1, 1)
        blocks += [last + dot(context[:, half:], a_away[span], 1, 1)]
        tail = jnp.concatenate((vector_sums[:, span], shared), axis=1)
        tail = jnp.concatenate((tail, jnp.zeros_like(tail)), axis=0).astype(BF16)
        for part in range(2):
            pair = jnp.concatenate(blocks[2 * part : 2 * part + 2], axis=1).astype(BF16)
            rest = none if part else tail
            for out, at in ((keep, odd), (give, 1 - odd)):

                @pl.when(at == part)
                def _():
                    out[k, :feats] = pair
                    out[k, feats:] = rest


def pack_add_kernel(keep, got, *outs):
    for k, out in enumerate(outs):
        out[...] = (keep[k].astype(F32) + got[k].astype(F32)).astype(BF16)


def unpack_kernel(flags, own, got, qkv, w_out, tail):
    odd = flags[1]
    feats, width = w_out.shape[1], w_out.shape[0]

    def write(first, second):
        qkv[:feats] = first[:feats, :width].astype(F32)
        qkv[feats : 2 * feats] = first[:feats, width:].astype(F32)
        qkv[2 * feats :] = second[:feats, :width].astype(F32)
        w_out[...] = second[:feats, width:].astype(F32)
        tail[:16] = first[feats:, :feats].astype(F32)
        tail[16:] = first[feats:, feats:].astype(F32)

    @pl.when(odd == 0)
    def _():
        write(own, got)

    @pl.when(odd == 1)
    def _():
        write(got, own)


def wide_unpack_kernel(flags, b_own, b_got, i_own, i_got, back, into):
    odd = flags[1]
    part = b_own.shape[0]
    for out, own, got in ((back, b_own, b_got), (into, i_own, i_got)):
        for ref, at in ((own, odd), (got, 1 - odd)):
            rows = pl.ds(pl.multiple_of(at * part, part), part)
            out[rows, :] = ref[...].astype(F32)


def join_kernel(flags, kept, got, own, away):
    high = flags[4]
    feats = own.shape[0]
    half = own.shape[1] // 2
    for out, at in ((own, high), (away, 1 - high)):
        rows = pl.ds(pl.multiple_of(at * feats, feats), feats)
        near = kept[rows, :half] + got[rows, half:].astype(F32)
        far = kept[rows, half:] + got[rows, :half].astype(F32)
        out[:, :half] = near.astype(out.dtype)
        out[:, half:] = far.astype(out.dtype)


def finish_kernel(flags, own, got, out):
    low = flags[0]
    half = own.shape[1] // 2
    total = (own[...] + got[...].astype(F32)).astype(BF16)

    @pl.when(low == 0)
    def _():
        out[...] = total

    @pl.when(low == 1)
    def _():
        out[:, :half] = total[:, half:]
        out[:, half:] = total[:, :half]


def shards(
    layer_in,
    seq_lengths,
    w_qkv,
    q_bias,
    v_bias,
    w_out,
    b_out,
    ln1_gain,
    ln1_bias,
    w_in,
    b_in,
    w_back,
    b_back,
    ln2_gain,
    ln2_bias,
    out_grad,
):
    n_rows = lax.axis_size("row")
    row, col = lax.axis_index("row"), lax.axis_index("col")
    low_bit = (col % 2) == 1
    odd_bit = lax.axis_index("dp") % 2
    odd = odd_bit == 1
    feats, slot = layer_in.shape
    half = slot // 2
    width = w_out.shape[0]
    model = n_rows * feats
    units = w_in.shape[1]
    heads = width // HEAD_DIM
    length = lax.dynamic_index_in_dim(seq_lengths, plane_of(row), 0, False)
    flags = jnp.stack((col % 2, odd_bit, col, length, col // 2, row)).astype(jnp.int32)
    halves = shape((model, half), BF16)
    wide_halves = shape((model, half), F32)

    def sum_cores(mine, other):
        return (mine + swap_bit(other, "col", 1).astype(F32)).astype(BF16)

    def add_rows(blocks):
        parts = [from_row(blocks[k], n_rows - k) for k in range(1, n_rows)]
        terms = [term.astype(F32) for term in (blocks[0], *parts)]
        while len(terms) > 1:
            pairs = len(terms) // 2
            terms = [terms[i] + terms[i + pairs] for i in range(pairs)]
        return terms[0].astype(BF16)

    def add_replicas(total, first):
        bit = first
        while bit < lax.axis_size("dp"):
            total = total.astype(F32) + swap_bit(total, "dp", bit).astype(F32)
            total = total.astype(BF16)
            bit *= 2
        return total

    x0 = to_slot(layer_in)
    qkv_part = w_qkv.transpose(1, 0, 2).reshape(3 * feats, width)
    pack_half, wide, vectors = call(
        send_kernel,
        "send",
        [
            shape((feats, 2 * width), BF16),
            shape((feats + 16, units), BF16),
            shape((16, units), BF16),
        ],
        [odd_bit.reshape(1), qkv_part, w_out, w_in, w_back, b_in]
        + [b_out, ln1_gain, ln1_bias, b_back, ln2_gain, ln2_bias, q_bias, v_bias],
        specs={k: pl.BlockSpec(memory_space=pl.ANY) for k in range(1, 14)},
        out_specs=[
            pl.BlockSpec(memory_space=pltpu.VMEM)
        ]
        * 3,
        scratch=[
            pltpu.VMEM((2, feats, width), BF16),
            pltpu.VMEM((units,), BF16),
            pltpu.SemaphoreType.DMA((12,)),
        ]
        + [pltpu.VMEM((feats,), BF16)] * 8,
        vmem_mib=56,
    )
    fetched = lax.all_gather(after(pack_half, wide), "row")
    swapped = swap_bit(fetched, "dp", 1)
    wide = after(wide, fetched)
    wide_fetched = [from_row(wide, k) for k in range(1, n_rows)]
    x0 = after(x0, flags, fetched)
    x2 = swap_bit(x0, "col", 2)
    x1 = swap_bit(x0, "col", 1)
    wide_swapped = [swap_bit(after(part, x2), "dp", 1) for part in wide_fetched]
    g_own = to_slot(after(out_grad.astype(BF16), fetched))
    ready = (wide_swapped[0], wide_fetched[1], wide_swapped[2])
    x3 = swap_bit(after(x2, swapped, g_own, *ready), "col", 1)

    in_all, back_all, vecs, in_bias = call(
        assemble_kernel,
        "assemble",
        [shape((model, units), BF16)] * 2 + [shape((model, 16), F32), shape((units, 16), F32)],
        [flags, w_in, w_back, vectors] + wide_fetched + wide_swapped,
        specs={k: pl.BlockSpec(memory_space=pl.ANY) for k in (1, 2, 4, 5, 6, 7, 8, 9)},
        scratch=[pltpu.VMEM((3, 16, units), BF16), pltpu.SemaphoreType.DMA((11,))],
    )

    xs, packs, qkv, prob, context, mine, other = call(
        attend_kernel,
        "attend",
        [
            shape((model, slot), BF16),
            shape((n_rows, 2, feats, 2 * width), BF16),
            shape((3 * width, slot), BF16),
            shape((heads, slot, slot), BF16),
            shape((width, slot), BF16),
            wide_halves,
            halves,
        ],
        [flags, x0, x1, x2, x3, fetched, swapped, vectors],
        specs={k: pl.BlockSpec(memory_space=pl.ANY) for k in range(1, 7)},
        scratch=[pltpu.VMEM((model, slot), BF16), pltpu.SemaphoreType.DMA((12,))],
        vmem_mib=56,
        weight=0,
    )

    own = sum_cores(mine, other)
    away = swap_bit(own, "col", 2)
    scaled_one, inverse_one, n_own = call(
        norm_kernel,
        "norm",
        [wide_halves, shape((8, half), F32), halves],
        [xs, own, away, vecs],
        specs={0: pl.BlockSpec((model, half), lambda _: (0, 0))},
        windowed=True,
        weight=0,
    )
    g_high = swap_bit(after(g_own, scaled_one), "col", 2)

    n_away = swap_bit(n_own, "col", 1)
    hidden, slope, mine, other = call(
        forward_kernel,
        "feed_forward",
        [shape((units, slot), BF16), shape((units, slot), BF16), wide_halves, halves],
        [n_own, n_away, in_all, back_all, in_bias],
        weight=0,
    )
    g_both = jnp.concatenate((after(g_own, hidden), g_high))
    g_low = swap_bit(jnp.where(low_bit, g_both[:, :half], g_both[:, half:]), "col", 1)
    own = sum_cores(after(mine, g_low), other)
    away = swap_bit(own, "col", 2)
    out_own, out_give, grad_second, r_own, sums = call(
        turn_kernel,
        "turn",
        [
            shape((feats, half), BF16),
            shape((feats, half), BF16),
            wide_halves,
            halves,
            shape((8, model), F32),
        ],
        [flags, scaled_one, own, away, vecs, g_own, g_high, g_low],
        scratch=[pltpu.VMEM((model, half), BF16), pltpu.VMEM((model, half), BF16)],
        weight=0,
    )
    r_away = swap_bit(r_own, "col", 1)
    mine, other, grad_pre, b_in_sums = call(
        backward_kernel,
        "feed_backward",
        [wide_halves, halves, shape((units, slot), BF16), shape((8, feats), F32)],
        [r_own, r_away, slope, in_all, back_all],
        weight=0,
    )
    own = sum_cores(mine, other)
    b_keep, b_give, i_keep, i_give = call(
        wide_grad_kernel,
        "wide_grads",
        [shape((n_rows, feats // 2, units), BF16)] * 4,
        [flags, after(r_own, own), r_away, hidden, n_own, n_away, grad_pre],
        weight=0,
    )
    b_got = swap_bit(b_give, "dp", 1)
    i_got = swap_bit(i_give, "dp", 1)
    away = swap_bit(own, "col", 2)
    grad_first, a_own, sums = call(
        norm_back_kernel,
        "norm_back",
        [wide_halves, halves, shape((8, model), F32)],
        [own, after(away, b_give), grad_second, scaled_one, inverse_one, vecs, sums],
        weight=0,
    )
    a_away = swap_bit(a_own, "col", 1)
    sums_away = swap_bit(sums, "col", 1)
    grad_qkv, kept, give = call(
        attend_back_kernel,
        "attend_back",
        [
            shape((3 * width, slot), BF16),
            shape((2 * feats, slot), F32),
            shape((2 * feats, slot), BF16),
        ],
        [flags, a_own, a_away, packs, qkv, prob, grad_first],
        scratch=[pltpu.VMEM((width, slot), BF16)],
        weight=0,
    )

    pack_keep, pack_give = call(
        pack_grad_kernel,
        "pack_grads",
        [shape((n_rows, feats + 16, 2 * width), BF16)] * 2,
        [flags, xs, grad_qkv, a_own, a_away, context, sums, sums_away, b_in_sums],
        weight=0,
    )

    in_own, in_away = call(
        join_kernel,
        "join",
        [shape((feats, slot), F32), shape((feats, slot), BF16)],
        [flags, after(kept, pack_give), swap_bit(give, "col", 1)],
    )
    (in_done,) = call(
        finish_kernel,
        "finish",
        [shape((feats, slot), BF16)],
        [flags, in_own, swap_bit(in_away, "col", 2)],
    )
    in_grad = from_slot(in_done).astype(F32)

    out_give = after(out_give, in_away)
    layer_out = from_slot(ordered(low_bit, out_own, swap_bit(out_give, "col", 1), 1))

    totals = []
    for name, keep, got in (
        ("back_add", b_keep, after(b_got, grad_qkv)),
        ("into_add", i_keep, after(i_got, pack_give)),
    ):
        parts = call(
            pack_add_kernel, name, [shape((feats // 2, units), BF16)] * n_rows, [keep, got]
        )
        totals += [add_replicas(add_rows(parts), 2)]
    b_back, i_back = (swap_bit(total, "dp", 1) for total in totals)
    pack_got = after(swap_bit(pack_give, "dp", 1), totals[1], b_back)
    w_back_grad, w_in_grad = call(
        wide_unpack_kernel,
        "wide_unpack",
        [shape((feats, units), F32)] * 2,
        [flags, totals[0], b_back, totals[1], i_back],
    )
    packs = call(
        pack_add_kernel,
        "pack_add",
        [shape(pack_keep.shape[1:], BF16)] * n_rows,
        [pack_keep, pack_got],
    )
    total = add_replicas(add_rows(packs), 2)
    w_qkv_grad, w_out_grad, tail = call(
        unpack_kernel,
        "unpack",
        [
            shape((3 * feats, width), F32),
            shape((width, feats), F32),
            shape((EXTRA, feats), F32),
        ],
        [flags, total, swap_bit(after(total, i_back), "dp", 1)],
    )
    w_qkv_grad = w_qkv_grad.reshape(3, feats, width).transpose(1, 0, 2)
    return (
        layer_out,
        in_grad,
        w_qkv_grad,
        tail[20],
        tail[21],
        w_out_grad,
        tail[4],
        tail[0],
        tail[1],
        w_in_grad,
        tail[16:20].reshape(-1),
        w_back_grad,
        tail[5],
        tail[2],
        tail[3],
    )


def solution(mesh):
    tokens = P("row", ("dp", "col"))
    block = P("row", "col")
    in_specs = (
        tokens,
        P("dp"),
        P("row", None, "col"),
        P("col"),
        P("col"),
        P("col", "row"),
        P("row"),
        P("row"),
        P("row"),
        block,
        P("col"),
        block,
        P("row"),
        P("row"),
        P("row"),
        tokens,
    )
    out_specs = (
        tokens,
        tokens,
        P("row", None, "col"),
        P("col"),
        P("col"),
        P("col", "row"),
        P("row"),
        P("row"),
        P("row"),
        block,
        P("col"),
        block,
        P("row"),
        P("row"),
        P("row"),
    )
    return jax.shard_map(shards, mesh=mesh, in_specs=in_specs, out_specs=out_specs, check_vma=False)
```

```python
import jax
import jax.numpy as jnp
from jax import lax
from jax.experimental import pallas as pl
from jax.experimental.pallas import tpu as pltpu
from jax.sharding import PartitionSpec as P

HEAD_DIM = 64
EPSILON = 1e-12
F32 = jnp.float32
BF16 = jnp.bfloat16


def dot(left, right, left_dim, right_dim):
    return lax.dot_general(
        left, right, (((left_dim,), (right_dim,)), ((), ())), preferred_element_type=F32
    )


def call(kernel, name, outs, args, weight=0, scratch=(), specs=None, windowed=False, vmem_mib=16, out_specs=None):
    vmem = pl.BlockSpec(memory_space=pltpu.VMEM)
    in_specs = [
        pl.BlockSpec(memory_space=pltpu.SMEM) if arg.dtype == jnp.int32 else vmem for arg in args
    ]
    for at, spec in (specs or {}).items():
        in_specs[at] = spec
    return pl.pallas_call(
        kernel,
        name=name,
        out_shape=outs,
        grid=(1,) if windowed else (),
        in_specs=in_specs,
        out_specs=out_specs or [vmem] * len(outs),
        scratch_shapes=list(scratch),
        compiler_params=pltpu.CompilerParams(vmem_limit_bytes=vmem_mib * 1024 * 1024),
        cost_estimate=pl.CostEstimate(
            flops=weight * 2**30, bytes_accessed=weight * 2**22, transcendentals=0
        ),
    )(*args)


def shape(dims, dtype):
    return jax.ShapeDtypeStruct(dims, dtype)


def swap_bit(value, axis, bit):
    size = lax.axis_size(axis)
    return lax.ppermute(value, axis, [(at, at ^ bit) for at in range(size)])


def plane_of(slot):
    return (slot % 2) * 2 + slot // 2


def grid_pairs():
    size = lax.axis_size("row")
    return [
        (a * size + b, plane_of(b) * size + (a - plane_of(b)) % size)
        for a in range(size)
        for b in range(size)
    ]


def to_slot(value):
    return lax.ppermute(value, ("row", "col"), grid_pairs())


def from_slot(value):
    return lax.ppermute(value, ("row", "col"), [(b, a) for a, b in grid_pairs()])


def from_row(value, away):
    size = lax.axis_size("row")
    return lax.ppermute(value, "row", [((a + away) % size, a) for a in range(size)])


def after(value, *others):
    return lax.optimization_barrier((value,) + others)[0]


def ordered(flag, own, other, axis):
    return jnp.concatenate(
        (jnp.where(flag, other, own), jnp.where(flag, own, other)), axis=axis
    )


def identity(size):
    at = lax.broadcasted_iota(jnp.int32, (size, size), 0)
    return (at == lax.broadcasted_iota(jnp.int32, (size, size), 1)).astype(BF16)


def row_sums(products):
    total = 0.0
    for at, product in products.items():
        pick = lax.broadcasted_iota(jnp.int32, (8, product.shape[1]), 0) == at
        pick = pick.astype(BF16)
        high = product.astype(BF16)
        rest = (product - high.astype(F32)).astype(BF16)
        total = total + dot(pick, high, 1, 1) + dot(pick, rest, 1, 1)
    return total


def send_kernel(
    odd, w_qkv, w_out, w_in, w_back, b_in, v0, v1, v2, v3, v4, v5, v6, v7,
    half, wide, vectors, blocks, long_line, sems, *lines,
):
    size = w_out.shape[0]
    feats = w_in.shape[0]
    copies = [pltpu.make_async_copy(b_in, long_line, sems.at[0])]
    for at, ref in enumerate((v0, v1, v2, v3, v4, v5, v6, v7)):
        copies += [pltpu.make_async_copy(ref, lines[at], sems.at[at + 1])]
    into = wide.at[pl.ds(0, feats)]
    for part in range(2):

        @pl.when(odd[0] == part)
        def _():
            pltpu.make_async_copy((w_in, w_back)[part], into, sems.at[9]).start()
            first = w_qkv.at[pl.ds(2 * part * size, size)]
            pltpu.make_async_copy(first, blocks.at[0], sems.at[10]).start()
            second = (w_qkv.at[pl.ds(size, size)], w_out)[part]
            pltpu.make_async_copy(second, blocks.at[1], sems.at[11]).start()

    for copy in copies:
        copy.start()
    vectors[...] = jnp.zeros_like(vectors)
    for copy in copies:
        copy.wait()
    for at in range(8):
        vectors[at : at + 1, :feats] = lines[at][...].reshape(1, feats)
    vectors[8:9, :] = long_line[...].reshape(1, long_line.shape[0])
    wide[feats:] = vectors[...]
    pltpu.make_async_copy(w_in, into, sems.at[9]).wait()
    for at in range(2):
        pltpu.make_async_copy(w_out, blocks.at[at], sems.at[10 + at]).wait()
        half[:, at * size : (at + 1) * size] = blocks[at]


def attend_kernel(
    flags, x0, x1, x2, x3, fetched, swapped, vectors,
    xs, packs, qkv, prob, context, mine, other, raw, sems,
):
    low, odd, col, length = flags[0], flags[1], flags[2], flags[3]
    feats, slot = x0.shape
    half = slot // 2
    width = context.shape[0]
    row = flags[5]
    copies = []
    for k in range(4):
        for ref, part in ((fetched, odd), (swapped, 1 - odd)):
            ref = ref.at[lax.rem(row + k, 4)]
            copies += [pltpu.make_async_copy(ref, packs.at[k, part], sems.at[len(copies)])]
    for bit, ref in enumerate((x0, x1, x2, x3)):
        rows = pl.ds(pl.multiple_of((col ^ bit) * feats, feats), feats)
        copies += [pltpu.make_async_copy(ref, raw.at[rows], sems.at[len(copies)])]
    for copy in copies:
        copy.start()
    for copy in copies:
        copy.wait()

    @pl.when(low == 0)
    def _():
        xs[...] = raw[...]

    @pl.when(low == 1)
    def _():
        xs[:, :half] = raw[:, half:]
        xs[:, half:] = raw[:, :half]

    columns = dot(identity(width), vectors[:, :width], 1, 1)
    for part, bias in enumerate((columns[:, 6:7], 0.0, columns[:, 7:8])):
        total = bias
        for k in range(4):
            block = packs[k, part // 2, :, part % 2 * width : (part % 2 + 1) * width]
            total = total + dot(block, xs[k * feats : (k + 1) * feats], 0, 0)
        qkv[part * width : (part + 1) * width] = total.astype(BF16)

    place = lax.broadcasted_iota(jnp.int32, (slot, half), 0)
    place = jnp.where(low == 1, (place + half) % slot, place)
    live = place < length
    scale = HEAD_DIM ** (-0.5)
    for h in range(width // HEAD_DIM):
        q_rows = pl.ds(h * HEAD_DIM, HEAD_DIM)
        k_rows = pl.ds(width + h * HEAD_DIM, HEAD_DIM)
        v_rows = pl.ds(2 * width + h * HEAD_DIM, HEAD_DIM)
        for part in range(2):
            cols = slice(part * half, (part + 1) * half)
            scores = dot(qkv[k_rows, :], qkv[q_rows, cols], 0, 0) * scale
            scores = jnp.where(live, scores, -1000000000.0)
            exponent = jnp.exp(scores - jnp.max(scores, axis=0, keepdims=True))
            inverse = 1.0 / jnp.sum(exponent, axis=0, keepdims=True)
            weights = (exponent * inverse).astype(BF16)
            prob[h, :, cols] = weights
            context[q_rows, cols] = dot(qkv[v_rows, :], weights, 1, 0).astype(BF16)

    for k in range(4):
        rows = slice(k * feats, (k + 1) * feats)
        part = dot(packs[k, 1, :, width:], context[...], 0, 0)
        mine[rows] = part[:, :half]
        other[rows] = part[:, half:].astype(BF16)


def assemble_kernel(
    flags, own_in, own_back, v0, f1, f2, f3, s1, s2, s3, w_in, w_back, vecs, bias, rows, sems
):
    odd = flags[1]
    feats = own_in.shape[0]
    first = pl.ds(0, feats)
    copies = [
        pltpu.make_async_copy(own_in, w_in.at[first], sems.at[0]),
        pltpu.make_async_copy(own_back, w_back.at[first], sems.at[1]),
    ]
    for k, (f, s) in enumerate(((f1, s1), (f2, s2), (f3, s3))):
        span = pl.ds((k + 1) * feats, feats)
        for ref, into in ((f, (w_in, w_back)), (s, (w_back, w_in))):
            at = len(copies)
            ref = ref.at[first]
            even = pltpu.make_async_copy(ref, into[0].at[span], sems.at[at])
            other = pltpu.make_async_copy(ref, into[1].at[span], sems.at[at])
            copies += [(even, other)]
    for k, ref in enumerate((f1, f2, f3)):
        tail = ref.at[pl.ds(feats, 16)]
        copies += [pltpu.make_async_copy(tail, rows.at[k], sems.at[len(copies)])]
    for begin in (True, False):
        for copy in copies:
            if isinstance(copy, tuple):

                @pl.when(odd == 0)
                def _():
                    copy[0].start() if begin else copy[0].wait()

                @pl.when(odd == 1)
                def _():
                    copy[1].start() if begin else copy[1].wait()

            elif begin:
                copy.start()
            else:
                copy.wait()
    eye = identity(feats)
    vecs[:feats] = dot(eye, v0[:, :feats], 1, 1)
    for k in range(4):
        span = slice(k * feats, (k + 1) * feats)
        bias[span] = dot(eye, v0[:, span], 1, 1)
    for k in range(3):
        span = slice((k + 1) * feats, (k + 2) * feats)
        vecs[span] = dot(eye, rows[k, :, :feats], 1, 1)


def norm_kernel(x, own, away, vecs, scaled, inverse, low_normed):
    first = x[...].astype(F32) + own[...].astype(F32) + away[...].astype(F32) + vecs[:, 0:1]
    center = jnp.mean(first, axis=0, keepdims=True)
    first = first - center
    inv = lax.rsqrt(jnp.mean(first * first, axis=0, keepdims=True) + EPSILON)
    first = first * inv
    scaled[...] = first
    inverse[...] = jnp.broadcast_to(inv, inverse.shape)
    low_normed[...] = (first * vecs[:, 1:2] + vecs[:, 2:3]).astype(BF16)


def forward_kernel(n_own, n_away, w_in, w_back, bias, hidden, slope, mine, other):
    half = n_own.shape[1]
    step = 256
    for part, ref in enumerate((n_own, n_away)):
        cols = slice(part * half, (part + 1) * half)
        for at in range(0, w_in.shape[1], step):
            rows = slice(at, at + step)
            pre = dot(w_in[:, rows], ref[...], 0, 0) + bias[rows, 8:9]
            share = 0.5 * (1.0 + lax.erf(pre * (0.5**0.5)))
            hidden[rows, cols] = (pre * share).astype(BF16)
            bell = jnp.exp(-0.5 * pre * pre) * ((0.5 / jnp.pi) ** 0.5)
            slope[rows, cols] = (share + pre * bell).astype(BF16)
    mine[...] = dot(w_back[...], hidden[:, :half], 1, 0)
    other[...] = dot(w_back[...], hidden[:, half:], 1, 0).astype(BF16)


def turn_kernel(
    flags, scaled_one, own, away, vecs, g_own, g_pair, g_high, g_last,
    keep, give, grad_second, grad_returned, sums, final, grad,
):
    low, col, length = flags[0], flags[2], flags[3]
    feats = g_own.shape[0]
    half = own.shape[1]

    def rows(bit):
        return pl.ds(pl.multiple_of((col ^ bit) * feats, feats), feats)

    for bit, ref in enumerate((g_own, g_pair, g_high, g_last)):

        @pl.when(low == 0)
        def _():
            grad[rows(bit), :] = ref[:, :half]

        @pl.when(low == 1)
        def _():
            grad[rows(bit), :] = ref[:, half:]

    normed = scaled_one[...] * vecs[:, 1:2] + vecs[:, 2:3]
    second = normed + own[...].astype(F32) + away[...].astype(F32) + vecs[:, 3:4]
    second = second - jnp.mean(second, axis=0, keepdims=True)
    inv = lax.rsqrt(jnp.mean(second * second, axis=0, keepdims=True) + EPSILON)
    scaled = second * inv
    place = low * half + lax.broadcasted_iota(jnp.int32, (1, half), 1)
    live = (place < length).astype(F32)
    final[...] = ((scaled * vecs[:, 4:5] + vecs[:, 5:6]) * live).astype(BF16)
    keep[...] = final[rows(0), :]
    give[...] = final[rows(1), :]
    upstream = grad[...].astype(F32) * live
    weighted = upstream * vecs[:, 4:5]
    mean = jnp.mean(weighted, axis=0, keepdims=True)
    tilt = jnp.mean(weighted * scaled, axis=0, keepdims=True)
    back = inv * (weighted - mean - scaled * tilt)
    grad_second[...] = back
    grad_returned[...] = back.astype(BF16)
    sums[...] = row_sums({2: upstream * scaled, 3: upstream, 5: back})


def backward_kernel(r_own, r_away, slope, w_in, w_back, mine, other, grad_pre, b_in_sums):
    half = r_own.shape[1]
    step = 256
    for part, ref in enumerate((r_own, r_away)):
        cols = slice(part * half, (part + 1) * half)
        for at in range(0, w_in.shape[1], step):
            rows = slice(at, at + step)
            grad_hidden = dot(w_back[:, rows], ref[...], 0, 0)
            grad_pre[rows, cols] = (grad_hidden * slope[rows, cols].astype(F32)).astype(BF16)
    mine[...] = dot(w_in[...], grad_pre[:, :half], 1, 0)
    other[...] = dot(w_in[...], grad_pre[:, half:], 1, 0).astype(BF16)
    size = b_in_sums.shape[1]
    total = 0.0
    for k in range(w_in.shape[1] // size):
        pick = lax.broadcasted_iota(jnp.int32, (8, 2 * half), 0) == k
        total = total + dot(pick.astype(BF16), grad_pre[k * size : (k + 1) * size], 1, 1)
    b_in_sums[...] = total


def wide_grad_kernel(flags, own, away, right, keep, give):
    odd = flags[1]
    half = own.shape[1]
    part = keep.shape[1]
    for k in range(4):
        for pick, out in ((1 - odd, give), (odd, keep)):
            rows = pl.ds(pl.multiple_of((2 * k + pick) * part, part), part)
            total = dot(own[rows, :], right[:, :half], 1, 1)
            total = total + dot(away[rows, :], right[:, half:], 1, 1)
            out[k] = total.astype(BF16)


def norm_back_kernel(
    own, away, grad_second, scaled, inverse, vecs, sums, grad_first, low_first, sums_out
):
    upstream = grad_second[...] + own[...].astype(F32) + away[...].astype(F32)
    weighted = upstream * vecs[:, 1:2]
    mean = jnp.mean(weighted, axis=0, keepdims=True)
    tilt = jnp.mean(weighted * scaled[...], axis=0, keepdims=True)
    back = inverse[0:1] * (weighted - mean - scaled[...] * tilt)
    grad_first[...] = back
    low_first[...] = back.astype(BF16)
    sums_out[...] = sums[...] + row_sums({0: upstream * scaled[...], 1: upstream, 4: back})


def attend_back_kernel(
    flags, a_own, a_away, packs, qkv, prob, grad_first, grad_qkv, keep, give, grad_context
):
    low = flags[0]
    half = a_own.shape[1]
    feats = packs.shape[2]
    width = grad_context.shape[0]
    for part, ref in enumerate((a_own, a_away)):
        cols = slice(part * half, (part + 1) * half)
        total = 0.0
        for k in range(4):
            total = total + dot(packs[k, 1, :, width:], ref[k * feats : (k + 1) * feats], 1, 0)
        grad_context[:, cols] = total.astype(BF16)
    scale = HEAD_DIM ** (-0.5)
    for h in range(width // HEAD_DIM):
        q_rows = pl.ds(h * HEAD_DIM, HEAD_DIM)
        k_rows = pl.ds(width + h * HEAD_DIM, HEAD_DIM)
        v_rows = pl.ds(2 * width + h * HEAD_DIM, HEAD_DIM)
        grad_keys, grad_values = 0.0, 0.0
        for part in range(2):
            cols = slice(part * half, (part + 1) * half)
            weights = prob[h, :, cols]
            wide = weights.astype(F32)
            grad_weights = dot(qkv[v_rows, :], grad_context[q_rows, cols], 0, 0)
            inner = jnp.sum(wide * grad_weights, axis=0, keepdims=True)
            grad_scores = (wide * (grad_weights - inner)).astype(BF16)
            grad_qkv[q_rows, cols] = (dot(qkv[k_rows, :], grad_scores, 1, 0) * scale).astype(BF16)
            grad_keys = grad_keys + dot(qkv[q_rows, cols], grad_scores, 1, 1)
            grad_values = grad_values + dot(grad_context[q_rows, cols], weights, 1, 1)
        grad_qkv[k_rows, :] = (grad_keys * scale).astype(BF16)
        grad_qkv[v_rows, :] = grad_values.astype(BF16)

    def block(k):
        part = 0.0
        for at in range(3):
            left = packs[k, at // 2, :, at % 2 * width : (at % 2 + 1) * width]
            part = part + dot(left, grad_qkv[at * width : (at + 1) * width], 1, 0)
        rows = pl.ds(pl.multiple_of(k * feats, feats), feats)
        return part[:, :half] + 0.5 * grad_first[rows, :], part[:, half:]

    for j in range(2):
        rows = slice(j * feats, (j + 1) * feats)
        near, far = block(2 * j + 1 - low)
        give[rows, :half] = near.astype(BF16)
        give[rows, half:] = far.astype(BF16)
        near, far = block(2 * j + low)
        keep[rows, :half] = near
        keep[rows, half:] = far


def pack_grad_kernel(
    flags, xs, grad_qkv, a_own, a_away, context, sums, sums_away, b_in_sums, keep, give
):
    odd = flags[1]
    width = context.shape[0]
    feats = keep.shape[1] - 16
    half = a_own.shape[1]
    ones = (lax.broadcasted_iota(jnp.int32, (8, 2 * half), 0) == 4).astype(BF16)
    more = (lax.broadcasted_iota(jnp.int32, (8, 2 * half), 0) == 5).astype(BF16)
    shared = b_in_sums[...] + dot(ones, grad_qkv[:width], 1, 1)
    shared = shared + dot(more, grad_qkv[2 * width :], 1, 1)
    vector_sums = sums[...] + sums_away[...]
    none = jnp.zeros((16, 2 * feats), BF16)
    for k in range(4):
        span = slice(k * feats, (k + 1) * feats)
        blocks = [
            dot(xs[span], grad_qkv[at * width : (at + 1) * width], 1, 1) for at in range(3)
        ]
        last = dot(context[:, :half], a_own[span], 1, 1)
        blocks += [last + dot(context[:, half:], a_away[span], 1, 1)]
        tail = jnp.concatenate((vector_sums[:, span], shared), axis=1)
        tail = jnp.concatenate((tail, jnp.zeros_like(tail)), axis=0).astype(BF16)
        for part in range(2):
            pair = jnp.concatenate(blocks[2 * part : 2 * part + 2], axis=1).astype(BF16)
            rest = none if part else tail
            for out, at in ((keep, odd), (give, 1 - odd)):

                @pl.when(at == part)
                def _():
                    out[k, :feats] = pair
                    out[k, feats:] = rest


def pack_add_kernel(keep, got, *outs):
    for k, out in enumerate(outs):
        out[...] = (keep[k].astype(F32) + got[k].astype(F32)).astype(BF16)


def unpack_kernel(flags, own, got, qkv, w_out, b_in, *lines):
    odd = flags[1]
    feats, width = w_out.shape[1], w_out.shape[0]

    def write(first, second):
        qkv[:feats] = first[:feats, :width].astype(F32)
        qkv[feats : 2 * feats] = first[:feats, width:].astype(F32)
        qkv[2 * feats :] = second[:feats, :width].astype(F32)
        w_out[...] = second[:feats, width:].astype(F32)
        tail = first[feats:].astype(F32)
        for at in range(6):
            lines[at][...] = tail[at, :feats]
        for at in range(4):
            b_in[at * feats : (at + 1) * feats] = tail[at, feats:]
        for at in range(2):
            lines[6 + at][...] = tail[4 + at, feats:]

    @pl.when(odd == 0)
    def _():
        write(own, got)

    @pl.when(odd == 1)
    def _():
        write(got, own)


def wide_unpack_kernel(flags, b_own, b_got, i_own, i_got, back, into):
    odd = flags[1]
    part = b_own.shape[0]
    for out, own, got in ((back, b_own, b_got), (into, i_own, i_got)):
        for ref, at in ((own, odd), (got, 1 - odd)):
            rows = pl.ds(pl.multiple_of(at * part, part), part)
            out[rows, :] = ref[...].astype(F32)


def join_kernel(flags, kept, got, own, away):
    high = flags[4]
    feats = own.shape[0]
    half = own.shape[1] // 2
    for out, at in ((own, high), (away, 1 - high)):
        rows = pl.ds(pl.multiple_of(at * feats, feats), feats)
        near = kept[rows, :half] + got[rows, half:].astype(F32)
        far = kept[rows, half:] + got[rows, :half].astype(F32)
        out[:, :half] = near.astype(out.dtype)
        out[:, half:] = far.astype(out.dtype)


def finish_kernel(flags, own, got, out):
    low = flags[0]
    half = own.shape[1] // 2
    total = (own[...] + got[...].astype(F32)).astype(BF16)

    @pl.when(low == 0)
    def _():
        out[...] = total

    @pl.when(low == 1)
    def _():
        out[:, :half] = total[:, half:]
        out[:, half:] = total[:, :half]


def shards(
    layer_in,
    seq_lengths,
    w_qkv,
    q_bias,
    v_bias,
    w_out,
    b_out,
    ln1_gain,
    ln1_bias,
    w_in,
    b_in,
    w_back,
    b_back,
    ln2_gain,
    ln2_bias,
    out_grad,
):
    n_rows = lax.axis_size("row")
    row, col = lax.axis_index("row"), lax.axis_index("col")
    low_bit = (col % 2) == 1
    odd_bit = lax.axis_index("dp") % 2
    odd = odd_bit == 1
    feats, slot = layer_in.shape
    half = slot // 2
    width = w_out.shape[0]
    model = n_rows * feats
    units = w_in.shape[1]
    heads = width // HEAD_DIM
    length = lax.dynamic_index_in_dim(seq_lengths, plane_of(row), 0, False)
    flags = jnp.stack((col % 2, odd_bit, col, length, col // 2, row)).astype(jnp.int32)
    halves = shape((model, half), BF16)
    wide_halves = shape((model, half), F32)

    def sum_cores(mine, other):
        return (mine + swap_bit(other, "col", 1).astype(F32)).astype(BF16)

    def add_rows(blocks):
        parts = [from_row(blocks[k], n_rows - k) for k in range(1, n_rows)]
        terms = [term.astype(F32) for term in (blocks[0], *parts)]
        while len(terms) > 1:
            pairs = len(terms) // 2
            terms = [terms[i] + terms[i + pairs] for i in range(pairs)]
        return terms[0].astype(BF16)

    def add_replicas(total, first):
        bit = first
        while bit < lax.axis_size("dp"):
            total = total.astype(F32) + swap_bit(total, "dp", bit).astype(F32)
            total = total.astype(BF16)
            bit *= 2
        return total

    x0 = to_slot(layer_in)
    qkv_part = w_qkv.transpose(1, 0, 2).reshape(3 * feats, width)
    pack_half, wide, vectors = call(
        send_kernel,
        "send",
        [
            shape((feats, 2 * width), BF16),
            shape((feats + 16, units), BF16),
            shape((16, units), BF16),
        ],
        [odd_bit.reshape(1), qkv_part, w_out, w_in, w_back, b_in]
        + [b_out, ln1_gain, ln1_bias, b_back, ln2_gain, ln2_bias, q_bias, v_bias],
        specs={k: pl.BlockSpec(memory_space=pl.ANY) for k in range(1, 14)},
        out_specs=[
            pl.BlockSpec(memory_space=pltpu.VMEM)
        ]
        * 3,
        scratch=[
            pltpu.VMEM((2, feats, width), BF16),
            pltpu.VMEM((units,), BF16),
            pltpu.SemaphoreType.DMA((12,)),
        ]
        + [pltpu.VMEM((feats,), BF16)] * 8,
        vmem_mib=56,
    )
    fetched = lax.all_gather(after(pack_half, wide), "row")
    swapped = swap_bit(fetched, "dp", 1)
    wide = after(wide, fetched)
    wide_fetched = [from_row(wide, 1), None, from_row(wide, 3)]
    wide_fetched[1] = from_row(wide_fetched[0], 1)
    x0 = after(x0, flags, fetched)
    x2 = swap_bit(x0, "col", 2)
    x1 = swap_bit(x0, "col", 1)
    wide_swapped = [swap_bit(after(part, x2), "dp", 1) for part in wide_fetched]
    g_own = to_slot(after(out_grad.astype(BF16), fetched))
    ready = (wide_swapped[0], wide_fetched[1], wide_swapped[2], g_own)
    x3 = swap_bit(after(x2, swapped, *ready), "col", 1)

    in_all, back_all, vecs, in_bias = call(
        assemble_kernel,
        "assemble",
        [shape((model, units), BF16)] * 2 + [shape((model, 16), F32), shape((units, 16), F32)],
        [flags, w_in, w_back, vectors] + wide_fetched + wide_swapped,
        specs={k: pl.BlockSpec(memory_space=pl.ANY) for k in (1, 2, 4, 5, 6, 7, 8, 9)},
        scratch=[pltpu.VMEM((3, 16, units), BF16), pltpu.SemaphoreType.DMA((11,))],
    )

    xs, packs, qkv, prob, context, mine, other = call(
        attend_kernel,
        "attend",
        [
            shape((model, slot), BF16),
            shape((n_rows, 2, feats, 2 * width), BF16),
            shape((3 * width, slot), BF16),
            shape((heads, slot, slot), BF16),
            shape((width, slot), BF16),
            wide_halves,
            halves,
        ],
        [flags, x0, x1, x2, x3, fetched, swapped, vectors],
        specs={k: pl.BlockSpec(memory_space=pl.ANY) for k in range(1, 7)},
        scratch=[pltpu.VMEM((model, slot), BF16), pltpu.SemaphoreType.DMA((12,))],
        vmem_mib=56,
        weight=0,
    )

    own = sum_cores(mine, other)
    away = swap_bit(own, "col", 2)
    scaled_one, inverse_one, n_own = call(
        norm_kernel,
        "norm",
        [wide_halves, shape((8, half), F32), halves],
        [xs, own, away, vecs],
        specs={0: pl.BlockSpec((model, half), lambda _: (0, 0))},
        windowed=True,
        weight=0,
    )
    g_high = swap_bit(after(g_own, scaled_one), "col", 2)

    n_away = swap_bit(n_own, "col", 1)
    hidden, slope, mine, other = call(
        forward_kernel,
        "feed_forward",
        [shape((units, slot), BF16), shape((units, slot), BF16), wide_halves, halves],
        [n_own, n_away, in_all, back_all, in_bias],
        weight=0,
    )
    g_pair = swap_bit(g_own, "col", 1)
    g_last = swap_bit(g_high, "col", 1)
    own = sum_cores(after(mine, g_last), other)
    away = swap_bit(own, "col", 2)
    out_own, out_give, grad_second, r_own, sums = call(
        turn_kernel,
        "turn",
        [
            shape((feats, half), BF16),
            shape((feats, half), BF16),
            wide_halves,
            halves,
            shape((8, model), F32),
        ],
        [flags, scaled_one, own, away, vecs, g_own, g_pair, g_high, g_last],
        scratch=[pltpu.VMEM((model, half), BF16), pltpu.VMEM((model, half), BF16)],
        weight=0,
    )
    r_away = swap_bit(r_own, "col", 1)
    b_keep, b_give = call(
        wide_grad_kernel,
        "back_grads",
        [shape((n_rows, feats // 2, units), BF16)] * 2,
        [flags, r_own, r_away, hidden],
    )
    b_got = swap_bit(b_give, "dp", 1)
    mine, other, grad_pre, b_in_sums = call(
        backward_kernel,
        "feed_backward",
        [wide_halves, halves, shape((units, slot), BF16), shape((8, feats), F32)],
        [r_own, r_away, after(slope, b_give), in_all, back_all],
        weight=0,
    )
    own = sum_cores(mine, other)
    i_keep, i_give = call(
        wide_grad_kernel,
        "into_grads",
        [shape((n_rows, feats // 2, units), BF16)] * 2,
        [flags, after(n_own, own), n_away, grad_pre],
    )
    i_got = swap_bit(i_give, "dp", 1)
    away = swap_bit(own, "col", 2)
    grad_first, a_own, sums = call(
        norm_back_kernel,
        "norm_back",
        [wide_halves, halves, shape((8, model), F32)],
        [own, after(away, i_give), grad_second, scaled_one, inverse_one, vecs, sums],
        weight=0,
    )
    a_away = swap_bit(a_own, "col", 1)
    sums_away = swap_bit(sums, "col", 1)
    grad_qkv, kept, give = call(
        attend_back_kernel,
        "attend_back",
        [
            shape((3 * width, slot), BF16),
            shape((2 * feats, slot), F32),
            shape((2 * feats, slot), BF16),
        ],
        [flags, a_own, a_away, packs, qkv, prob, grad_first],
        scratch=[pltpu.VMEM((width, slot), BF16)],
        weight=0,
    )

    pack_keep, pack_give = call(
        pack_grad_kernel,
        "pack_grads",
        [shape((n_rows, feats + 16, 2 * width), BF16)] * 2,
        [flags, xs, grad_qkv, a_own, a_away, context, sums, sums_away, b_in_sums],
        weight=0,
    )

    in_own, in_away = call(
        join_kernel,
        "join",
        [shape((feats, slot), F32), shape((feats, slot), BF16)],
        [flags, after(kept, pack_give), swap_bit(give, "col", 1)],
    )
    (in_done,) = call(
        finish_kernel,
        "finish",
        [shape((feats, slot), BF16)],
        [flags, in_own, swap_bit(in_away, "col", 2)],
    )
    in_grad = from_slot(in_done).astype(F32)

    out_give = after(out_give, in_away)
    layer_out = from_slot(ordered(low_bit, out_own, swap_bit(out_give, "col", 1), 1))

    totals = []
    for name, keep, got in (
        ("back_add", b_keep, after(b_got, i_give)),
        ("into_add", i_keep, after(i_got, pack_give)),
    ):
        got = after(got, *totals)
        parts = call(
            pack_add_kernel, name, [shape((feats // 2, units), BF16)] * n_rows, [keep, got]
        )
        totals += [add_replicas(add_rows(parts), 2)]
    b_back, i_back = (swap_bit(total, "dp", 1) for total in totals)
    pack_got = after(swap_bit(pack_give, "dp", 1), totals[1], b_back)
    w_back_grad, w_in_grad = call(
        wide_unpack_kernel,
        "wide_unpack",
        [shape((feats, units), F32)] * 2,
        [flags, totals[0], b_back, totals[1], i_back],
    )
    packs = call(
        pack_add_kernel,
        "pack_add",
        [shape(pack_keep.shape[1:], BF16)] * n_rows,
        [pack_keep, pack_got],
    )
    total = add_replicas(add_rows(packs), 2)
    w_qkv_grad, w_out_grad, b_in_grad, *lines = call(
        unpack_kernel,
        "unpack",
        [
            shape((3 * feats, width), F32),
            shape((width, feats), F32),
            shape((units,), F32),
        ]
        + [shape((feats,), F32)] * 8,
        [flags, total, swap_bit(after(total, i_back), "dp", 1)],
    )
    w_qkv_grad = w_qkv_grad.reshape(3, feats, width).transpose(1, 0, 2)
    return (
        layer_out,
        in_grad,
        w_qkv_grad,
        lines[6],
        lines[7],
        w_out_grad,
        lines[4],
        lines[0],
        lines[1],
        w_in_grad,
        b_in_grad,
        w_back_grad,
        lines[5],
        lines[2],
        lines[3],
    )


def solution(mesh):
    tokens = P("row", ("dp", "col"))
    block = P("row", "col")
    in_specs = (
        tokens,
        P("dp"),
        P("row", None, "col"),
        P("col"),
        P("col"),
        P("col", "row"),
        P("row"),
        P("row"),
        P("row"),
        block,
        P("col"),
        block,
        P("row"),
        P("row"),
        P("row"),
        tokens,
    )
    out_specs = (
        tokens,
        tokens,
        P("row", None, "col"),
        P("col"),
        P("col"),
        P("col", "row"),
        P("row"),
        P("row"),
        P("row"),
        block,
        P("col"),
        block,
        P("row"),
        P("row"),
        P("row"),
    )
    return jax.shard_map(shards, mesh=mesh, in_specs=in_specs, out_specs=out_specs, check_vma=False)
```

```python
import jax
import jax.numpy as jnp
from jax import lax
from jax.experimental import pallas as pl
from jax.experimental.pallas import tpu as pltpu
from jax.sharding import PartitionSpec as P

HEAD_DIM = 64
EPSILON = 1e-12
F32 = jnp.float32
BF16 = jnp.bfloat16


def dot(left, right, left_dim, right_dim):
    return lax.dot_general(
        left, right, (((left_dim,), (right_dim,)), ((), ())), preferred_element_type=F32
    )


def call(kernel, name, outs, args, weight=0, scratch=(), specs=None, windowed=False, vmem_mib=16, out_specs=None):
    vmem = pl.BlockSpec(memory_space=pltpu.VMEM)
    in_specs = [
        pl.BlockSpec(memory_space=pltpu.SMEM) if arg.dtype == jnp.int32 else vmem for arg in args
    ]
    for at, spec in (specs or {}).items():
        in_specs[at] = spec
    return pl.pallas_call(
        kernel,
        name=name,
        out_shape=outs,
        grid=(1,) if windowed else (),
        in_specs=in_specs,
        out_specs=out_specs or [vmem] * len(outs),
        scratch_shapes=list(scratch),
        compiler_params=pltpu.CompilerParams(vmem_limit_bytes=vmem_mib * 1024 * 1024),
        cost_estimate=pl.CostEstimate(
            flops=weight * 2**30, bytes_accessed=weight * 2**22, transcendentals=0
        ),
    )(*args)


def shape(dims, dtype):
    return jax.ShapeDtypeStruct(dims, dtype)


def swap_bit(value, axis, bit):
    size = lax.axis_size(axis)
    return lax.ppermute(value, axis, [(at, at ^ bit) for at in range(size)])


def plane_of(slot):
    return (slot % 2) * 2 + slot // 2


def grid_pairs():
    size = lax.axis_size("row")
    return [
        (a * size + b, plane_of(b) * size + (a - plane_of(b)) % size)
        for a in range(size)
        for b in range(size)
    ]


def to_slot(value):
    return lax.ppermute(value, ("row", "col"), grid_pairs())


def from_slot(value):
    return lax.ppermute(value, ("row", "col"), [(b, a) for a, b in grid_pairs()])


def from_row(value, away):
    size = lax.axis_size("row")
    return lax.ppermute(value, "row", [((a + away) % size, a) for a in range(size)])


def after(value, *others):
    return lax.optimization_barrier((value,) + others)[0]


def ordered(flag, own, other, axis):
    return jnp.concatenate(
        (jnp.where(flag, other, own), jnp.where(flag, own, other)), axis=axis
    )


def identity(size):
    at = lax.broadcasted_iota(jnp.int32, (size, size), 0)
    return (at == lax.broadcasted_iota(jnp.int32, (size, size), 1)).astype(BF16)


def row_sums(products):
    total = 0.0
    for at, product in products.items():
        pick = lax.broadcasted_iota(jnp.int32, (8, product.shape[1]), 0) == at
        pick = pick.astype(BF16)
        high = product.astype(BF16)
        rest = (product - high.astype(F32)).astype(BF16)
        total = total + dot(pick, high, 1, 1) + dot(pick, rest, 1, 1)
    return total


def send_kernel(
    odd, w_qkv, w_out, w_in, w_back, b_in, v0, v1, v2, v3, v4, v5, v6, v7,
    half, wide, vectors, blocks, long_line, sems, *lines,
):
    size = w_out.shape[0]
    feats = w_in.shape[0]
    copies = [pltpu.make_async_copy(b_in, long_line, sems.at[0])]
    for at, ref in enumerate((v0, v1, v2, v3, v4, v5, v6, v7)):
        copies += [pltpu.make_async_copy(ref, lines[at], sems.at[at + 1])]
    into = wide.at[pl.ds(0, feats)]
    for part in range(2):

        @pl.when(odd[0] == part)
        def _():
            pltpu.make_async_copy((w_in, w_back)[part], into, sems.at[9]).start()
            first = w_qkv.at[pl.ds(2 * part * size, size)]
            pltpu.make_async_copy(first, blocks.at[0], sems.at[10]).start()
            second = (w_qkv.at[pl.ds(size, size)], w_out)[part]
            pltpu.make_async_copy(second, blocks.at[1], sems.at[11]).start()

    for copy in copies:
        copy.start()
    vectors[...] = jnp.zeros_like(vectors)
    for copy in copies:
        copy.wait()
    for at in range(8):
        vectors[at : at + 1, :feats] = lines[at][...].reshape(1, feats)
    vectors[8:9, :] = long_line[...].reshape(1, long_line.shape[0])
    wide[feats:] = vectors[...]
    pltpu.make_async_copy(w_in, into, sems.at[9]).wait()
    for at in range(2):
        pltpu.make_async_copy(w_out, blocks.at[at], sems.at[10 + at]).wait()
        half[:, at * size : (at + 1) * size] = blocks[at]


def attend_kernel(
    flags, x0, x1, x2, x3, fetched, swapped, vectors,
    xs, packs, qkv, prob, context, mine, other, raw, sems,
):
    low, odd, col, length = flags[0], flags[1], flags[2], flags[3]
    feats, slot = x0.shape
    half = slot // 2
    width = context.shape[0]
    row = flags[5]
    copies = []
    for k in range(4):
        for ref, part in ((fetched, odd), (swapped, 1 - odd)):
            ref = ref.at[lax.rem(row + k, 4)]
            copies += [pltpu.make_async_copy(ref, packs.at[k, part], sems.at[len(copies)])]
    for bit, ref in enumerate((x0, x1, x2, x3)):
        rows = pl.ds(pl.multiple_of((col ^ bit) * feats, feats), feats)
        copies += [pltpu.make_async_copy(ref, raw.at[rows], sems.at[len(copies)])]
    for copy in copies:
        copy.start()
    for copy in copies:
        copy.wait()

    @pl.when(low == 0)
    def _():
        xs[...] = raw[...]

    @pl.when(low == 1)
    def _():
        xs[:, :half] = raw[:, half:]
        xs[:, half:] = raw[:, :half]

    columns = dot(identity(width), vectors[:, :width], 1, 1)
    for part, bias in enumerate((columns[:, 6:7], 0.0, columns[:, 7:8])):
        total = bias
        for k in range(4):
            block = packs[k, part // 2, :, part % 2 * width : (part % 2 + 1) * width]
            total = total + dot(block, xs[k * feats : (k + 1) * feats], 0, 0)
        qkv[part * width : (part + 1) * width] = total.astype(BF16)

    place = lax.broadcasted_iota(jnp.int32, (slot, half), 0)
    place = jnp.where(low == 1, (place + half) % slot, place)
    live = place < length
    scale = HEAD_DIM ** (-0.5)
    for h in range(width // HEAD_DIM):
        q_rows = pl.ds(h * HEAD_DIM, HEAD_DIM)
        k_rows = pl.ds(width + h * HEAD_DIM, HEAD_DIM)
        v_rows = pl.ds(2 * width + h * HEAD_DIM, HEAD_DIM)
        for part in range(2):
            cols = slice(part * half, (part + 1) * half)
            scores = dot(qkv[k_rows, :], qkv[q_rows, cols], 0, 0) * scale
            scores = jnp.where(live, scores, -1000000000.0)
            exponent = jnp.exp(scores - jnp.max(scores, axis=0, keepdims=True))
            inverse = 1.0 / jnp.sum(exponent, axis=0, keepdims=True)
            weights = (exponent * inverse).astype(BF16)
            prob[h, :, cols] = weights
            context[q_rows, cols] = dot(qkv[v_rows, :], weights, 1, 0).astype(BF16)

    for k in range(4):
        rows = slice(k * feats, (k + 1) * feats)
        part = dot(packs[k, 1, :, width:], context[...], 0, 0)
        mine[rows] = part[:, :half]
        other[rows] = part[:, half:].astype(BF16)


def assemble_kernel(
    flags, own_in, own_back, v0, f1, f2, f3, s1, s2, s3, w_in, w_back, vecs, bias, rows, sems
):
    odd = flags[1]
    feats = own_in.shape[0]
    first = pl.ds(0, feats)
    copies = [
        pltpu.make_async_copy(own_in, w_in.at[first], sems.at[0]),
        pltpu.make_async_copy(own_back, w_back.at[first], sems.at[1]),
    ]
    for k, (f, s) in enumerate(((f1, s1), (f2, s2), (f3, s3))):
        span = pl.ds((k + 1) * feats, feats)
        for ref, into in ((f, (w_in, w_back)), (s, (w_back, w_in))):
            at = len(copies)
            ref = ref.at[first]
            even = pltpu.make_async_copy(ref, into[0].at[span], sems.at[at])
            other = pltpu.make_async_copy(ref, into[1].at[span], sems.at[at])
            copies += [(even, other)]
    for k, ref in enumerate((f1, f2, f3)):
        tail = ref.at[pl.ds(feats, 16)]
        copies += [pltpu.make_async_copy(tail, rows.at[k], sems.at[len(copies)])]
    for begin in (True, False):
        for copy in copies:
            if isinstance(copy, tuple):

                @pl.when(odd == 0)
                def _():
                    copy[0].start() if begin else copy[0].wait()

                @pl.when(odd == 1)
                def _():
                    copy[1].start() if begin else copy[1].wait()

            elif begin:
                copy.start()
            else:
                copy.wait()
    eye = identity(feats)
    vecs[:feats] = dot(eye, v0[:, :feats], 1, 1)
    for k in range(4):
        span = slice(k * feats, (k + 1) * feats)
        bias[span] = dot(eye, v0[:, span], 1, 1)
    for k in range(3):
        span = slice((k + 1) * feats, (k + 2) * feats)
        vecs[span] = dot(eye, rows[k, :, :feats], 1, 1)


def norm_kernel(x, own, away, vecs, scaled, inverse, low_normed):
    first = x[...].astype(F32) + own[...].astype(F32) + away[...].astype(F32) + vecs[:, 0:1]
    center = jnp.mean(first, axis=0, keepdims=True)
    first = first - center
    inv = lax.rsqrt(jnp.mean(first * first, axis=0, keepdims=True) + EPSILON)
    first = first * inv
    scaled[...] = first
    inverse[...] = jnp.broadcast_to(inv, inverse.shape)
    low_normed[...] = (first * vecs[:, 1:2] + vecs[:, 2:3]).astype(BF16)


def forward_kernel(n_own, n_away, w_in, w_back, bias, hidden, slope, mine, other):
    half = n_own.shape[1]
    step = 256
    for part, ref in enumerate((n_own, n_away)):
        cols = slice(part * half, (part + 1) * half)
        for at in range(0, w_in.shape[1], step):
            rows = slice(at, at + step)
            pre = dot(w_in[:, rows], ref[...], 0, 0) + bias[rows, 8:9]
            share = 0.5 * (1.0 + lax.erf(pre * (0.5**0.5)))
            hidden[rows, cols] = (pre * share).astype(BF16)
            bell = jnp.exp(-0.5 * pre * pre) * ((0.5 / jnp.pi) ** 0.5)
            slope[rows, cols] = (share + pre * bell).astype(BF16)
    mine[...] = dot(w_back[...], hidden[:, :half], 1, 0)
    other[...] = dot(w_back[...], hidden[:, half:], 1, 0).astype(BF16)


def turn_kernel(
    flags, scaled_one, own, away, vecs, g_own, g_pair, g_high, g_last,
    keep, give, grad_second, grad_returned, sums, final, grad,
):
    low, col, length = flags[0], flags[2], flags[3]
    feats = g_own.shape[0]
    half = own.shape[1]

    def rows(bit):
        return pl.ds(pl.multiple_of((col ^ bit) * feats, feats), feats)

    for bit, ref in enumerate((g_own, g_pair, g_high, g_last)):

        @pl.when(low == 0)
        def _():
            grad[rows(bit), :] = ref[:, :half]

        @pl.when(low == 1)
        def _():
            grad[rows(bit), :] = ref[:, half:]

    normed = scaled_one[...] * vecs[:, 1:2] + vecs[:, 2:3]
    second = normed + own[...].astype(F32) + away[...].astype(F32) + vecs[:, 3:4]
    second = second - jnp.mean(second, axis=0, keepdims=True)
    inv = lax.rsqrt(jnp.mean(second * second, axis=0, keepdims=True) + EPSILON)
    scaled = second * inv
    place = low * half + lax.broadcasted_iota(jnp.int32, (1, half), 1)
    live = (place < length).astype(F32)
    final[...] = ((scaled * vecs[:, 4:5] + vecs[:, 5:6]) * live).astype(BF16)
    keep[...] = final[rows(0), :]
    give[...] = final[rows(1), :]
    upstream = grad[...].astype(F32) * live
    weighted = upstream * vecs[:, 4:5]
    mean = jnp.mean(weighted, axis=0, keepdims=True)
    tilt = jnp.mean(weighted * scaled, axis=0, keepdims=True)
    back = inv * (weighted - mean - scaled * tilt)
    grad_second[...] = back
    grad_returned[...] = back.astype(BF16)
    sums[...] = row_sums({2: upstream * scaled, 3: upstream, 5: back})


def backward_kernel(r_own, r_away, slope, w_in, w_back, mine, other, grad_pre, b_in_sums):
    half = r_own.shape[1]
    step = 256
    for part, ref in enumerate((r_own, r_away)):
        cols = slice(part * half, (part + 1) * half)
        for at in range(0, w_in.shape[1], step):
            rows = slice(at, at + step)
            grad_hidden = dot(w_back[:, rows], ref[...], 0, 0)
            grad_pre[rows, cols] = (grad_hidden * slope[rows, cols].astype(F32)).astype(BF16)
    mine[...] = dot(w_in[...], grad_pre[:, :half], 1, 0)
    other[...] = dot(w_in[...], grad_pre[:, half:], 1, 0).astype(BF16)
    size = b_in_sums.shape[1]
    total = 0.0
    for k in range(w_in.shape[1] // size):
        pick = lax.broadcasted_iota(jnp.int32, (8, 2 * half), 0) == k
        total = total + dot(pick.astype(BF16), grad_pre[k * size : (k + 1) * size], 1, 1)
    b_in_sums[...] = total


def wide_grad_kernel(flags, own, away, right, keep, give):
    odd = flags[1]
    half = own.shape[1]
    part = keep.shape[1]
    for k in range(4):
        for pick, out in ((1 - odd, give), (odd, keep)):
            rows = pl.ds(pl.multiple_of((2 * k + pick) * part, part), part)
            total = dot(own[rows, :], right[:, :half], 1, 1)
            total = total + dot(away[rows, :], right[:, half:], 1, 1)
            out[k] = total.astype(BF16)


def norm_back_kernel(
    own, away, grad_second, scaled, inverse, vecs, sums, grad_first, low_first, sums_out
):
    upstream = grad_second[...] + own[...].astype(F32) + away[...].astype(F32)
    weighted = upstream * vecs[:, 1:2]
    mean = jnp.mean(weighted, axis=0, keepdims=True)
    tilt = jnp.mean(weighted * scaled[...], axis=0, keepdims=True)
    back = inverse[0:1] * (weighted - mean - scaled[...] * tilt)
    grad_first[...] = back
    low_first[...] = back.astype(BF16)
    sums_out[...] = sums[...] + row_sums({0: upstream * scaled[...], 1: upstream, 4: back})


def attend_back_kernel(
    flags, a_own, a_away, packs, qkv, prob, grad_first, grad_qkv, keep, give, grad_context
):
    low = flags[0]
    half = a_own.shape[1]
    feats = packs.shape[2]
    width = grad_context.shape[0]
    for part, ref in enumerate((a_own, a_away)):
        cols = slice(part * half, (part + 1) * half)
        total = 0.0
        for k in range(4):
            total = total + dot(packs[k, 1, :, width:], ref[k * feats : (k + 1) * feats], 1, 0)
        grad_context[:, cols] = total.astype(BF16)
    scale = HEAD_DIM ** (-0.5)
    for h in range(width // HEAD_DIM):
        q_rows = pl.ds(h * HEAD_DIM, HEAD_DIM)
        k_rows = pl.ds(width + h * HEAD_DIM, HEAD_DIM)
        v_rows = pl.ds(2 * width + h * HEAD_DIM, HEAD_DIM)
        grad_keys, grad_values = 0.0, 0.0
        for part in range(2):
            cols = slice(part * half, (part + 1) * half)
            weights = prob[h, :, cols]
            wide = weights.astype(F32)
            grad_weights = dot(qkv[v_rows, :], grad_context[q_rows, cols], 0, 0)
            inner = jnp.sum(wide * grad_weights, axis=0, keepdims=True)
            grad_scores = (wide * (grad_weights - inner)).astype(BF16)
            grad_qkv[q_rows, cols] = (dot(qkv[k_rows, :], grad_scores, 1, 0) * scale).astype(BF16)
            grad_keys = grad_keys + dot(qkv[q_rows, cols], grad_scores, 1, 1)
            grad_values = grad_values + dot(grad_context[q_rows, cols], weights, 1, 1)
        grad_qkv[k_rows, :] = (grad_keys * scale).astype(BF16)
        grad_qkv[v_rows, :] = grad_values.astype(BF16)

    def block(k):
        part = 0.0
        for at in range(3):
            left = packs[k, at // 2, :, at % 2 * width : (at % 2 + 1) * width]
            part = part + dot(left, grad_qkv[at * width : (at + 1) * width], 1, 0)
        rows = pl.ds(pl.multiple_of(k * feats, feats), feats)
        return part[:, :half] + 0.5 * grad_first[rows, :], part[:, half:]

    for j in range(2):
        rows = slice(j * feats, (j + 1) * feats)
        near, far = block(2 * j + 1 - low)
        give[rows, :half] = near.astype(BF16)
        give[rows, half:] = far.astype(BF16)
        near, far = block(2 * j + low)
        keep[rows, :half] = near
        keep[rows, half:] = far


def pack_grad_kernel(
    flags, xs, grad_qkv, a_own, a_away, context, sums, sums_away, b_in_sums, keep, give
):
    odd = flags[1]
    width = context.shape[0]
    feats = keep.shape[1] - 16
    half = a_own.shape[1]
    ones = (lax.broadcasted_iota(jnp.int32, (8, 2 * half), 0) == 4).astype(BF16)
    more = (lax.broadcasted_iota(jnp.int32, (8, 2 * half), 0) == 5).astype(BF16)
    shared = b_in_sums[...] + dot(ones, grad_qkv[:width], 1, 1)
    shared = shared + dot(more, grad_qkv[2 * width :], 1, 1)
    vector_sums = sums[...] + sums_away[...]
    none = jnp.zeros((16, 2 * feats), BF16)
    for k in range(4):
        span = slice(k * feats, (k + 1) * feats)
        blocks = [
            dot(xs[span], grad_qkv[at * width : (at + 1) * width], 1, 1) for at in range(3)
        ]
        last = dot(context[:, :half], a_own[span], 1, 1)
        blocks += [last + dot(context[:, half:], a_away[span], 1, 1)]
        tail = jnp.concatenate((vector_sums[:, span], shared), axis=1)
        tail = jnp.concatenate((tail, jnp.zeros_like(tail)), axis=0).astype(BF16)
        for part in range(2):
            pair = jnp.concatenate(blocks[2 * part : 2 * part + 2], axis=1).astype(BF16)
            rest = none if part else tail
            for out, at in ((keep, odd), (give, 1 - odd)):

                @pl.when(at == part)
                def _():
                    out[k, :feats] = pair
                    out[k, feats:] = rest


def pack_add_kernel(keep, got, *outs):
    for k, out in enumerate(outs):
        out[...] = (keep[k].astype(F32) + got[k].astype(F32)).astype(BF16)


def unpack_kernel(flags, own, got, qkv, w_out, b_in, *lines):
    odd = flags[1]
    feats, width = w_out.shape[1], w_out.shape[0]

    def write(first, second):
        qkv[:feats] = first[:feats, :width].astype(F32)
        qkv[feats : 2 * feats] = first[:feats, width:].astype(F32)
        qkv[2 * feats :] = second[:feats, :width].astype(F32)
        w_out[...] = second[:feats, width:].astype(F32)
        tail = first[feats:].astype(F32)
        for at in range(6):
            lines[at][...] = tail[at, :feats]
        for at in range(4):
            b_in[at * feats : (at + 1) * feats] = tail[at, feats:]
        for at in range(2):
            lines[6 + at][...] = tail[4 + at, feats:]

    @pl.when(odd == 0)
    def _():
        write(own, got)

    @pl.when(odd == 1)
    def _():
        write(got, own)


def wide_unpack_kernel(flags, b_own, b_got, i_own, i_got, back, into):
    odd = flags[1]
    part = b_own.shape[0]
    for out, own, got in ((back, b_own, b_got), (into, i_own, i_got)):
        for ref, at in ((own, odd), (got, 1 - odd)):
            rows = pl.ds(pl.multiple_of(at * part, part), part)
            out[rows, :] = ref[...].astype(F32)


def join_kernel(flags, kept, got, own, away):
    high = flags[4]
    feats = own.shape[0]
    half = own.shape[1] // 2
    for out, at in ((own, high), (away, 1 - high)):
        rows = pl.ds(pl.multiple_of(at * feats, feats), feats)
        near = kept[rows, :half] + got[rows, half:].astype(F32)
        far = kept[rows, half:] + got[rows, :half].astype(F32)
        out[:, :half] = near.astype(out.dtype)
        out[:, half:] = far.astype(out.dtype)


def finish_kernel(flags, own, got, out):
    low = flags[0]
    half = own.shape[1] // 2
    total = (own[...] + got[...].astype(F32)).astype(BF16)

    @pl.when(low == 0)
    def _():
        out[...] = total

    @pl.when(low == 1)
    def _():
        out[:, :half] = total[:, half:]
        out[:, half:] = total[:, :half]


def shards(
    layer_in,
    seq_lengths,
    w_qkv,
    q_bias,
    v_bias,
    w_out,
    b_out,
    ln1_gain,
    ln1_bias,
    w_in,
    b_in,
    w_back,
    b_back,
    ln2_gain,
    ln2_bias,
    out_grad,
):
    n_rows = lax.axis_size("row")
    row, col = lax.axis_index("row"), lax.axis_index("col")
    low_bit = (col % 2) == 1
    odd_bit = lax.axis_index("dp") % 2
    odd = odd_bit == 1
    feats, slot = layer_in.shape
    half = slot // 2
    width = w_out.shape[0]
    model = n_rows * feats
    units = w_in.shape[1]
    heads = width // HEAD_DIM
    length = lax.dynamic_index_in_dim(seq_lengths, plane_of(row), 0, False)
    flags = jnp.stack((col % 2, odd_bit, col, length, col // 2, row)).astype(jnp.int32)
    halves = shape((model, half), BF16)
    wide_halves = shape((model, half), F32)

    def sum_cores(mine, other):
        return (mine + swap_bit(other, "col", 1).astype(F32)).astype(BF16)

    def add_rows(blocks):
        parts = [from_row(blocks[k], n_rows - k) for k in range(1, n_rows)]
        terms = [term.astype(F32) for term in (blocks[0], *parts)]
        while len(terms) > 1:
            pairs = len(terms) // 2
            terms = [terms[i] + terms[i + pairs] for i in range(pairs)]
        return terms[0].astype(BF16)

    def add_replicas(total, first):
        bit = first
        while bit < lax.axis_size("dp"):
            total = total.astype(F32) + swap_bit(total, "dp", bit).astype(F32)
            total = total.astype(BF16)
            bit *= 2
        return total

    x0 = to_slot(layer_in)
    qkv_part = w_qkv.transpose(1, 0, 2).reshape(3 * feats, width)
    pack_half, wide, vectors = call(
        send_kernel,
        "send",
        [
            shape((feats, 2 * width), BF16),
            shape((feats + 16, units), BF16),
            shape((16, units), BF16),
        ],
        [odd_bit.reshape(1), qkv_part, w_out, w_in, w_back, b_in]
        + [b_out, ln1_gain, ln1_bias, b_back, ln2_gain, ln2_bias, q_bias, v_bias],
        specs={k: pl.BlockSpec(memory_space=pl.ANY) for k in range(1, 14)},
        out_specs=[
            pl.BlockSpec(memory_space=pltpu.VMEM)
        ]
        * 3,
        scratch=[
            pltpu.VMEM((2, feats, width), BF16),
            pltpu.VMEM((units,), BF16),
            pltpu.SemaphoreType.DMA((12,)),
        ]
        + [pltpu.VMEM((feats,), BF16)] * 8,
        vmem_mib=56,
    )
    fetched = lax.all_gather(after(pack_half, wide), "row")
    swapped = swap_bit(fetched, "dp", 1)
    wide = after(wide, fetched)
    wide_fetched = [from_row(wide, 1), None, from_row(wide, 3)]
    wide_fetched[1] = from_row(wide_fetched[0], 1)
    x0 = after(x0, flags, fetched)
    x2 = swap_bit(x0, "col", 2)
    x1 = swap_bit(x0, "col", 1)
    wide_swapped = [swap_bit(after(part, x2), "dp", 1) for part in wide_fetched]
    g_own = to_slot(after(out_grad.astype(BF16), fetched))
    g_high = swap_bit(g_own, "col", 2)
    ready = (wide_swapped[0], wide_fetched[1], wide_swapped[2], g_high)
    x3 = swap_bit(after(x2, swapped, *ready), "col", 1)

    in_all, back_all, vecs, in_bias = call(
        assemble_kernel,
        "assemble",
        [shape((model, units), BF16)] * 2 + [shape((model, 16), F32), shape((units, 16), F32)],
        [flags, w_in, w_back, vectors] + wide_fetched + wide_swapped,
        specs={k: pl.BlockSpec(memory_space=pl.ANY) for k in (1, 2, 4, 5, 6, 7, 8, 9)},
        scratch=[pltpu.VMEM((3, 16, units), BF16), pltpu.SemaphoreType.DMA((11,))],
    )

    xs, packs, qkv, prob, context, mine, other = call(
        attend_kernel,
        "attend",
        [
            shape((model, slot), BF16),
            shape((n_rows, 2, feats, 2 * width), BF16),
            shape((3 * width, slot), BF16),
            shape((heads, slot, slot), BF16),
            shape((width, slot), BF16),
            wide_halves,
            halves,
        ],
        [flags, x0, x1, x2, x3, fetched, swapped, vectors],
        specs={k: pl.BlockSpec(memory_space=pl.ANY) for k in range(1, 7)},
        scratch=[pltpu.VMEM((model, slot), BF16), pltpu.SemaphoreType.DMA((12,))],
        vmem_mib=40,
        weight=0,
    )

    own = sum_cores(mine, other)
    away = swap_bit(own, "col", 2)
    scaled_one, inverse_one, n_own = call(
        norm_kernel,
        "norm",
        [wide_halves, shape((8, half), F32), halves],
        [xs, own, away, vecs],
        specs={0: pl.BlockSpec((model, half), lambda _: (0, 0))},
        windowed=True,
        weight=0,
    )

    n_away = swap_bit(n_own, "col", 1)
    hidden, slope, mine, other = call(
        forward_kernel,
        "feed_forward",
        [shape((units, slot), BF16), shape((units, slot), BF16), wide_halves, halves],
        [n_own, n_away, in_all, back_all, in_bias],
        weight=0,
    )
    g_pair = swap_bit(g_own, "col", 1)
    g_last = swap_bit(g_high, "col", 1)
    own = sum_cores(mine, other)
    away = swap_bit(own, "col", 2)
    out_own, out_give, grad_second, r_own, sums = call(
        turn_kernel,
        "turn",
        [
            shape((feats, half), BF16),
            shape((feats, half), BF16),
            wide_halves,
            halves,
            shape((8, model), F32),
        ],
        [flags, scaled_one, own, away, vecs, g_own, g_pair, g_high, g_last],
        scratch=[pltpu.VMEM((model, half), BF16), pltpu.VMEM((model, half), BF16)],
        weight=0,
    )
    r_away = swap_bit(r_own, "col", 1)
    b_keep, b_give = call(
        wide_grad_kernel,
        "back_grads",
        [shape((n_rows, feats // 2, units), BF16)] * 2,
        [flags, r_own, r_away, hidden],
    )
    b_got = swap_bit(b_give, "dp", 1)
    mine, other, grad_pre, b_in_sums = call(
        backward_kernel,
        "feed_backward",
        [wide_halves, halves, shape((units, slot), BF16), shape((8, feats), F32)],
        [r_own, r_away, after(slope, b_give), in_all, back_all],
        weight=0,
    )
    own = sum_cores(mine, other)
    i_keep, i_give = call(
        wide_grad_kernel,
        "into_grads",
        [shape((n_rows, feats // 2, units), BF16)] * 2,
        [flags, after(n_own, own), n_away, grad_pre],
    )
    i_got = swap_bit(i_give, "dp", 1)
    away = swap_bit(own, "col", 2)
    grad_first, a_own, sums = call(
        norm_back_kernel,
        "norm_back",
        [wide_halves, halves, shape((8, model), F32)],
        [own, after(away, i_give), grad_second, scaled_one, inverse_one, vecs, sums],
        weight=0,
    )
    a_away = swap_bit(a_own, "col", 1)
    sums_away = swap_bit(sums, "col", 1)
    grad_qkv, kept, give = call(
        attend_back_kernel,
        "attend_back",
        [
            shape((3 * width, slot), BF16),
            shape((2 * feats, slot), F32),
            shape((2 * feats, slot), BF16),
        ],
        [flags, a_own, a_away, packs, qkv, prob, grad_first],
        scratch=[pltpu.VMEM((width, slot), BF16)],
        weight=0,
    )

    pack_keep, pack_give = call(
        pack_grad_kernel,
        "pack_grads",
        [shape((n_rows, feats + 16, 2 * width), BF16)] * 2,
        [flags, xs, grad_qkv, a_own, a_away, context, sums, sums_away, b_in_sums],
        weight=0,
    )

    in_own, in_away = call(
        join_kernel,
        "join",
        [shape((feats, slot), F32), shape((feats, slot), BF16)],
        [flags, after(kept, pack_give), swap_bit(give, "col", 1)],
    )
    (in_done,) = call(
        finish_kernel,
        "finish",
        [shape((feats, slot), BF16)],
        [flags, in_own, swap_bit(in_away, "col", 2)],
    )
    in_grad = from_slot(in_done).astype(F32)

    out_give = after(out_give, in_away)
    layer_out = from_slot(ordered(low_bit, out_own, swap_bit(out_give, "col", 1), 1))

    totals = []
    for name, keep, got in (
        ("back_add", b_keep, after(b_got, i_give)),
        ("into_add", i_keep, after(i_got, pack_give)),
    ):
        got = after(got, *totals)
        parts = call(
            pack_add_kernel, name, [shape((feats // 2, units), BF16)] * n_rows, [keep, got]
        )
        totals += [add_replicas(add_rows(parts), 2)]
    b_back, i_back = (swap_bit(total, "dp", 1) for total in totals)
    pack_got = after(swap_bit(pack_give, "dp", 1), b_back)
    w_back_grad, w_in_grad = call(
        wide_unpack_kernel,
        "wide_unpack",
        [shape((feats, units), F32)] * 2,
        [flags, totals[0], b_back, totals[1], i_back],
    )
    packs = call(
        pack_add_kernel,
        "pack_add",
        [shape(pack_keep.shape[1:], BF16)] * n_rows,
        [pack_keep, pack_got],
    )
    total = add_replicas(add_rows(packs), 2)
    w_qkv_grad, w_out_grad, b_in_grad, *lines = call(
        unpack_kernel,
        "unpack",
        [
            shape((3 * feats, width), F32),
            shape((width, feats), F32),
            shape((units,), F32),
        ]
        + [shape((feats,), F32)] * 8,
        [flags, total, swap_bit(after(total, i_back), "dp", 1)],
    )
    w_qkv_grad = w_qkv_grad.reshape(3, feats, width).transpose(1, 0, 2)
    return (
        layer_out,
        in_grad,
        w_qkv_grad,
        lines[6],
        lines[7],
        w_out_grad,
        lines[4],
        lines[0],
        lines[1],
        w_in_grad,
        b_in_grad,
        w_back_grad,
        lines[5],
        lines[2],
        lines[3],
    )


def solution(mesh):
    tokens = P("row", ("dp", "col"))
    block = P("row", "col")
    in_specs = (
        tokens,
        P("dp"),
        P("row", None, "col"),
        P("col"),
        P("col"),
        P("col", "row"),
        P("row"),
        P("row"),
        P("row"),
        block,
        P("col"),
        block,
        P("row"),
        P("row"),
        P("row"),
        tokens,
    )
    out_specs = (
        tokens,
        tokens,
        P("row", None, "col"),
        P("col"),
        P("col"),
        P("col", "row"),
        P("row"),
        P("row"),
        P("row"),
        block,
        P("col"),
        block,
        P("row"),
        P("row"),
        P("row"),
    )
    return jax.shard_map(shards, mesh=mesh, in_specs=in_specs, out_specs=out_specs, check_vma=False)
```

```python
import jax
import jax.numpy as jnp
from jax import lax
from jax.experimental import pallas as pl
from jax.experimental.pallas import tpu as pltpu
from jax.sharding import PartitionSpec as P

HEAD_DIM = 64
EPSILON = 1e-12
F32 = jnp.float32
BF16 = jnp.bfloat16


def dot(left, right, left_dim, right_dim):
    return lax.dot_general(
        left, right, (((left_dim,), (right_dim,)), ((), ())), preferred_element_type=F32
    )


def call(kernel, name, outs, args, weight=0, scratch=(), specs=None, windowed=False, vmem_mib=16, out_specs=None):
    vmem = pl.BlockSpec(memory_space=pltpu.VMEM)
    in_specs = [
        pl.BlockSpec(memory_space=pltpu.SMEM) if arg.dtype == jnp.int32 else vmem for arg in args
    ]
    for at, spec in (specs or {}).items():
        in_specs[at] = spec
    return pl.pallas_call(
        kernel,
        name=name,
        out_shape=outs,
        grid=(1,) if windowed else (),
        in_specs=in_specs,
        out_specs=out_specs or [vmem] * len(outs),
        scratch_shapes=list(scratch),
        compiler_params=pltpu.CompilerParams(vmem_limit_bytes=vmem_mib * 1024 * 1024),
        cost_estimate=pl.CostEstimate(
            flops=weight * 2**30, bytes_accessed=weight * 2**22, transcendentals=0
        ),
    )(*args)


def shape(dims, dtype):
    return jax.ShapeDtypeStruct(dims, dtype)


def swap_bit(value, axis, bit):
    size = lax.axis_size(axis)
    return lax.ppermute(value, axis, [(at, at ^ bit) for at in range(size)])


def plane_of(slot):
    return (slot % 2) * 2 + slot // 2


def grid_pairs():
    size = lax.axis_size("row")
    return [
        (a * size + b, plane_of(b) * size + (a - plane_of(b)) % size)
        for a in range(size)
        for b in range(size)
    ]


def to_slot(value):
    return lax.ppermute(value, ("row", "col"), grid_pairs())


def from_slot(value):
    return lax.ppermute(value, ("row", "col"), [(b, a) for a, b in grid_pairs()])


def from_row(value, away):
    size = lax.axis_size("row")
    return lax.ppermute(value, "row", [((a + away) % size, a) for a in range(size)])


def after(value, *others):
    return lax.optimization_barrier((value,) + others)[0]


def ordered(flag, own, other, axis):
    return jnp.concatenate(
        (jnp.where(flag, other, own), jnp.where(flag, own, other)), axis=axis
    )


def identity(size):
    at = lax.broadcasted_iota(jnp.int32, (size, size), 0)
    return (at == lax.broadcasted_iota(jnp.int32, (size, size), 1)).astype(BF16)


def row_sums(products):
    total = 0.0
    for at, product in products.items():
        pick = lax.broadcasted_iota(jnp.int32, (8, product.shape[1]), 0) == at
        pick = pick.astype(BF16)
        high = product.astype(BF16)
        rest = (product - high.astype(F32)).astype(BF16)
        total = total + dot(pick, high, 1, 1) + dot(pick, rest, 1, 1)
    return total


def send_kernel(
    odd, w_qkv, w_out, w_in, w_back, b_in, v0, v1, v2, v3, v4, v5, v6, v7,
    half, wide, vectors, blocks, long_line, sems, *lines,
):
    size = w_out.shape[0]
    feats = w_in.shape[0]
    copies = [pltpu.make_async_copy(b_in, long_line, sems.at[0])]
    for at, ref in enumerate((v0, v1, v2, v3, v4, v5, v6, v7)):
        copies += [pltpu.make_async_copy(ref, lines[at], sems.at[at + 1])]
    into = wide.at[pl.ds(0, feats)]
    for part in range(2):

        @pl.when(odd[0] == part)
        def _():
            pltpu.make_async_copy((w_in, w_back)[part], into, sems.at[9]).start()
            first = w_qkv.at[pl.ds(2 * part * size, size)]
            pltpu.make_async_copy(first, blocks.at[0], sems.at[10]).start()
            second = (w_qkv.at[pl.ds(size, size)], w_out)[part]
            pltpu.make_async_copy(second, blocks.at[1], sems.at[11]).start()

    for copy in copies:
        copy.start()
    for copy in copies:
        copy.wait()
    units = long_line.shape[0]
    short = jnp.concatenate([line[...].astype(F32).reshape(1, feats) for line in lines], axis=0)
    short = jnp.concatenate((short, jnp.zeros((8, units - feats), F32)), axis=1)
    long = long_line[...].astype(F32).reshape(1, units)
    long = jnp.concatenate((long, jnp.zeros((7, units), F32)), axis=0)
    vectors[...] = jnp.concatenate((short, long), axis=0).astype(BF16)
    wide[feats:] = vectors[...]
    pltpu.make_async_copy(w_in, into, sems.at[9]).wait()
    for at in range(2):
        pltpu.make_async_copy(w_out, blocks.at[at], sems.at[10 + at]).wait()
        half[:, at * size : (at + 1) * size] = blocks[at]


def attend_kernel(
    flags, x0, x1, x2, x3, fetched, swapped, vectors,
    xs, packs, qkv, prob, context, mine, other, raw, sems,
):
    low, odd, col, length = flags[0], flags[1], flags[2], flags[3]
    feats, slot = x0.shape
    half = slot // 2
    width = context.shape[0]
    row = flags[5]
    copies = []
    for k in range(4):
        for ref, part in ((fetched, odd), (swapped, 1 - odd)):
            ref = ref.at[lax.rem(row + k, 4)]
            copies += [pltpu.make_async_copy(ref, packs.at[k, part], sems.at[len(copies)])]
    for bit, ref in enumerate((x0, x1, x2, x3)):
        rows = pl.ds(pl.multiple_of((col ^ bit) * feats, feats), feats)
        copies += [pltpu.make_async_copy(ref, raw.at[rows], sems.at[len(copies)])]
    for copy in copies:
        copy.start()
    for copy in copies:
        copy.wait()

    @pl.when(low == 0)
    def _():
        xs[...] = raw[...]

    @pl.when(low == 1)
    def _():
        xs[:, :half] = raw[:, half:]
        xs[:, half:] = raw[:, :half]

    columns = dot(identity(width), vectors[:, :width], 1, 1)
    for part, bias in enumerate((columns[:, 6:7], 0.0, columns[:, 7:8])):
        total = bias
        for k in range(4):
            block = packs[k, part // 2, :, part % 2 * width : (part % 2 + 1) * width]
            total = total + dot(block, xs[k * feats : (k + 1) * feats], 0, 0)
        qkv[part * width : (part + 1) * width] = total.astype(BF16)

    place = lax.broadcasted_iota(jnp.int32, (slot, half), 0)
    place = jnp.where(low == 1, (place + half) % slot, place)
    live = place < length
    scale = HEAD_DIM ** (-0.5)
    for h in range(width // HEAD_DIM):
        q_rows = pl.ds(h * HEAD_DIM, HEAD_DIM)
        k_rows = pl.ds(width + h * HEAD_DIM, HEAD_DIM)
        v_rows = pl.ds(2 * width + h * HEAD_DIM, HEAD_DIM)
        for part in range(2):
            cols = slice(part * half, (part + 1) * half)
            scores = dot(qkv[k_rows, :], qkv[q_rows, cols], 0, 0) * scale
            scores = jnp.where(live, scores, -1000000000.0)
            exponent = jnp.exp(scores - jnp.max(scores, axis=0, keepdims=True))
            inverse = 1.0 / jnp.sum(exponent, axis=0, keepdims=True)
            weights = (exponent * inverse).astype(BF16)
            prob[h, :, cols] = weights
            context[q_rows, cols] = dot(qkv[v_rows, :], weights, 1, 0).astype(BF16)

    for k in range(4):
        rows = slice(k * feats, (k + 1) * feats)
        part = dot(packs[k, 1, :, width:], context[...], 0, 0)
        mine[rows] = part[:, :half]
        other[rows] = part[:, half:].astype(BF16)


def assemble_kernel(
    flags, own_in, own_back, v0, f1, f2, f3, s1, s2, s3, w_in, w_back, vecs, bias, rows, sems
):
    odd = flags[1]
    feats = own_in.shape[0]
    first = pl.ds(0, feats)
    copies = [
        pltpu.make_async_copy(own_in, w_in.at[first], sems.at[0]),
        pltpu.make_async_copy(own_back, w_back.at[first], sems.at[1]),
    ]
    for k, (f, s) in enumerate(((f1, s1), (f2, s2), (f3, s3))):
        span = pl.ds((k + 1) * feats, feats)
        for ref, into in ((f, (w_in, w_back)), (s, (w_back, w_in))):
            at = len(copies)
            ref = ref.at[first]
            even = pltpu.make_async_copy(ref, into[0].at[span], sems.at[at])
            other = pltpu.make_async_copy(ref, into[1].at[span], sems.at[at])
            copies += [(even, other)]
    for k, ref in enumerate((f1, f2, f3)):
        tail = ref.at[pl.ds(feats, 16)]
        copies += [pltpu.make_async_copy(tail, rows.at[k], sems.at[len(copies)])]
    for begin in (True, False):
        for copy in copies:
            if isinstance(copy, tuple):

                @pl.when(odd == 0)
                def _():
                    copy[0].start() if begin else copy[0].wait()

                @pl.when(odd == 1)
                def _():
                    copy[1].start() if begin else copy[1].wait()

            elif begin:
                copy.start()
            else:
                copy.wait()
    eye = identity(feats)
    vecs[:feats] = dot(eye, v0[:, :feats], 1, 1)
    for k in range(4):
        span = slice(k * feats, (k + 1) * feats)
        bias[span] = dot(eye, v0[:, span], 1, 1)
    for k in range(3):
        span = slice((k + 1) * feats, (k + 2) * feats)
        vecs[span] = dot(eye, rows[k, :, :feats], 1, 1)


def norm_kernel(x, own, away, vecs, scaled, inverse, low_normed):
    first = x[...].astype(F32) + own[...].astype(F32) + away[...].astype(F32) + vecs[:, 0:1]
    center = jnp.mean(first, axis=0, keepdims=True)
    first = first - center
    inv = lax.rsqrt(jnp.mean(first * first, axis=0, keepdims=True) + EPSILON)
    first = first * inv
    scaled[...] = first
    inverse[...] = jnp.broadcast_to(inv, inverse.shape)
    low_normed[...] = (first * vecs[:, 1:2] + vecs[:, 2:3]).astype(BF16)


def forward_kernel(n_own, n_away, w_in, w_back, bias, hidden, slope, mine, other):
    half = n_own.shape[1]
    step = 256
    for part, ref in enumerate((n_own, n_away)):
        cols = slice(part * half, (part + 1) * half)
        for at in range(0, w_in.shape[1], step):
            rows = slice(at, at + step)
            pre = dot(w_in[:, rows], ref[...], 0, 0) + bias[rows, 8:9]
            share = 0.5 * (1.0 + lax.erf(pre * (0.5**0.5)))
            hidden[rows, cols] = (pre * share).astype(BF16)
            bell = jnp.exp(-0.5 * pre * pre) * ((0.5 / jnp.pi) ** 0.5)
            slope[rows, cols] = (share + pre * bell).astype(BF16)
    mine[...] = dot(w_back[...], hidden[:, :half], 1, 0)
    other[...] = dot(w_back[...], hidden[:, half:], 1, 0).astype(BF16)


def turn_kernel(
    flags, scaled_one, own, away, vecs, g_own, g_pair, g_high, g_last,
    keep, give, grad_second, grad_returned, sums, final, grad,
):
    low, col, length = flags[0], flags[2], flags[3]
    feats = g_own.shape[0]
    half = own.shape[1]

    def rows(bit):
        return pl.ds(pl.multiple_of((col ^ bit) * feats, feats), feats)

    for bit, ref in enumerate((g_own, g_pair, g_high, g_last)):

        @pl.when(low == 0)
        def _():
            grad[rows(bit), :] = ref[:, :half]

        @pl.when(low == 1)
        def _():
            grad[rows(bit), :] = ref[:, half:]

    normed = scaled_one[...] * vecs[:, 1:2] + vecs[:, 2:3]
    second = normed + own[...].astype(F32) + away[...].astype(F32) + vecs[:, 3:4]
    second = second - jnp.mean(second, axis=0, keepdims=True)
    inv = lax.rsqrt(jnp.mean(second * second, axis=0, keepdims=True) + EPSILON)
    scaled = second * inv
    place = low * half + lax.broadcasted_iota(jnp.int32, (1, half), 1)
    live = (place < length).astype(F32)
    final[...] = ((scaled * vecs[:, 4:5] + vecs[:, 5:6]) * live).astype(BF16)
    keep[...] = final[rows(0), :]
    give[...] = final[rows(1), :]
    upstream = grad[...].astype(F32) * live
    weighted = upstream * vecs[:, 4:5]
    mean = jnp.mean(weighted, axis=0, keepdims=True)
    tilt = jnp.mean(weighted * scaled, axis=0, keepdims=True)
    back = inv * (weighted - mean - scaled * tilt)
    grad_second[...] = back
    grad_returned[...] = back.astype(BF16)
    sums[...] = row_sums({2: upstream * scaled, 3: upstream, 5: back})


def backward_kernel(r_own, r_away, slope, w_in, w_back, mine, other, grad_pre, b_in_sums):
    half = r_own.shape[1]
    step = 256
    for part, ref in enumerate((r_own, r_away)):
        cols = slice(part * half, (part + 1) * half)
        for at in range(0, w_in.shape[1], step):
            rows = slice(at, at + step)
            grad_hidden = dot(w_back[:, rows], ref[...], 0, 0)
            grad_pre[rows, cols] = (grad_hidden * slope[rows, cols].astype(F32)).astype(BF16)
    mine[...] = dot(w_in[...], grad_pre[:, :half], 1, 0)
    other[...] = dot(w_in[...], grad_pre[:, half:], 1, 0).astype(BF16)
    size = b_in_sums.shape[1]
    total = 0.0
    for k in range(w_in.shape[1] // size):
        pick = lax.broadcasted_iota(jnp.int32, (8, 2 * half), 0) == k
        total = total + dot(pick.astype(BF16), grad_pre[k * size : (k + 1) * size], 1, 1)
    b_in_sums[...] = total


def wide_grad_kernel(flags, own, away, right, keep, give):
    odd = flags[1]
    half = own.shape[1]
    part = keep.shape[1]
    for k in range(4):
        for pick, out in ((1 - odd, give), (odd, keep)):
            rows = pl.ds(pl.multiple_of((2 * k + pick) * part, part), part)
            total = dot(own[rows, :], right[:, :half], 1, 1)
            total = total + dot(away[rows, :], right[:, half:], 1, 1)
            out[k] = total.astype(BF16)


def norm_back_kernel(
    own, away, grad_second, scaled, inverse, vecs, sums, grad_first, low_first, sums_out
):
    upstream = grad_second[...] + own[...].astype(F32) + away[...].astype(F32)
    weighted = upstream * vecs[:, 1:2]
    mean = jnp.mean(weighted, axis=0, keepdims=True)
    tilt = jnp.mean(weighted * scaled[...], axis=0, keepdims=True)
    back = inverse[0:1] * (weighted - mean - scaled[...] * tilt)
    grad_first[...] = back
    low_first[...] = back.astype(BF16)
    sums_out[...] = sums[...] + row_sums({0: upstream * scaled[...], 1: upstream, 4: back})


def attend_back_kernel(
    flags, a_own, a_away, packs, qkv, prob, grad_first, grad_qkv, keep, give, grad_context
):
    low = flags[0]
    half = a_own.shape[1]
    feats = packs.shape[2]
    width = grad_context.shape[0]
    for part, ref in enumerate((a_own, a_away)):
        cols = slice(part * half, (part + 1) * half)
        total = 0.0
        for k in range(4):
            total = total + dot(packs[k, 1, :, width:], ref[k * feats : (k + 1) * feats], 1, 0)
        grad_context[:, cols] = total.astype(BF16)
    scale = HEAD_DIM ** (-0.5)
    for h in range(width // HEAD_DIM):
        q_rows = pl.ds(h * HEAD_DIM, HEAD_DIM)
        k_rows = pl.ds(width + h * HEAD_DIM, HEAD_DIM)
        v_rows = pl.ds(2 * width + h * HEAD_DIM, HEAD_DIM)
        grad_keys, grad_values = 0.0, 0.0
        for part in range(2):
            cols = slice(part * half, (part + 1) * half)
            weights = prob[h, :, cols]
            wide = weights.astype(F32)
            grad_weights = dot(qkv[v_rows, :], grad_context[q_rows, cols], 0, 0)
            inner = jnp.sum(wide * grad_weights, axis=0, keepdims=True)
            grad_scores = (wide * (grad_weights - inner)).astype(BF16)
            grad_qkv[q_rows, cols] = (dot(qkv[k_rows, :], grad_scores, 1, 0) * scale).astype(BF16)
            grad_keys = grad_keys + dot(qkv[q_rows, cols], grad_scores, 1, 1)
            grad_values = grad_values + dot(grad_context[q_rows, cols], weights, 1, 1)
        grad_qkv[k_rows, :] = (grad_keys * scale).astype(BF16)
        grad_qkv[v_rows, :] = grad_values.astype(BF16)

    def block(k):
        part = 0.0
        for at in range(3):
            left = packs[k, at // 2, :, at % 2 * width : (at % 2 + 1) * width]
            part = part + dot(left, grad_qkv[at * width : (at + 1) * width], 1, 0)
        rows = pl.ds(pl.multiple_of(k * feats, feats), feats)
        return part[:, :half] + 0.5 * grad_first[rows, :], part[:, half:]

    for j in range(2):
        rows = slice(j * feats, (j + 1) * feats)
        near, far = block(2 * j + 1 - low)
        give[rows, :half] = near.astype(BF16)
        give[rows, half:] = far.astype(BF16)
        near, far = block(2 * j + low)
        keep[rows, :half] = near
        keep[rows, half:] = far


def pack_grad_kernel(
    flags, xs, grad_qkv, a_own, a_away, context, sums, sums_away, b_in_sums, keep, give
):
    odd = flags[1]
    width = context.shape[0]
    feats = keep.shape[1] - 16
    half = a_own.shape[1]
    ones = (lax.broadcasted_iota(jnp.int32, (8, 2 * half), 0) == 4).astype(BF16)
    more = (lax.broadcasted_iota(jnp.int32, (8, 2 * half), 0) == 5).astype(BF16)
    shared = b_in_sums[...] + dot(ones, grad_qkv[:width], 1, 1)
    shared = shared + dot(more, grad_qkv[2 * width :], 1, 1)
    vector_sums = sums[...] + sums_away[...]
    none = jnp.zeros((16, 2 * feats), BF16)
    for k in range(4):
        span = slice(k * feats, (k + 1) * feats)
        blocks = [
            dot(xs[span], grad_qkv[at * width : (at + 1) * width], 1, 1) for at in range(3)
        ]
        last = dot(context[:, :half], a_own[span], 1, 1)
        blocks += [last + dot(context[:, half:], a_away[span], 1, 1)]
        tail = jnp.concatenate((vector_sums[:, span], shared), axis=1)
        tail = jnp.concatenate((tail, jnp.zeros_like(tail)), axis=0).astype(BF16)
        for part in range(2):
            pair = jnp.concatenate(blocks[2 * part : 2 * part + 2], axis=1).astype(BF16)
            rest = none if part else tail
            for out, at in ((keep, odd), (give, 1 - odd)):

                @pl.when(at == part)
                def _():
                    out[k, :feats] = pair
                    out[k, feats:] = rest


def pack_add_kernel(keep, got, *outs):
    for k, out in enumerate(outs):
        out[...] = (keep[k].astype(F32) + got[k].astype(F32)).astype(BF16)


def unpack_kernel(flags, own, got, qkv, w_out, b_in, *lines):
    odd = flags[1]
    feats, width = w_out.shape[1], w_out.shape[0]

    def write(first, second):
        qkv[:feats] = first[:feats, :width].astype(F32)
        qkv[feats : 2 * feats] = first[:feats, width:].astype(F32)
        qkv[2 * feats :] = second[:feats, :width].astype(F32)
        w_out[...] = second[:feats, width:].astype(F32)
        tail = first[feats:].astype(F32)
        for at in range(6):
            lines[at][...] = tail[at, :feats]
        for at in range(4):
            b_in[at * feats : (at + 1) * feats] = tail[at, feats:]
        for at in range(2):
            lines[6 + at][...] = tail[4 + at, feats:]

    @pl.when(odd == 0)
    def _():
        write(own, got)

    @pl.when(odd == 1)
    def _():
        write(got, own)


def wide_unpack_kernel(flags, b_own, b_got, i_own, i_got, back, into):
    odd = flags[1]
    part = b_own.shape[0]
    for out, own, got in ((back, b_own, b_got), (into, i_own, i_got)):
        for ref, at in ((own, odd), (got, 1 - odd)):
            rows = pl.ds(pl.multiple_of(at * part, part), part)
            out[rows, :] = ref[...].astype(F32)


def join_kernel(flags, kept, got, own, away):
    high = flags[4]
    feats = own.shape[0]
    half = own.shape[1] // 2
    for out, at in ((own, high), (away, 1 - high)):
        rows = pl.ds(pl.multiple_of(at * feats, feats), feats)
        near = kept[rows, :half] + got[rows, half:].astype(F32)
        far = kept[rows, half:] + got[rows, :half].astype(F32)
        out[:, :half] = near.astype(out.dtype)
        out[:, half:] = far.astype(out.dtype)


def finish_kernel(flags, own, got, out):
    low = flags[0]
    half = own.shape[1] // 2
    total = (own[...] + got[...].astype(F32)).astype(BF16)

    @pl.when(low == 0)
    def _():
        out[...] = total

    @pl.when(low == 1)
    def _():
        out[:, :half] = total[:, half:]
        out[:, half:] = total[:, :half]


def shards(
    layer_in,
    seq_lengths,
    w_qkv,
    q_bias,
    v_bias,
    w_out,
    b_out,
    ln1_gain,
    ln1_bias,
    w_in,
    b_in,
    w_back,
    b_back,
    ln2_gain,
    ln2_bias,
    out_grad,
):
    n_rows = lax.axis_size("row")
    row, col = lax.axis_index("row"), lax.axis_index("col")
    low_bit = (col % 2) == 1
    odd_bit = lax.axis_index("dp") % 2
    odd = odd_bit == 1
    feats, slot = layer_in.shape
    half = slot // 2
    width = w_out.shape[0]
    model = n_rows * feats
    units = w_in.shape[1]
    heads = width // HEAD_DIM
    length = lax.dynamic_index_in_dim(seq_lengths, plane_of(row), 0, False)
    flags = jnp.stack((col % 2, odd_bit, col, length, col // 2, row)).astype(jnp.int32)
    halves = shape((model, half), BF16)
    wide_halves = shape((model, half), F32)

    def sum_cores(mine, other):
        return (mine + swap_bit(other, "col", 1).astype(F32)).astype(BF16)

    def add_rows(blocks):
        parts = [from_row(blocks[k], n_rows - k) for k in range(1, n_rows)]
        terms = [term.astype(F32) for term in (blocks[0], *parts)]
        while len(terms) > 1:
            pairs = len(terms) // 2
            terms = [terms[i] + terms[i + pairs] for i in range(pairs)]
        return terms[0].astype(BF16)

    def add_replicas(total, first):
        bit = first
        while bit < lax.axis_size("dp"):
            total = total.astype(F32) + swap_bit(total, "dp", bit).astype(F32)
            total = total.astype(BF16)
            bit *= 2
        return total

    x0 = to_slot(layer_in)
    qkv_part = w_qkv.transpose(1, 0, 2).reshape(3 * feats, width)
    pack_half, wide, vectors = call(
        send_kernel,
        "send",
        [
            shape((feats, 2 * width), BF16),
            shape((feats + 16, units), BF16),
            shape((16, units), BF16),
        ],
        [odd_bit.reshape(1), qkv_part, w_out, w_in, w_back, b_in]
        + [b_out, ln1_gain, ln1_bias, b_back, ln2_gain, ln2_bias, q_bias, v_bias],
        specs={k: pl.BlockSpec(memory_space=pl.ANY) for k in range(1, 14)},
        out_specs=[
            pl.BlockSpec(memory_space=pltpu.VMEM)
        ]
        * 3,
        scratch=[
            pltpu.VMEM((2, feats, width), BF16),
            pltpu.VMEM((units,), BF16),
            pltpu.SemaphoreType.DMA((12,)),
        ]
        + [pltpu.VMEM((feats,), BF16)] * 8,
        vmem_mib=56,
    )
    fetched = lax.all_gather(after(pack_half, wide), "row")
    swapped = swap_bit(fetched, "dp", 1)
    wide = after(wide, fetched)
    wide_fetched = [from_row(wide, 1), None, from_row(wide, 3)]
    wide_fetched[1] = from_row(wide_fetched[0], 1)
    x0 = after(x0, flags, fetched)
    x2 = swap_bit(x0, "col", 2)
    x1 = swap_bit(x0, "col", 1)
    wide_swapped = [swap_bit(after(part, x2), "dp", 1) for part in wide_fetched]
    g_own = to_slot(after(out_grad.astype(BF16), fetched))
    g_high = swap_bit(g_own, "col", 2)
    ready = (wide_swapped[0], wide_fetched[1], wide_swapped[2], g_high)
    x3 = swap_bit(after(x2, swapped, *ready), "col", 1)

    in_all, back_all, vecs, in_bias = call(
        assemble_kernel,
        "assemble",
        [shape((model, units), BF16)] * 2 + [shape((model, 16), F32), shape((units, 16), F32)],
        [flags, w_in, w_back, vectors] + wide_fetched + wide_swapped,
        specs={k: pl.BlockSpec(memory_space=pl.ANY) for k in (1, 2, 4, 5, 6, 7, 8, 9)},
        scratch=[pltpu.VMEM((3, 16, units), BF16), pltpu.SemaphoreType.DMA((11,))],
    )

    xs, packs, qkv, prob, context, mine, other = call(
        attend_kernel,
        "attend",
        [
            shape((model, slot), BF16),
            shape((n_rows, 2, feats, 2 * width), BF16),
            shape((3 * width, slot), BF16),
            shape((heads, slot, slot), BF16),
            shape((width, slot), BF16),
            wide_halves,
            halves,
        ],
        [flags, x0, x1, x2, x3, fetched, swapped, vectors],
        specs={k: pl.BlockSpec(memory_space=pl.ANY) for k in range(1, 7)},
        scratch=[pltpu.VMEM((model, slot), BF16), pltpu.SemaphoreType.DMA((12,))],
        vmem_mib=40,
        weight=0,
    )

    own = sum_cores(mine, other)
    away = swap_bit(own, "col", 2)
    scaled_one, inverse_one, n_own = call(
        norm_kernel,
        "norm",
        [wide_halves, shape((8, half), F32), halves],
        [xs, own, away, vecs],
        specs={0: pl.BlockSpec((model, half), lambda _: (0, 0))},
        windowed=True,
        weight=0,
    )

    n_away = swap_bit(n_own, "col", 1)
    hidden, slope, mine, other = call(
        forward_kernel,
        "feed_forward",
        [shape((units, slot), BF16), shape((units, slot), BF16), wide_halves, halves],
        [n_own, n_away, in_all, back_all, in_bias],
        weight=0,
    )
    g_pair = swap_bit(g_own, "col", 1)
    g_last = swap_bit(g_high, "col", 1)
    own = sum_cores(mine, other)
    away = swap_bit(own, "col", 2)
    out_own, out_give, grad_second, r_own, sums = call(
        turn_kernel,
        "turn",
        [
            shape((feats, half), BF16),
            shape((feats, half), BF16),
            wide_halves,
            halves,
            shape((8, model), F32),
        ],
        [flags, scaled_one, own, away, vecs, g_own, g_pair, g_high, g_last],
        scratch=[pltpu.VMEM((model, half), BF16), pltpu.VMEM((model, half), BF16)],
        weight=0,
    )
    r_away = swap_bit(r_own, "col", 1)
    b_keep, b_give = call(
        wide_grad_kernel,
        "back_grads",
        [shape((n_rows, feats // 2, units), BF16)] * 2,
        [flags, r_own, r_away, hidden],
    )
    b_got = swap_bit(b_give, "dp", 1)
    mine, other, grad_pre, b_in_sums = call(
        backward_kernel,
        "feed_backward",
        [wide_halves, halves, shape((units, slot), BF16), shape((8, feats), F32)],
        [r_own, r_away, after(slope, b_give), in_all, back_all],
        weight=0,
    )
    own = sum_cores(mine, other)
    i_keep, i_give = call(
        wide_grad_kernel,
        "into_grads",
        [shape((n_rows, feats // 2, units), BF16)] * 2,
        [flags, after(n_own, own), n_away, grad_pre],
    )
    i_got = swap_bit(i_give, "dp", 1)
    away = swap_bit(own, "col", 2)
    grad_first, a_own, sums = call(
        norm_back_kernel,
        "norm_back",
        [wide_halves, halves, shape((8, model), F32)],
        [own, after(away, i_give), grad_second, scaled_one, inverse_one, vecs, sums],
        weight=0,
    )
    a_away = swap_bit(a_own, "col", 1)
    sums_away = swap_bit(sums, "col", 1)
    grad_qkv, kept, give = call(
        attend_back_kernel,
        "attend_back",
        [
            shape((3 * width, slot), BF16),
            shape((2 * feats, slot), F32),
            shape((2 * feats, slot), BF16),
        ],
        [flags, a_own, a_away, packs, qkv, prob, grad_first],
        scratch=[pltpu.VMEM((width, slot), BF16)],
        weight=0,
    )

    pack_keep, pack_give = call(
        pack_grad_kernel,
        "pack_grads",
        [shape((n_rows, feats + 16, 2 * width), BF16)] * 2,
        [flags, xs, grad_qkv, a_own, a_away, context, sums, sums_away, b_in_sums],
        weight=0,
    )

    in_own, in_away = call(
        join_kernel,
        "join",
        [shape((feats, slot), F32), shape((feats, slot), BF16)],
        [flags, after(kept, pack_give), swap_bit(give, "col", 1)],
    )
    (in_done,) = call(
        finish_kernel,
        "finish",
        [shape((feats, slot), BF16)],
        [flags, in_own, swap_bit(in_away, "col", 2)],
    )
    in_grad = from_slot(in_done).astype(F32)

    out_give = after(out_give, in_away)
    layer_out = from_slot(ordered(low_bit, out_own, swap_bit(out_give, "col", 1), 1))

    totals = []
    for name, keep, got in (
        ("back_add", b_keep, after(b_got, i_give)),
        ("into_add", i_keep, after(i_got, pack_give)),
    ):
        got = after(got, *totals)
        parts = call(
            pack_add_kernel, name, [shape((feats // 2, units), BF16)] * n_rows, [keep, got]
        )
        totals += [add_replicas(add_rows(parts), 2)]
    b_back, i_back = (swap_bit(total, "dp", 1) for total in totals)
    pack_got = after(swap_bit(pack_give, "dp", 1), b_back)
    w_back_grad, w_in_grad = call(
        wide_unpack_kernel,
        "wide_unpack",
        [shape((feats, units), F32)] * 2,
        [flags, totals[0], b_back, totals[1], i_back],
    )
    packs = call(
        pack_add_kernel,
        "pack_add",
        [shape(pack_keep.shape[1:], BF16)] * n_rows,
        [pack_keep, pack_got],
    )
    total = add_replicas(add_rows(packs), 2)
    w_qkv_grad, w_out_grad, b_in_grad, *lines = call(
        unpack_kernel,
        "unpack",
        [
            shape((3 * feats, width), F32),
            shape((width, feats), F32),
            shape((units,), F32),
        ]
        + [shape((feats,), F32)] * 8,
        [flags, total, swap_bit(after(total, i_back), "dp", 1)],
    )
    w_qkv_grad = w_qkv_grad.reshape(3, feats, width).transpose(1, 0, 2)
    return (
        layer_out,
        in_grad,
        w_qkv_grad,
        lines[6],
        lines[7],
        w_out_grad,
        lines[4],
        lines[0],
        lines[1],
        w_in_grad,
        b_in_grad,
        w_back_grad,
        lines[5],
        lines[2],
        lines[3],
    )


def solution(mesh):
    tokens = P("row", ("dp", "col"))
    block = P("row", "col")
    in_specs = (
        tokens,
        P("dp"),
        P("row", None, "col"),
        P("col"),
        P("col"),
        P("col", "row"),
        P("row"),
        P("row"),
        P("row"),
        block,
        P("col"),
        block,
        P("row"),
        P("row"),
        P("row"),
        tokens,
    )
    out_specs = (
        tokens,
        tokens,
        P("row", None, "col"),
        P("col"),
        P("col"),
        P("col", "row"),
        P("row"),
        P("row"),
        P("row"),
        block,
        P("col"),
        block,
        P("row"),
        P("row"),
        P("row"),
    )
    return jax.shard_map(shards, mesh=mesh, in_specs=in_specs, out_specs=out_specs, check_vma=False)
```
